32 devices in a mesh: dp: 8 (over y, x, core), tensor: 4 (over z).
Axes of the slice: x: 2, y: 2, z: 4, core: 2. Of those that a mesh axis runs over, the one named last changes fastest.
Arguments:
- activations: bfloat16 [584, 16, 1024], P('tensor', 'dp'), may hold values from -6 to 6
- cotangent: bfloat16 [584, 16, 1024], P('tensor', 'dp'), may hold values from -6 to 6
- token_valid: int32 [16, 584], P('dp'), may hold values from 0 to 1, as said below
- image_counts: int32 [8], P('dp'), may hold values from 1 to 2, as said below
- pre_gain: bfloat16 [1024], P('dp'), may hold values from 0.5 to 1.5
- pre_shift: bfloat16 [1024], P('dp'), may hold values from -3 to 3
- attn_weight: bfloat16 [3, 1024, 1024], P(None, 'dp', 'tensor'), may hold values from -0.1875 to 0.1875
- attn_bias: bfloat16 [2, 1024], P(None, 'tensor'), may hold values from -3 to 3
- proj_weight: bfloat16 [1024, 1024], P('tensor', 'dp'), may hold values from -0.5 to 0.5
- proj_bias: bfloat16 [1024], P('dp'), may hold values from -3 to 3
- mid_gain: bfloat16 [1024], P('dp'), may hold values from 0.5 to 1.5
- mid_shift: bfloat16 [1024], P('dp'), may hold values from -3 to 3
- up_weight: bfloat16 [1024, 4096], P('dp', 'tensor'), may hold values from -0.1875 to 0.1875
- up_bias: bfloat16 [4096], P('tensor'), may hold values from -3 to 3
- down_weight: bfloat16 [4096, 1024], P('tensor', 'dp'), may hold values from -0.09375 to 0.09375
- down_bias: bfloat16 [1024], P('dp'), may hold values from -3 to 3
Outputs:
- block_out: bfloat16 [584, 16, 1024], P('tensor', 'dp')
- input_grad: float32 [584, 16, 1024], P('tensor', 'dp')
- pregain_grad: float32 [1024], P('dp')
- preshift_grad: float32 [1024], P('dp')
- attnweight_grad: float32 [3, 1024, 1024], P(None, 'dp', 'tensor')
- attnbias_grad: float32 [2, 1024], P(None, 'tensor')
- projweight_grad: float32 [1024, 1024], P('tensor', 'dp')
- projbias_grad: float32 [1024], P('dp')
- midgain_grad: float32 [1024], P('dp')
- midshift_grad: float32 [1024], P('dp')
- upweight_grad: float32 [1024, 4096], P('dp', 'tensor')
- upbias_grad: float32 [4096], P('tensor')
- downweight_grad: float32 [4096, 1024], P('tensor', 'dp')
- downbias_grad: float32 [1024], P('dp')
The draws below stay inside these ranges and needn't reach their ends.
Inputs may be any that keep to these rules, and one draw needn't show every extreme that they name: `token_valid`: the valid tokens of each image are a leading run of 292 or more positions, followed only by padding. The slots of a dp index that hold images are its first image_counts ones; in every draw some dp index holds 2 images.
All inputs are finite; a program needn't handle non-finite values.
Results may differ from the reference program's by a relative error of at most 0.012.
Values may be sent and summed in bfloat16 or wider, within the bound.
A program may use at most 192 MiB of HBM per device.

```python
import jax
import jax.numpy as jnp
from jax import lax

D = 1024
H = 16
HD = 64
FF = 4096
SEQ = 584
IMG_DEV = 2
IMAGES = 16
N_DP = 8


def draw_token_valid(key, part):
    lengths = jax.random.randint(key, (IMAGES, 1), SEQ // 2, SEQ + 1)
    positions = jnp.arange(SEQ, dtype=jnp.int32)[None, :]
    return (positions < lengths).astype(jnp.int32)


def draw_image_counts(key, part):
    first, second = jax.random.split(key)
    counts = jax.random.randint(first, (N_DP,), 1, IMG_DEV + 1)
    chosen = jax.random.randint(second, (), 0, N_DP)
    return jnp.where(jnp.arange(N_DP, dtype=jnp.int32) == chosen, IMG_DEV, counts).astype(jnp.int32)


def strengthened(entries, key, source, target, shards_of, factor):
    owner, partner = [(jnp.arange(entries.shape[axis_at]) // (entries.shape[axis_at] // shards_of)).reshape([-1 if axis == axis_at else 1 for axis in range(entries.ndim)]) for axis_at in (source, target)]
    chosen = jax.random.permutation(key, shards_of)[partner]
    strong = (owner == chosen) | (owner == (partner + shards_of // 2) % shards_of)
    return jnp.where(strong, factor * entries, entries)


def steps_of(stream_key, dims, pieces, low, top_value):
    factor_of = 1.0
    for dim, shards_of in pieces:
        steps = jax.random.uniform(jax.random.fold_in(jax.random.fold_in(stream_key, 6), dim), (shards_of,), jnp.float32, low / len(pieces), top_value / len(pieces))
        factor_of = factor_of * jnp.repeat(jnp.exp(steps), dims[dim] // shards_of).reshape((-1,) + (1,) * (len(dims) - 1 - dim))
    return factor_of


def centred(stream_key, shape, scale, limit, cuts=(), kind=jnp.bfloat16):
    values = jax.random.normal(stream_key, shape, jnp.float32) * scale
    if len(cuts) > 0:
        values = steps_of(stream_key, shape, cuts, -0.22, 0.18) * values
    return jnp.clip(values, min=-limit, max=limit).astype(kind)


def gaussian_with(own_key, dims, deviation, bound, pieces, heavy, kind=jnp.bfloat16):
    values = deviation * jax.random.normal(own_key, dims, jnp.float32)
    if pieces:
        values = values * steps_of(own_key, dims, pieces, -0.22, 0.18)
    return jnp.clip(strengthened(values, jax.random.fold_in(own_key, 3), *heavy), -bound, bound).astype(kind)


def setup_inputs(seed: int = 0) -> dict:
    seeds = jax.random.split(jax.random.key(seed), 17)
    activations = centred(seeds[0], (SEQ, IMAGES, D), 1.0, 6.0, ((0, 4), (1, 8)))
    cotangent = gaussian_with(seeds[1], (SEQ, IMAGES, D), 1.0, 6.0, ((0, 4), (1, 8)), (1, 2, 8, 2.0))
    token_valid = draw_token_valid(jax.random.fold_in(seeds[16], 71), 0)
    image_counts = draw_image_counts(jax.random.fold_in(seeds[16], 71), 0)
    pre_gain = jnp.clip(1.0 + 0.1 * jax.random.normal(seeds[4], (D,), jnp.float32), 0.5, 1.5).astype(jnp.bfloat16)
    pre_shift = centred(seeds[5], (D,), 0.5, 3.0, ((0, 8),))
    attn_weight = centred(seeds[6], (3, D, D), D ** -0.5, 0.1875, ((1, 8), (2, 4)))
    attn_bias = centred(seeds[7], (2, D), 0.5, 3.0, ((1, 4),))
    proj_weight = centred(seeds[8], (D, D), (D // 8) ** -0.5, 0.5, ((0, 4), (1, 8)))
    proj_bias = centred(seeds[9], (D,), 0.5, 3.0, ((0, 8),))
    mid_gain = jnp.clip(1.0 + 0.1 * jax.random.normal(seeds[10], (D,), jnp.float32), 0.5, 1.5).astype(jnp.bfloat16)
    mid_shift = centred(seeds[11], (D,), 0.5, 3.0, ((0, 8),))
    up_weight = centred(seeds[12], (D, FF), D ** -0.5, 0.1875, ((0, 8), (1, 4)))
    up_bias = centred(seeds[13], (FF,), 0.5, 3.0, ((0, 4),))
    down_weight = centred(seeds[14], (FF, D), FF ** -0.5, 0.09375, ((0, 4), (1, 8)))
    down_bias = centred(seeds[15], (D,), 0.5, 3.0, ((0, 8),))
    return dict(activations=activations, cotangent=cotangent, token_valid=token_valid, image_counts=image_counts, pre_gain=pre_gain, pre_shift=pre_shift, attn_weight=attn_weight, attn_bias=attn_bias, proj_weight=proj_weight, proj_bias=proj_bias, mid_gain=mid_gain, mid_shift=mid_shift, up_weight=up_weight, up_bias=up_bias, down_weight=down_weight, down_bias=down_bias)


EPS = 1e-06
NEG = -1000000000.0
HP = lax.Precision.HIGHEST

@jax.custom_vjp
def low(v):
    return lax.optimization_barrier(v.astype(jnp.bfloat16)).astype(jnp.float32)

@jax.custom_vjp
def low_back(v):
    return v

def low_keep(v):
    return (low(v), None)

def low_pass(kept, grad):
    return (grad,)

def back_keep(v):
    return (v, None)

def back_low(kept, grad):
    return (low(grad),)
low.defvjp(low_keep, low_pass)
low_back.defvjp(back_keep, back_low)

def layer_norm(values, gain, shift):
    center = values - lax.optimization_barrier(jnp.mean(values, axis=-1, keepdims=True))
    spread = lax.optimization_barrier(jnp.mean(center * center, axis=-1, keepdims=True))
    return center * lax.rsqrt(spread + EPS) * gain + shift

def forward(inputs, pre_gain, pre_shift, attn_weight, attn_bias, proj_weight, proj_bias, mid_gain, mid_shift, up_weight, up_bias, down_weight, down_bias, key_bias, out_mask):
    groups, length, width = inputs.shape
    normed = low(layer_norm(inputs, pre_gain, pre_shift))
    queries = jnp.einsum('gsd,de->gse', normed, attn_weight[0], precision=HP) + attn_bias[0]
    keys = jnp.einsum('gsd,de->gse', normed, attn_weight[1], precision=HP)
    values = jnp.einsum('gsd,de->gse', normed, attn_weight[2], precision=HP) + attn_bias[1]
    queries = low(low_back(queries)).reshape(groups, length, H, HD)
    keys = low(low_back(keys)).reshape(groups, length, H, HD)
    values = low(low_back(values)).reshape(groups, length, H, HD)
    scores = jnp.einsum('gqhe,gkhe->ghqk', queries, keys, precision=HP) * HD ** (-0.5) + key_bias[:, None, None, :]
    scores = low_back(scores)
    probs = low(jax.nn.softmax(scores, axis=-1))
    attended = jnp.einsum('ghqk,gkhe->gqhe', probs, values, precision=HP).reshape(groups, length, width)
    attended = low(low_back(attended))
    branch = low_back(jnp.einsum('gse,ed->gsd', attended, proj_weight, precision=HP) + proj_bias)
    resid = inputs + branch
    normed2 = low(layer_norm(resid, mid_gain, mid_shift))
    hidden_pre = low_back(jnp.einsum('gsd,df->gsf', normed2, up_weight, precision=HP) + up_bias)
    hidden = low(jax.nn.gelu(hidden_pre, approximate=False))
    mlp_out = low_back(jnp.einsum('gsf,fd->gsd', hidden, down_weight, precision=HP) + down_bias)
    return (resid + mlp_out) * out_mask[:, :, None]

def reference(activations, cotangent, token_valid, image_counts, pre_gain, pre_shift, attn_weight, attn_bias, proj_weight, proj_bias, mid_gain, mid_shift, up_weight, up_bias, down_weight, down_bias):
    params = tuple((item.astype(jnp.float32) for item in (pre_gain, pre_shift, attn_weight, attn_bias, proj_weight, proj_bias, mid_gain, mid_shift, up_weight, up_bias, down_weight, down_bias)))
    image_index = jnp.arange(IMAGES, dtype=jnp.int32)
    owner_count = image_counts[image_index // IMG_DEV]
    live = (image_index % IMG_DEV < owner_count).astype(jnp.float32)
    valid_f = token_valid.astype(jnp.float32)
    out_mask = (live[:, None] * valid_f).reshape(N_DP, IMG_DEV, SEQ)
    key_bias = jnp.where(token_valid > 0, 0.0, NEG).astype(jnp.float32).reshape(N_DP, IMG_DEV, SEQ)
    inputs_all = jnp.transpose(activations, (1, 0, 2)).reshape(N_DP, IMG_DEV, SEQ, D)
    grads_all = jnp.transpose(cotangent, (1, 0, 2)).reshape(N_DP, IMG_DEV, SEQ, D)

    def group_step(carry, items):
        group_in, group_cot, group_bias, group_mask = items

        def apply(values_in, *weights):
            return forward(values_in, *weights, group_bias, group_mask)
        result, backward = jax.vjp(apply, group_in.astype(jnp.float32), *params)
        grads = backward(group_cot.astype(jnp.float32))
        carry = tuple((total + part for total, part in zip(carry, grads[1:])))
        return (carry, (result.astype(jnp.bfloat16), grads[0]))
    start = tuple((jnp.zeros(item.shape, jnp.float32) for item in params))
    totals, (outputs, input_grads) = lax.scan(group_step, start, (inputs_all, grads_all, key_bias, out_mask))
    block_out = jnp.transpose(outputs.reshape(IMAGES, SEQ, D), (1, 0, 2))
    input_grad = jnp.transpose(input_grads.reshape(IMAGES, SEQ, D), (1, 0, 2))
    return (block_out, input_grad, totals[0], totals[1], totals[2], totals[3], totals[4], totals[5], totals[6], totals[7], totals[8], totals[9], totals[10], totals[11])
```

```python
import functools

import jax
import jax.numpy as jnp
from jax import lax
from jax.experimental import pallas as pl
from jax.experimental.pallas import tpu as pltpu
from jax.sharding import PartitionSpec as P

D = 1024
H = 16
HD = 64
MB = 2


EPS = 1e-06
NEG = -1000000000.0


def layer_norm(values, gain, shift):
    center = values - jnp.mean(values, axis=-1, keepdims=True)
    spread = jnp.mean(center * center, axis=-1, keepdims=True)
    return center * lax.rsqrt(spread + EPS) * gain + shift


def gelu_exact(values):
    return jax.nn.gelu(values, approximate=False)


def per_device_general(
    activations,
    cotangent,
    token_valid,
    image_counts,
    pre_gain,
    pre_shift,
    attn_weight,
    attn_bias,
    proj_weight,
    proj_bias,
    mid_gain,
    mid_shift,
    up_weight,
    up_bias,
    down_weight,
    down_bias,
):
    f32 = jnp.float32
    bf16 = jnp.bfloat16
    tensor_size = lax.axis_size("tensor")
    local_rows = activations.shape[0]
    slots = activations.shape[1]
    per_micro = slots // MB
    heads_here = H // tensor_size
    width_here = attn_weight.shape[2]
    hidden_here = up_weight.shape[1]
    scale = HD ** (-0.5)
    first_row = lax.axis_index("tensor") * local_rows
    my_valid = lax.dynamic_slice_in_dim(token_valid, first_row, local_rows, 1).astype(f32)
    slot_live = (jnp.arange(slots, dtype=jnp.int32) < image_counts[0]).astype(f32)
    attn_bias_f = attn_bias.astype(f32)
    up_bias_f = up_bias.astype(f32)
    acc_attn = jnp.zeros((3, D, width_here), f32)
    acc_proj = jnp.zeros((width_here, D), f32)
    acc_up = jnp.zeros((D, hidden_here), f32)
    acc_down = jnp.zeros((hidden_here, D), f32)
    acc_attn_bias = jnp.zeros((2, width_here), f32)
    acc_up_bias = jnp.zeros((hidden_here,), f32)
    acc_vectors = [jnp.zeros((D,), f32) for unused in range(6)]
    block_parts = []
    input_parts = []
    for micro_step in range(MB):
        gathered = (
            lax.all_gather(attn_weight, "dp", axis=1, tiled=True),
            lax.all_gather(proj_weight, "dp", axis=1, tiled=True),
            lax.all_gather(up_weight, "dp", axis=0, tiled=True),
            lax.all_gather(down_weight, "dp", axis=1, tiled=True),
            lax.all_gather(pre_gain, "dp", axis=0, tiled=True),
            lax.all_gather(pre_shift, "dp", axis=0, tiled=True),
            lax.all_gather(proj_bias, "dp", axis=0, tiled=True),
            lax.all_gather(mid_gain, "dp", axis=0, tiled=True),
            lax.all_gather(mid_shift, "dp", axis=0, tiled=True),
            lax.all_gather(down_bias, "dp", axis=0, tiled=True),
        )
        qkv_full, proj_full, upw_full, downw_full = (
            gathered[0],
            gathered[1],
            gathered[2],
            gathered[3],
        )
        gain_one, shift_one, proj_bias_f, gain_two, shift_two, down_bias_f = [
            item.astype(f32) for item in gathered[4:]
        ]
        offset = micro_step * per_micro
        inputs_f = activations[:, offset : offset + per_micro].astype(f32)
        key_valid = token_valid[offset : offset + per_micro]
        key_bias = jnp.where(key_valid > 0, 0.0, NEG).astype(f32)
        out_mask = jnp.transpose(
            slot_live[offset : offset + per_micro][:, None] * my_valid[offset : offset + per_micro]
        )[:, :, None]
        normed = layer_norm(inputs_f, gain_one, shift_one).astype(bf16)
        normed_all = lax.all_gather(normed, "tensor", axis=0, tiled=True)
        full_rows = normed_all.shape[0]
        projected = jnp.einsum("sid,cde->csie", normed_all, qkv_full, preferred_element_type=f32)
        queries = (
            (projected[0] + attn_bias_f[0])
            .astype(bf16)
            .reshape(full_rows, per_micro, heads_here, HD)
        )
        keys = projected[1].astype(bf16).reshape(full_rows, per_micro, heads_here, HD)
        values = (
            (projected[2] + attn_bias_f[1])
            .astype(bf16)
            .reshape(full_rows, per_micro, heads_here, HD)
        )

        def scores_of(query_part, key_part):
            raw = jnp.einsum("qihe,kihe->ihqk", query_part, key_part, preferred_element_type=f32)
            return raw * scale + key_bias[:, None, None, :]

        scores = scores_of(queries, keys)
        top = jnp.max(scores, axis=-1, keepdims=True)
        expo = jnp.exp(scores - top)
        total = jnp.sum(expo, axis=-1, keepdims=True)
        logsum = top + jnp.log(total)
        probs_low = (expo / total).astype(bf16)
        attended = (
            jnp.einsum("ihqk,kihe->qihe", probs_low, values, preferred_element_type=f32)
            .astype(bf16)
            .reshape(full_rows, per_micro, width_here)
        )
        resid = (
            inputs_f
            + lax.psum_scatter(
                jnp.einsum("sie,ed->sid", attended, proj_full, preferred_element_type=f32),
                "tensor",
                scatter_dimension=0,
                tiled=True,
            )
            + proj_bias_f
        )
        normed2 = layer_norm(resid, gain_two, shift_two).astype(bf16)
        normed2_all = lax.all_gather(normed2, "tensor", axis=0, tiled=True)
        hidden_pre = (
            jnp.einsum("sid,df->sif", normed2_all, upw_full, preferred_element_type=f32) + up_bias_f
        )
        hidden = gelu_exact(hidden_pre).astype(bf16)
        mlp_out = (
            lax.psum_scatter(
                jnp.einsum("sif,fd->sid", hidden, downw_full, preferred_element_type=f32).astype(
                    jnp.bfloat16
                ),
                "tensor",
                scatter_dimension=0,
                tiled=True,
            ).astype(jnp.float32)
            + down_bias_f
        )
        block_parts.append(((resid + mlp_out) * out_mask).astype(bf16))
        outer = cotangent[:, offset : offset + per_micro].astype(f32) * out_mask
        mlp_grad = outer.astype(bf16)
        acc_vectors[5] = acc_vectors[5] + jnp.sum(mlp_grad.astype(f32), axis=(0, 1))
        mlp_grad_all = lax.all_gather(mlp_grad, "tensor", axis=0, tiled=True)
        acc_down = acc_down + jnp.einsum(
            "sif,sid->fd", hidden, mlp_grad_all, preferred_element_type=f32
        )
        hidden_grad = jnp.einsum(
            "sid,fd->sif", mlp_grad_all, downw_full, preferred_element_type=f32
        )
        unused, gelu_back = jax.vjp(gelu_exact, hidden_pre)
        pre_grad = gelu_back(hidden_grad)[0].astype(bf16)
        acc_up_bias = acc_up_bias + jnp.sum(pre_grad.astype(f32), axis=(0, 1))
        acc_up = acc_up + jnp.einsum(
            "sid,sif->df", normed2_all, pre_grad, preferred_element_type=f32
        )
        normed2_grad = lax.psum_scatter(
            jnp.einsum("sif,df->sid", pre_grad, upw_full, preferred_element_type=f32),
            "tensor",
            scatter_dimension=0,
            tiled=True,
        )
        unused, second_back = jax.vjp(layer_norm, resid, gain_two, shift_two)
        resid_part, gain_two_grad, shift_two_grad = second_back(normed2_grad)
        acc_vectors[3] = acc_vectors[3] + gain_two_grad
        acc_vectors[4] = acc_vectors[4] + shift_two_grad
        resid_grad = outer + resid_part
        branch_grad = resid_grad.astype(bf16)
        acc_vectors[2] = acc_vectors[2] + jnp.sum(branch_grad.astype(f32), axis=(0, 1))
        branch_all = lax.all_gather(branch_grad, "tensor", axis=0, tiled=True)
        acc_proj = acc_proj + jnp.einsum(
            "sie,sid->ed", attended, branch_all, preferred_element_type=f32
        )
        att_grad = (
            jnp.einsum("sid,ed->sie", branch_all, proj_full, preferred_element_type=f32)
            .astype(bf16)
            .reshape(full_rows, per_micro, heads_here, HD)
        )
        probs = jnp.exp(scores_of(queries, keys) - logsum)
        probs_again = probs.astype(bf16)
        value_grad = jnp.einsum(
            "ihqk,qihe->kihe", probs_again, att_grad, preferred_element_type=f32
        ).astype(bf16)
        prob_grad = jnp.einsum("qihe,kihe->ihqk", att_grad, values, preferred_element_type=f32)
        score_grad = (
            probs * (prob_grad - jnp.sum(prob_grad * probs, axis=-1, keepdims=True))
        ).astype(bf16)
        query_grad = (
            jnp.einsum("ihqk,kihe->qihe", score_grad, keys, preferred_element_type=f32) * scale
        ).astype(bf16)
        key_grad = (
            jnp.einsum("ihqk,qihe->kihe", score_grad, queries, preferred_element_type=f32) * scale
        ).astype(bf16)
        qkv_grad = jnp.stack([query_grad, key_grad, value_grad]).reshape(
            3, full_rows, per_micro, width_here
        )
        acc_attn_bias = acc_attn_bias + jnp.stack(
            [
                jnp.sum(qkv_grad[0].astype(f32), axis=(0, 1)),
                jnp.sum(qkv_grad[2].astype(f32), axis=(0, 1)),
            ]
        )
        acc_attn = acc_attn + jnp.einsum(
            "sid,csie->cde", normed_all, qkv_grad, preferred_element_type=f32
        )
        normed_grad = lax.psum_scatter(
            jnp.einsum("csie,cde->sid", qkv_grad, qkv_full, preferred_element_type=f32),
            "tensor",
            scatter_dimension=0,
            tiled=True,
        )
        unused, first_back = jax.vjp(layer_norm, inputs_f, gain_one, shift_one)
        input_part, gain_one_grad, shift_one_grad = first_back(normed_grad)
        acc_vectors[0] = acc_vectors[0] + gain_one_grad
        acc_vectors[1] = acc_vectors[1] + shift_one_grad
        input_parts.append(resid_grad + input_part)
    summed = lax.psum(
        (
            acc_vectors[0],
            acc_vectors[1],
            acc_vectors[2],
            acc_vectors[3],
            acc_vectors[4],
            acc_vectors[5],
        ),
        "tensor",
    )
    owned = (
        lax.psum_scatter(acc_attn, "dp", scatter_dimension=1, tiled=True),
        lax.psum_scatter(acc_proj, "dp", scatter_dimension=1, tiled=True),
        lax.psum_scatter(acc_up, "dp", scatter_dimension=0, tiled=True),
        lax.psum_scatter(acc_down, "dp", scatter_dimension=1, tiled=True),
        lax.psum_scatter(summed[0], "dp", scatter_dimension=0, tiled=True),
        lax.psum_scatter(summed[1], "dp", scatter_dimension=0, tiled=True),
        lax.psum_scatter(summed[2], "dp", scatter_dimension=0, tiled=True),
        lax.psum_scatter(summed[3], "dp", scatter_dimension=0, tiled=True),
        lax.psum_scatter(summed[4], "dp", scatter_dimension=0, tiled=True),
        lax.psum_scatter(summed[5], "dp", scatter_dimension=0, tiled=True),
    )
    bias_sums = lax.psum((acc_attn_bias, acc_up_bias), "dp")
    block_out = jnp.concatenate(block_parts, axis=1)
    input_grad = jnp.concatenate(input_parts, axis=1)
    return (
        block_out,
        input_grad,
        owned[4],
        owned[5],
        owned[0],
        bias_sums[0],
        owned[1],
        owned[6],
        owned[7],
        owned[8],
        owned[2],
        bias_sums[1],
        owned[3],
        owned[9],
    )

MESH = pl.DeviceIdType.MESH
F32 = jnp.float32
BF16 = jnp.bfloat16
TILES = 12
T = 4
NP = 4
ROWS = D // (2 * NP)
COLS = D // T
VROWS = 32


def place():
    d = lax.axis_index("dp")
    t = lax.axis_index("tensor")
    c = lax.rem(d, 2)
    p = d // 2
    px = p + 1 - 2 * lax.rem(p, 2)
    py = p + 2 - 4 * (p // 2)
    return d, t, c, p, px, py, 3 - p


def greet(d, t, c, p, px, py):
    barrier = pltpu.get_barrier_semaphore()
    me = c * T + t
    for step in range(1, 2 * T):
        other = lax.rem(me + step, 2 * T)
        pl.semaphore_signal(
            barrier, inc=1, device_id=(2 * p + other // T, lax.rem(other, T)), device_id_type=MESH
        )
    for q in (px, py):
        pl.semaphore_signal(barrier, inc=1, device_id=(2 * q + c, t), device_id_type=MESH)
    pl.semaphore_wait(barrier, 2 * T + 1)


def remote(src, dst, send, recv, device):
    return pltpu.make_async_remote_copy(
        src_ref=src,
        dst_ref=dst,
        send_sem=send,
        recv_sem=recv,
        device_id=device,
        device_id_type=MESH,
    )


class Exchange:
    def __init__(self, src, dst, send, recv, spot, full):
        d, t, c, p, px, py, pd = spot
        self.c, self.t, self.p = c, t, p
        self.src, self.dst, self.send, self.recv = src, dst, send, recv
        self.full = full

    def slot_out(self):
        return self.t if self.full else lax.rem(self.t, 2)

    def slot_in(self, k):
        return 2 * self.c + k if self.full else k

    def mine(self, k):
        return jnp.logical_and(self.t // 2 == self.c, lax.rem(self.t, 2) == k)

    def copy(self, k):
        return remote(
            self.src.at[k],
            self.dst.at[self.slot_out()],
            self.send.at[k],
            self.recv.at[lax.rem(self.t, 2)],
            (2 * self.p + self.t // 2, 2 * self.c + k),
        )

    def local(self, k):
        return pltpu.make_async_copy(
            self.src.at[k], self.dst.at[self.slot_out()], self.send.at[k]
        )

    def start(self):
        for k in range(2):

            @pl.when(self.mine(k))
            def _():
                self.local(k).start()

            @pl.when(jnp.logical_not(self.mine(k)))
            def _():
                self.copy(k).start()

    def wait_in(self, k):
        @pl.when(self.mine(k))
        def _():
            self.local(k).wait()

        @pl.when(jnp.logical_not(self.mine(k)))
        def _():
            remote(
                self.src.at[k],
                self.dst.at[self.slot_in(k)],
                self.send.at[k],
                self.recv.at[k],
                (2 * self.p + self.t // 2, 2 * self.c + k),
            ).wait_recv()

    def wait_out(self, k):
        @pl.when(jnp.logical_not(self.mine(k)))
        def _():
            self.copy(k).wait_send()


class Gather:
    def __init__(self, src, dst, sems, j, spot):
        self.d, self.t, self.c, self.p, self.px, self.py, self.pd = spot
        self.src, self.dst, self.j = src, dst, j
        self.zin, self.zout, self.own_sem, self.rin, self.rout, self.cin, self.cout = sems
        self.half = src.shape[0] // 2
        self.width = src.shape[1]

    def row(self, q):
        return self.dst.at[q, self.c]

    def cell(self, tau):
        start = pl.multiple_of(tau * self.width, self.width)
        return self.dst.at[self.p, self.c, :, pl.ds(start, self.width)]

    def local(self):
        return pltpu.make_async_copy(self.src, self.cell(self.t), self.own_sem.at[self.j])

    def line(self, tau, way, k):
        src = self.src if k == 0 else self.cell(tau)
        return remote(
            src,
            self.cell(tau),
            self.zout.at[self.j, way, k],
            self.zin.at[self.j, tau],
            (self.d, self.t + (1 if way == 0 else -1)),
        )

    def own(self):
        self.local().start()

        @pl.when(self.t < T - 1)
        def _():
            self.line(self.t, 0, 0).start()

        @pl.when(self.t > 0)
        def _():
            self.line(self.t, 1, 0).start()

    def hop(self, k):
        t = self.t

        @pl.when(t >= k)
        def _():
            self.line(t - k, 0, k).wait_recv()

            @pl.when(t < T - 1)
            def _():
                self.line(t - k, 0, k).start()

        @pl.when(t + k < T)
        def _():
            self.line(t + k, 1, k).wait_recv()

            @pl.when(t > 0)
            def _():
                self.line(t + k, 1, k).start()

    def side(self, way):
        q = self.px if way == 0 else self.py
        return (2 * q + self.c, self.t)

    def near(self, way):
        return remote(
            self.row(self.p),
            self.row(self.p),
            self.rout.at[self.j, way],
            self.rin.at[self.j, way],
            self.side(way),
        )

    def near_in(self, way):
        q = self.px if way == 0 else self.py
        return remote(
            self.row(q), self.row(q), self.rout.at[self.j, way], self.rin.at[self.j, way], self.side(way)
        )

    def far(self, way):
        q = self.px if way == 0 else self.py
        part = self.row(q).at[pl.ds(way * self.half, self.half)]
        return remote(
            part, part, self.rout.at[self.j, 2 + way], self.rin.at[self.j, 2 + way], self.side(1 - way)
        )

    def far_in(self, way):
        part = self.row(self.pd).at[pl.ds(way * self.half, self.half)]
        return remote(
            part, part, self.rout.at[self.j, 2 + way], self.rin.at[self.j, 2 + way], self.side(1 - way)
        )

    def ring_one(self):
        self.local().wait()
        self.near(0).start()
        self.near(1).start()

    def ring_two(self):
        for way in range(2):
            self.near_in(way).wait_recv()
            self.far(way).start()

    def pair(self, c):
        return remote(
            self.dst.at[:, c],
            self.dst.at[:, c],
            self.cout.at[self.j],
            self.cin.at[self.j],
            (2 * self.p + 1 - self.c, self.t),
        )

    def ring_three(self):
        for way in range(2):
            self.far_in(way).wait_recv()
        self.pair(self.c).start()

    def finish(self):
        self.pair(1 - self.c).wait_recv()
        t = self.t
        for k in range(T):

            @pl.when(jnp.logical_and(t >= k, t < T - 1))
            def _():
                self.line(t - k, 0, k).wait_send()

            @pl.when(jnp.logical_and(t + k < T, t > 0))
            def _():
                self.line(t + k, 1, k).wait_send()

        for way in range(2):
            self.near(way).wait_send()
            self.far(way).wait_send()
        self.pair(self.c).wait_send()


def gather_kernel(
    w, v, x, cot, valid, full_w, full_v, full_x, full_cot, full_valid, *sems
):
    ex_sem, mask_sem, pass_sem, chunk_sems = sems[0], sems[1], sems[2], sems[3:]
    spot = place()
    d, t, c, p, px, py, pd = spot
    greet(d, t, c, p, px, py)
    partner = (2 * p + 1 - c, t)
    swap_x = Exchange(x, full_x, ex_sem.at[0], ex_sem.at[1], spot, True)
    swap_c = Exchange(cot, full_cot, ex_sem.at[2], ex_sem.at[3], spot, False)
    swap_x.start()
    mask_out = remote(valid, full_valid.at[c], mask_sem.at[0], mask_sem.at[1], partner)
    mask_in = remote(valid, full_valid.at[1 - c], mask_sem.at[0], mask_sem.at[1], partner)
    mask_own = pltpu.make_async_copy(valid, full_valid.at[c], mask_sem.at[2])
    mask_out.start()
    mask_own.start()

    def passed(core, k):
        view = full_x.at[2 * core + k]
        return remote(view, view, pass_sem.at[0, k], pass_sem.at[1, k], partner)

    chunks = [Gather(v, full_v, chunk_sems, 0, spot)]
    for j in range(TILES):
        chunks.append(Gather(w.at[j], full_w.at[j], chunk_sems, j + 1, spot))
    count = len(chunks)
    for s in range(count + 6):
        for lag, stage in (
            (5, lambda g: g.ring_three()),
            (4, lambda g: g.ring_two()),
            (3, lambda g: (g.hop(3), g.ring_one())),
            (2, lambda g: g.hop(2)),
            (1, lambda g: g.hop(1)),
            (0, lambda g: g.own()),
        ):
            if 0 <= s - lag < count:
                stage(chunks[s - lag])
        if s == 0:
            swap_c.start()
        if s == 3:
            for k in range(2):
                swap_x.wait_in(k)
                passed(c, k).start()
    for k in range(2):
        swap_c.wait_in(k)
        passed(1 - c, k).wait_recv()
    mask_in.wait_recv()
    mask_own.wait()
    for chunk in chunks:
        chunk.finish()
    for k in range(2):
        passed(c, k).wait_send()
        swap_x.wait_out(k)
        swap_c.wait_out(k)
    mask_out.wait_send()


def gather_all(w, v, x, cot, valid):
    any_space = pl.BlockSpec(memory_space=pl.ANY)
    dma = pltpu.SemaphoreType.DMA
    n = TILES + 1
    lead = NP, 2
    return pl.pallas_call(
        gather_kernel,
        out_shape=(
            jax.ShapeDtypeStruct((TILES,) + lead + (ROWS, D), BF16),
            jax.ShapeDtypeStruct(lead + (VROWS, 128 * T), BF16),
            jax.ShapeDtypeStruct((T,) + x.shape[1:], BF16),
            jax.ShapeDtypeStruct(cot.shape, BF16),
            jax.ShapeDtypeStruct((2,) + valid.shape, F32),
        ),
        in_specs=[any_space] * 5,
        out_specs=[any_space] * 5,
        scratch_shapes=[
            dma((4, 2)),
            dma((3,)),
            dma((2, 2)),
            dma((n, T)),
            dma((n, 2, T)),
            dma((n,)),
            dma((n, 4)),
            dma((n, 4)),
            dma((n,)),
            dma((n,)),
        ],
        name="gather_all",
        compiler_params=pltpu.CompilerParams(collective_id=0, has_side_effects=True, vmem_limit_bytes=8 << 20),
    )(w, v, x, cot, valid)


def scatter_kernel(
    at, b, vec, blk, ig, out, vec_out, own_blk, own_ig,
    stage, held, far_in, near_in, line_in, vec_held, vec_in,
    pair_out, pair_in, far_sem, near_sem, line_sem, vec_sem, ex_sem,
):
    spot = place()
    d, t, c, p, px, py, pd = spot
    greet(d, t, c, p, px, py)
    partner = (2 * p + 1 - c, t)
    side = ((2 * px + c, t), (2 * py + c, t))
    swap_b = Exchange(blk, own_blk, ex_sem.at[0], ex_sem.at[1], spot, False)
    swap_i = Exchange(ig, own_ig, ex_sem.at[2], ex_sem.at[3], spot, False)
    half = ROWS // 2

    def pair(j):
        return remote(
            stage.at[lax.rem(j, 2)], held.at[j], pair_out.at[lax.rem(j, 2)], pair_in.at[j], partner
        )

    def far(j, way):
        return remote(
            held.at[j, pd, pl.ds(way * half, half)],
            far_in.at[j, way],
            far_sem.at[0, j, way],
            far_sem.at[1, j, way],
            side[way],
        )

    def near(j, way):
        return remote(
            held.at[j, (px, py)[way]],
            near_in.at[j, way],
            near_sem.at[0, j, way],
            near_sem.at[1, j, way],
            side[way],
        )

    def line(j, tau, way):
        return remote(
            held.at[j, p, :, pl.ds(tau * COLS, COLS)],
            line_in.at[j, way, tau],
            line_sem.at[0, j, way, tau],
            line_sem.at[1, j, way, tau],
            (d, t + (1 if way == 0 else -1)),
        )

    vec_partners = (
        partner,
        side[0],
        side[1],
        (d, t + 1 - 2 * lax.rem(t, 2)),
        (d, t + 2 - 4 * (t // 2)),
    )

    def vec_copy(r):
        return remote(vec_held.at[r], vec_in.at[r], vec_sem.at[0, r], vec_sem.at[1, r], vec_partners[r])

    def product(j, q, core):
        kind = (j + 4) // 4 - (14 - j) // 12
        rows = pl.ds(pl.multiple_of((2 * q + core) * ROWS, ROWS), ROWS)
        return jnp.dot(at[kind, rows], b[j], preferred_element_type=F32)

    vec_held[0] = vec[...]
    vec_copy(0).start()
    swap_b.start()
    swap_i.start()

    def step(s, carry):
        for r in range(5):

            @pl.when(s == 2 * r + 1)
            def _():
                vec_copy(r).wait_recv()
                vec_held[r + 1] = vec_held[r] + vec_in[r]
                if r < 4:
                    vec_copy(r + 1).start()

        @pl.when(s < TILES)
        def _():
            @pl.when(s >= 2)
            def _():
                pair(s - 2).wait_send()

            slot = lax.rem(s, 2)
            for q in range(NP):
                stage[slot, q] = product(s, q, 1 - c).astype(BF16)
            pair(s).start()

        @pl.when(jnp.logical_and(s >= 1, s < TILES + 1))
        def _():
            j = s - 1
            pair(j).wait_recv()
            for q in range(NP):
                held[j, q] = (product(j, q, c) + held[j, q].astype(F32)).astype(BF16)
            for way in range(2):
                far(j, way).start()

        @pl.when(jnp.logical_and(s >= 2, s < TILES + 2))
        def _():
            j = s - 2
            for way in range(2):
                far(j, way).wait_recv()
                part = pl.ds(way * half, half)
                q = (py, px)[way]
                held[j, q, part] = (
                    held[j, q, part].astype(F32) + far_in[j, way].astype(F32)
                ).astype(BF16)
                near(j, 1 - way).start()

        @pl.when(jnp.logical_and(s >= 3, s < TILES + 3))
        def _():
            j = s - 3
            near(j, 0).wait_recv()
            near(j, 1).wait_recv()
            for tau in range(T):
                cols = pl.ds(tau * COLS, COLS)
                total = (
                    held[j, p, :, cols].astype(F32)
                    + near_in[j, 0, :, cols].astype(F32)
                    + near_in[j, 1, :, cols].astype(F32)
                )
                held[j, p, :, cols] = total.astype(BF16)

                @pl.when(t == tau)
                def _():
                    out[j] = total

        for way in range(2):
            hop = t if way == 0 else T - 1 - t
            j = s - 4 - hop

            @pl.when(jnp.logical_and(j >= 0, j < TILES))
            def _():
                for tau in range(T):

                    @pl.when((tau > t) if way == 0 else (tau < t))
                    def _():
                        cols = pl.ds(tau * COLS, COLS)

                        @pl.when(hop > 0)
                        def _():
                            line(j, tau, way).wait_recv()
                            held[j, p, :, cols] = (
                                held[j, p, :, cols].astype(F32) + line_in[j, way, tau].astype(F32)
                            ).astype(BF16)

                        line(j, tau, way).start()

        @pl.when(s >= 8)
        def _():
            j = s - 8
            for way in range(2):

                @pl.when((t > 0) if way == 0 else (t < T - 1))
                def _():
                    for tau in range(T):

                        @pl.when(t == tau)
                        def _():
                            line(j, tau, way).wait_recv()
                            out[j] += line_in[j, way, tau].astype(F32)

        return carry

    lax.fori_loop(0, TILES + 8, step, 0)

    def drain(j, carry):
        for way in range(2):
            far(j, way).wait_send()
            near(j, way).wait_send()
            for tau in range(T):

                @pl.when((tau > t) if way == 0 else (tau < t))
                def _():
                    line(j, tau, way).wait_send()

        return carry

    lax.fori_loop(0, TILES, drain, 0)
    pair(TILES - 2).wait_send()
    pair(TILES - 1).wait_send()
    vec_out[...] = vec_held[5]
    for r in range(5):
        vec_copy(r).wait_send()
    for swap in (swap_b, swap_i):
        for k in range(2):
            swap.wait_in(k)
            swap.wait_out(k)


def scatter_all(at, b, vec, blk, ig):
    any_space = pl.BlockSpec(memory_space=pl.ANY)
    vmem = pl.BlockSpec(memory_space=pltpu.VMEM)
    dma = pltpu.SemaphoreType.DMA
    n = TILES
    return pl.pallas_call(
        scatter_kernel,
        out_shape=(
            jax.ShapeDtypeStruct((n, ROWS, COLS), F32),
            jax.ShapeDtypeStruct(vec.shape, F32),
            jax.ShapeDtypeStruct(blk.shape, BF16),
            jax.ShapeDtypeStruct(ig.shape, BF16),
        ),
        in_specs=[vmem, vmem, vmem, any_space, any_space],
        out_specs=[vmem, vmem, any_space, any_space],
        scratch_shapes=[
            pltpu.VMEM((2, NP, ROWS, D), BF16),
            pltpu.VMEM((n, NP, ROWS, D), BF16),
            pltpu.VMEM((n, 2, ROWS // 2, D), BF16),
            pltpu.VMEM((n, 2, ROWS, D), BF16),
            pltpu.VMEM((n, 2, T, ROWS, COLS), BF16),
            pltpu.VMEM((6,) + vec.shape, F32),
            pltpu.VMEM((5,) + vec.shape, F32),
            dma((2,)),
            dma((n,)),
            dma((2, n, 2)),
            dma((2, n, 2)),
            dma((2, n, 2, T)),
            dma((2, 5)),
            dma((4, 2)),
        ],
        name="scatter_all",
        compiler_params=pltpu.CompilerParams(
            collective_id=1, has_side_effects=True, vmem_limit_bytes=58 << 20
        ),
    )(at, b, vec, blk, ig)


def head_probs(k, q_t, bias):
    s = jnp.dot(k, q_t, preferred_element_type=F32) + bias
    e = jnp.exp(s - jnp.max(s, axis=0, keepdims=True))
    return e / jnp.sum(e, axis=0, keepdims=True)


def head_rows(q_t, h):
    row = lax.broadcasted_iota(jnp.int32, q_t.shape, 0) // HD
    return jnp.where(row == h, q_t, jnp.zeros_like(q_t))


def head_lanes(q, h):
    lane = lax.broadcasted_iota(jnp.int32, q.shape, 1) // HD
    return jnp.where(lane == h, q, jnp.zeros_like(q))


def attend_kernel(q, k, v, bias, out):
    q_t = (q[...].astype(F32).T * HD ** (-0.5)).astype(BF16)
    v_t = v[...].astype(F32).T.astype(BF16)
    parts = []
    for h in range(2):
        probs = head_probs(k[...], head_rows(q_t, h), bias[...]).astype(BF16)
        parts.append(
            jnp.dot(v_t[h * HD : (h + 1) * HD], probs, preferred_element_type=F32)
        )
    out[...] = jnp.concatenate(parts, axis=0).T.astype(BF16)


def attend_back_kernel(q, k, v, g, bias, dq, dk, dv):
    q_s = (q[...].astype(F32) * HD ** (-0.5)).astype(BF16)
    q_t = q_s.astype(F32).T.astype(BF16)
    g_t = g[...].astype(F32).T.astype(BF16)
    k_t = k[...].astype(F32).T.astype(BF16)
    parts = []
    dk_sum = jnp.zeros(dk.shape, F32)
    dv_sum = jnp.zeros(dv.shape, F32)
    for h in range(2):
        probs = head_probs(k[...], head_rows(q_t, h), bias[...])
        dv_sum += jnp.dot(probs.astype(BF16), head_lanes(g[...], h), preferred_element_type=F32)
        dp = jnp.dot(v[...], head_rows(g_t, h), preferred_element_type=F32)
        ds = (probs * (dp - jnp.sum(dp * probs, axis=0, keepdims=True))).astype(BF16)
        parts.append(jnp.dot(k_t[h * HD : (h + 1) * HD], ds, preferred_element_type=F32))
        dk_sum += jnp.dot(ds, head_lanes(q_s, h), preferred_element_type=F32)
    dq[...] = (jnp.concatenate(parts, axis=0).T * HD ** (-0.5)).astype(BF16)
    dk[...] = dk_sum.astype(dk.dtype)
    dv[...] = dv_sum.astype(dv.dtype)


def columns(rows):
    return pl.BlockSpec((rows, 2 * HD), lambda i: (0, i))


def attend(q, k, v, bias):
    nq, nk = q.shape[0], k.shape[0]
    return pl.pallas_call(
        attend_kernel,
        grid=(H // 2,),
        out_shape=jax.ShapeDtypeStruct((nq, D), BF16),
        in_specs=[columns(nq), columns(nk), columns(nk), pl.BlockSpec((nk, 1), lambda i: (0, 0))],
        out_specs=columns(nq),
        name="attend",
        compiler_params=pltpu.CompilerParams(vmem_limit_bytes=48 << 20),
    )(q, k, v, bias)


def attend_back(q, k, v, g, bias):
    nq, nk = q.shape[0], k.shape[0]
    return pl.pallas_call(
        attend_back_kernel,
        grid=(H // 2,),
        out_shape=(
            jax.ShapeDtypeStruct((nq, D), BF16),
            jax.ShapeDtypeStruct((nk, D), BF16),
            jax.ShapeDtypeStruct((nk, D), BF16),
        ),
        in_specs=[
            columns(nq),
            columns(nk),
            columns(nk),
            columns(nq),
            pl.BlockSpec((nk, 1), lambda i: (0, 0)),
        ],
        out_specs=(columns(nq), columns(nk), columns(nk)),
        name="attend_back",
        compiler_params=pltpu.CompilerParams(vmem_limit_bytes=48 << 20),
    )(q, k, v, g, bias)


def norm_parts(values):
    center = values - jnp.mean(values, axis=-1, keepdims=True)
    spread = jnp.mean(center * center, axis=-1, keepdims=True)
    inverse = lax.rsqrt(spread + EPS)
    return center * inverse, inverse


def norm_back(grad, unit, inverse, gain):
    scaled = grad * gain
    return inverse * (
        scaled
        - jnp.mean(scaled, axis=-1, keepdims=True)
        - unit * jnp.mean(scaled * unit, axis=-1, keepdims=True)
    )


def dot_nn(a, b):
    return lax.dot_general(a, b, (((1,), (0,)), ((), ())), preferred_element_type=F32)


def dot_nt(a, b):
    return lax.dot_general(a, b, (((1,), (1,)), ((), ())), preferred_element_type=F32)


def per_device_chips(
    activations, cotangent, token_valid, image_counts, pre_gain, pre_shift, attn_weight,
    attn_bias, proj_weight, proj_bias, mid_gain, mid_shift, up_weight, up_bias, down_weight,
    down_bias,
):
    local_rows = activations.shape[0]
    slots = activations.shape[1]
    block = -(-local_rows // 16) * 16
    pad = block - local_rows
    d = lax.axis_index("dp")
    t = lax.axis_index("tensor")
    c = lax.rem(d, 2)
    first_row = t * local_rows
    my_valid = lax.dynamic_slice_in_dim(token_valid, first_row, local_rows, 1).astype(F32)
    slot_live = (jnp.arange(slots, dtype=jnp.int32) < image_counts[0]).astype(F32)
    out_mask = jnp.transpose(slot_live[:, None] * my_valid)[:, :, None]

    def to_blocks(a):
        return jnp.pad(jnp.transpose(a, (1, 0, 2)), ((0, 0), (0, pad), (0, 0)))

    x_blocks = to_blocks(activations)
    c_blocks = to_blocks((cotangent.astype(F32) * out_mask).astype(BF16))
    valid = jnp.pad(
        token_valid.astype(F32).reshape(slots, T, local_rows), ((0, 0), (0, 0), (0, pad))
    ).reshape(slots, T * block)
    valid = jnp.pad(valid, ((0, 8 - slots), (0, 0)))
    per_j = up_weight.shape[1] // COLS
    w = jnp.concatenate(
        [
            attn_weight,
            jnp.transpose(proj_weight)[None],
            jnp.transpose(up_weight.reshape(ROWS, per_j, COLS), (1, 0, 2)),
            jnp.transpose(down_weight.reshape(per_j, COLS, ROWS), (0, 2, 1)),
        ],
        axis=0,
    )
    v = jnp.concatenate(
        [
            jnp.stack([pre_gain, pre_shift, proj_bias, mid_gain, mid_shift, down_bias]),
            attn_bias.reshape(-1, 128),
            up_bias.reshape(-1, 128),
        ],
        axis=0,
    )
    v = jnp.pad(v, ((0, VROWS - v.shape[0]), (0, 0)))
    full_w, full_v, full_x, own_cot, full_valid = gather_all(w, v, x_blocks, c_blocks, valid)
    g = full_w.reshape(TILES, D, D)
    vectors = full_v[:, :, :6, :128].astype(F32)
    gain_one, shift_one, proj_b, gain_two, shift_two, down_b = [
        vectors[:, :, i].reshape(1, D) for i in range(6)
    ]
    split = full_v[0, 0].reshape(VROWS, T, 128).astype(F32)
    per_tau = COLS // 128

    def spread_out(first, count):
        part = split[first : first + count * per_tau].reshape(count, per_tau, T, 128)
        return jnp.transpose(part, (0, 2, 1, 3)).reshape(count, 1, D)

    attn_b = spread_out(6, 2)
    up_b = spread_out(6 + 2 * per_tau, per_j)

    nk = T * block
    nq = nk // 2
    x_all = full_x.reshape(nk, D).astype(F32)
    image_valid = lax.dynamic_slice(
        full_valid, (t // 2, lax.rem(t, 2), 0), (1, 1, nk)
    ).reshape(nk, 1)
    bias = jnp.where(image_valid > 0, 0.0, NEG).astype(F32)

    def mine(a):
        return lax.dynamic_slice_in_dim(a, c * nq, nq, 0)

    def other(a):
        return lax.dynamic_slice_in_dim(a, (1 - c) * nq, nq, 0)

    unit_all, inverse_all = norm_parts(x_all)
    normed_all = (unit_all * gain_one + shift_one).astype(BF16)
    normed = mine(normed_all)
    x_own = mine(x_all)
    queries = (dot_nn(normed, g[0]) + attn_b[0]).astype(BF16)
    keys = dot_nn(normed_all, g[1]).astype(BF16)
    values = (dot_nn(normed_all, g[2]) + attn_b[1]).astype(BF16)
    attended = attend(queries, keys, values, bias)
    resid = x_own + dot_nt(attended, g[3]) + proj_b
    unit_two, inverse_two = norm_parts(resid)
    normed2 = (unit_two * gain_two + shift_two).astype(BF16)
    mlp_grad = own_cot.reshape(nq, D)
    outer = mlp_grad.astype(F32)
    hidden, pre_grad, up_sums = [], [], []
    mlp_out = jnp.zeros((nq, D), F32)
    normed2_grad = jnp.zeros((nq, D), F32)
    for j in range(per_j):
        hidden_pre = dot_nn(normed2, g[4 + j]) + up_b[j]
        act, back = jax.vjp(gelu_exact, hidden_pre)
        act = act.astype(BF16)
        hidden.append(act)
        mlp_out = mlp_out + dot_nt(act, g[8 + j])
        grad = back(dot_nn(mlp_grad, g[8 + j]))[0].astype(BF16)
        pre_grad.append(grad)
        up_sums.append(jnp.sum(grad.astype(F32), axis=0))
        normed2_grad = normed2_grad + dot_nt(grad, g[4 + j])
    block_own = (resid + mlp_out + down_b).astype(BF16)
    resid_grad = outer + norm_back(normed2_grad, unit_two, inverse_two, gain_two)
    branch = resid_grad.astype(BF16)
    att_grad = dot_nn(branch, g[3]).astype(BF16)
    dq, dk, dv = attend_back(queries, keys, values, att_grad, bias)
    swap = [(i, i + 1 - 2 * (i % 2)) for i in range(2 * NP)]
    dkv = jnp.concatenate([dk, dv], axis=1)
    came = lax.ppermute(other(dkv), "dp", swap)
    dkv = (mine(dkv).astype(F32) + came.astype(F32)).astype(BF16)
    dk, dv = dkv[:, :D], dkv[:, D:]
    normed_grad = dot_nt(dq, g[0]) + dot_nt(dk, g[1]) + dot_nt(dv, g[2])
    unit_one, inverse_one = mine(unit_all), mine(inverse_all)
    input_own = resid_grad + norm_back(normed_grad, unit_one, inverse_one, gain_one)
    sums = jnp.stack(
        [
            jnp.sum(normed_grad * unit_one, axis=0),
            jnp.sum(normed_grad, axis=0),
            jnp.sum(branch.astype(F32), axis=0),
            jnp.sum(normed2_grad * unit_two, axis=0),
            jnp.sum(normed2_grad, axis=0),
            jnp.sum(outer, axis=0),
            jnp.sum(dq.astype(F32), axis=0),
            jnp.sum(dv.astype(F32), axis=0),
        ]
        + up_sums
    )
    at = jnp.stack([jnp.transpose(a) for a in (normed, branch, normed2, mlp_grad)])
    b = jnp.stack([dq, dk, dv, attended] + pre_grad + hidden)
    grads, totals, own_block, own_input = scatter_all(
        at,
        b,
        sums.reshape(-1, 128),
        block_own.reshape(2, block, D),
        input_own.astype(BF16).reshape(2, block, D),
    )
    totals = totals.reshape(-1, D)
    owned = lax.dynamic_slice(totals, (0, d * ROWS), (6, ROWS))
    parted = lax.dynamic_slice(totals, (0, t * COLS), (totals.shape[0], COLS))

    def from_blocks(a):
        return jnp.transpose(a[:, :local_rows], (1, 0, 2))

    block_out = (from_blocks(own_block).astype(F32) * out_mask).astype(BF16)
    input_grad = from_blocks(own_input).astype(F32)
    return (
        block_out,
        input_grad,
        owned[0],
        owned[1],
        grads[0:3],
        parted[6:8],
        jnp.transpose(grads[3]),
        owned[2],
        owned[3],
        owned[4],
        jnp.transpose(grads[4 : 4 + per_j], (1, 0, 2)).reshape(ROWS, per_j * COLS),
        parted[8 : 8 + per_j].reshape(-1),
        jnp.transpose(grads[4 + per_j :], (0, 2, 1)).reshape(per_j * COLS, ROWS),
        owned[5],
    )


def solution(mesh):
    sizes = (mesh.shape["dp"], mesh.shape["tensor"])
    per_device = per_device_chips if sizes == (2 * NP, T) else per_device_general
    return jax.shard_map(
        per_device,
        mesh=mesh,
        in_specs=(
            P("tensor", "dp", None),
            P("tensor", "dp", None),
            P("dp", None),
            P("dp"),
            P("dp"),
            P("dp"),
            P(None, "dp", "tensor"),
            P(None, "tensor"),
            P("tensor", "dp"),
            P("dp"),
            P("dp"),
            P("dp"),
            P("dp", "tensor"),
            P("tensor"),
            P("tensor", "dp"),
            P("dp"),
        ),
        out_specs=(
            P("tensor", "dp", None),
            P("tensor", "dp", None),
            P("dp"),
            P("dp"),
            P(None, "dp", "tensor"),
            P(None, "tensor"),
            P("tensor", "dp"),
            P("dp"),
            P("dp"),
            P("dp"),
            P("dp", "tensor"),
            P("tensor"),
            P("tensor", "dp"),
            P("dp"),
        ),
        check_vma=False,
    )
```

```python
import functools

import jax
import jax.numpy as jnp
from jax import lax
from jax.experimental import pallas as pl
from jax.experimental.pallas import tpu as pltpu
from jax.sharding import PartitionSpec as P

D = 1024
H = 16
HD = 64
MB = 2


EPS = 1e-06
NEG = -1000000000.0


def layer_norm(values, gain, shift):
    center = values - jnp.mean(values, axis=-1, keepdims=True)
    spread = jnp.mean(center * center, axis=-1, keepdims=True)
    return center * lax.rsqrt(spread + EPS) * gain + shift


def gelu_exact(values):
    return jax.nn.gelu(values, approximate=False)


def per_device_general(
    activations,
    cotangent,
    token_valid,
    image_counts,
    pre_gain,
    pre_shift,
    attn_weight,
    attn_bias,
    proj_weight,
    proj_bias,
    mid_gain,
    mid_shift,
    up_weight,
    up_bias,
    down_weight,
    down_bias,
):
    f32 = jnp.float32
    bf16 = jnp.bfloat16
    tensor_size = lax.axis_size("tensor")
    local_rows = activations.shape[0]
    slots = activations.shape[1]
    per_micro = slots // MB
    heads_here = H // tensor_size
    width_here = attn_weight.shape[2]
    hidden_here = up_weight.shape[1]
    scale = HD ** (-0.5)
    first_row = lax.axis_index("tensor") * local_rows
    my_valid = lax.dynamic_slice_in_dim(token_valid, first_row, local_rows, 1).astype(f32)
    slot_live = (jnp.arange(slots, dtype=jnp.int32) < image_counts[0]).astype(f32)
    attn_bias_f = attn_bias.astype(f32)
    up_bias_f = up_bias.astype(f32)
    acc_attn = jnp.zeros((3, D, width_here), f32)
    acc_proj = jnp.zeros((width_here, D), f32)
    acc_up = jnp.zeros((D, hidden_here), f32)
    acc_down = jnp.zeros((hidden_here, D), f32)
    acc_attn_bias = jnp.zeros((2, width_here), f32)
    acc_up_bias = jnp.zeros((hidden_here,), f32)
    acc_vectors = [jnp.zeros((D,), f32) for unused in range(6)]
    block_parts = []
    input_parts = []
    for micro_step in range(MB):
        gathered = (
            lax.all_gather(attn_weight, "dp", axis=1, tiled=True),
            lax.all_gather(proj_weight, "dp", axis=1, tiled=True),
            lax.all_gather(up_weight, "dp", axis=0, tiled=True),
            lax.all_gather(down_weight, "dp", axis=1, tiled=True),
            lax.all_gather(pre_gain, "dp", axis=0, tiled=True),
            lax.all_gather(pre_shift, "dp", axis=0, tiled=True),
            lax.all_gather(proj_bias, "dp", axis=0, tiled=True),
            lax.all_gather(mid_gain, "dp", axis=0, tiled=True),
            lax.all_gather(mid_shift, "dp", axis=0, tiled=True),
            lax.all_gather(down_bias, "dp", axis=0, tiled=True),
        )
        qkv_full, proj_full, upw_full, downw_full = (
            gathered[0],
            gathered[1],
            gathered[2],
            gathered[3],
        )
        gain_one, shift_one, proj_bias_f, gain_two, shift_two, down_bias_f = [
            item.astype(f32) for item in gathered[4:]
        ]
        offset = micro_step * per_micro
        inputs_f = activations[:, offset : offset + per_micro].astype(f32)
        key_valid = token_valid[offset : offset + per_micro]
        key_bias = jnp.where(key_valid > 0, 0.0, NEG).astype(f32)
        out_mask = jnp.transpose(
            slot_live[offset : offset + per_micro][:, None] * my_valid[offset : offset + per_micro]
        )[:, :, None]
        normed = layer_norm(inputs_f, gain_one, shift_one).astype(bf16)
        normed_all = lax.all_gather(normed, "tensor", axis=0, tiled=True)
        full_rows = normed_all.shape[0]
        projected = jnp.einsum("sid,cde->csie", normed_all, qkv_full, preferred_element_type=f32)
        queries = (
            (projected[0] + attn_bias_f[0])
            .astype(bf16)
            .reshape(full_rows, per_micro, heads_here, HD)
        )
        keys = projected[1].astype(bf16).reshape(full_rows, per_micro, heads_here, HD)
        values = (
            (projected[2] + attn_bias_f[1])
            .astype(bf16)
            .reshape(full_rows, per_micro, heads_here, HD)
        )

        def scores_of(query_part, key_part):
            raw = jnp.einsum("qihe,kihe->ihqk", query_part, key_part, preferred_element_type=f32)
            return raw * scale + key_bias[:, None, None, :]

        scores = scores_of(queries, keys)
        top = jnp.max(scores, axis=-1, keepdims=True)
        expo = jnp.exp(scores - top)
        total = jnp.sum(expo, axis=-1, keepdims=True)
        logsum = top + jnp.log(total)
        probs_low = (expo / total).astype(bf16)
        attended = (
            jnp.einsum("ihqk,kihe->qihe", probs_low, values, preferred_element_type=f32)
            .astype(bf16)
            .reshape(full_rows, per_micro, width_here)
        )
        resid = (
            inputs_f
            + lax.psum_scatter(
                jnp.einsum("sie,ed->sid", attended, proj_full, preferred_element_type=f32),
                "tensor",
                scatter_dimension=0,
                tiled=True,
            )
            + proj_bias_f
        )
        normed2 = layer_norm(resid, gain_two, shift_two).astype(bf16)
        normed2_all = lax.all_gather(normed2, "tensor", axis=0, tiled=True)
        hidden_pre = (
            jnp.einsum("sid,df->sif", normed2_all, upw_full, preferred_element_type=f32) + up_bias_f
        )
        hidden = gelu_exact(hidden_pre).astype(bf16)
        mlp_out = (
            lax.psum_scatter(
                jnp.einsum("sif,fd->sid", hidden, downw_full, preferred_element_type=f32).astype(
                    jnp.bfloat16
                ),
                "tensor",
                scatter_dimension=0,
                tiled=True,
            ).astype(jnp.float32)
            + down_bias_f
        )
        block_parts.append(((resid + mlp_out) * out_mask).astype(bf16))
        outer = cotangent[:, offset : offset + per_micro].astype(f32) * out_mask
        mlp_grad = outer.astype(bf16)
        acc_vectors[5] = acc_vectors[5] + jnp.sum(mlp_grad.astype(f32), axis=(0, 1))
        mlp_grad_all = lax.all_gather(mlp_grad, "tensor", axis=0, tiled=True)
        acc_down = acc_down + jnp.einsum(
            "sif,sid->fd", hidden, mlp_grad_all, preferred_element_type=f32
        )
        hidden_grad = jnp.einsum(
            "sid,fd->sif", mlp_grad_all, downw_full, preferred_element_type=f32
        )
        unused, gelu_back = jax.vjp(gelu_exact, hidden_pre)
        pre_grad = gelu_back(hidden_grad)[0].astype(bf16)
        acc_up_bias = acc_up_bias + jnp.sum(pre_grad.astype(f32), axis=(0, 1))
        acc_up = acc_up + jnp.einsum(
            "sid,sif->df", normed2_all, pre_grad, preferred_element_type=f32
        )
        normed2_grad = lax.psum_scatter(
            jnp.einsum("sif,df->sid", pre_grad, upw_full, preferred_element_type=f32),
            "tensor",
            scatter_dimension=0,
            tiled=True,
        )
        unused, second_back = jax.vjp(layer_norm, resid, gain_two, shift_two)
        resid_part, gain_two_grad, shift_two_grad = second_back(normed2_grad)
        acc_vectors[3] = acc_vectors[3] + gain_two_grad
        acc_vectors[4] = acc_vectors[4] + shift_two_grad
        resid_grad = outer + resid_part
        branch_grad = resid_grad.astype(bf16)
        acc_vectors[2] = acc_vectors[2] + jnp.sum(branch_grad.astype(f32), axis=(0, 1))
        branch_all = lax.all_gather(branch_grad, "tensor", axis=0, tiled=True)
        acc_proj = acc_proj + jnp.einsum(
            "sie,sid->ed", attended, branch_all, preferred_element_type=f32
        )
        att_grad = (
            jnp.einsum("sid,ed->sie", branch_all, proj_full, preferred_element_type=f32)
            .astype(bf16)
            .reshape(full_rows, per_micro, heads_here, HD)
        )
        probs = jnp.exp(scores_of(queries, keys) - logsum)
        probs_again = probs.astype(bf16)
        value_grad = jnp.einsum(
            "ihqk,qihe->kihe", probs_again, att_grad, preferred_element_type=f32
        ).astype(bf16)
        prob_grad = jnp.einsum("qihe,kihe->ihqk", att_grad, values, preferred_element_type=f32)
        score_grad = (
            probs * (prob_grad - jnp.sum(prob_grad * probs, axis=-1, keepdims=True))
        ).astype(bf16)
        query_grad = (
            jnp.einsum("ihqk,kihe->qihe", score_grad, keys, preferred_element_type=f32) * scale
        ).astype(bf16)
        key_grad = (
            jnp.einsum("ihqk,qihe->kihe", score_grad, queries, preferred_element_type=f32) * scale
        ).astype(bf16)
        qkv_grad = jnp.stack([query_grad, key_grad, value_grad]).reshape(
            3, full_rows, per_micro, width_here
        )
        acc_attn_bias = acc_attn_bias + jnp.stack(
            [
                jnp.sum(qkv_grad[0].astype(f32), axis=(0, 1)),
                jnp.sum(qkv_grad[2].astype(f32), axis=(0, 1)),
            ]
        )
        acc_attn = acc_attn + jnp.einsum(
            "sid,csie->cde", normed_all, qkv_grad, preferred_element_type=f32
        )
        normed_grad = lax.psum_scatter(
            jnp.einsum("csie,cde->sid", qkv_grad, qkv_full, preferred_element_type=f32),
            "tensor",
            scatter_dimension=0,
            tiled=True,
        )
        unused, first_back = jax.vjp(layer_norm, inputs_f, gain_one, shift_one)
        input_part, gain_one_grad, shift_one_grad = first_back(normed_grad)
        acc_vectors[0] = acc_vectors[0] + gain_one_grad
        acc_vectors[1] = acc_vectors[1] + shift_one_grad
        input_parts.append(resid_grad + input_part)
    summed = lax.psum(
        (
            acc_vectors[0],
            acc_vectors[1],
            acc_vectors[2],
            acc_vectors[3],
            acc_vectors[4],
            acc_vectors[5],
        ),
        "tensor",
    )
    owned = (
        lax.psum_scatter(acc_attn, "dp", scatter_dimension=1, tiled=True),
        lax.psum_scatter(acc_proj, "dp", scatter_dimension=1, tiled=True),
        lax.psum_scatter(acc_up, "dp", scatter_dimension=0, tiled=True),
        lax.psum_scatter(acc_down, "dp", scatter_dimension=1, tiled=True),
        lax.psum_scatter(summed[0], "dp", scatter_dimension=0, tiled=True),
        lax.psum_scatter(summed[1], "dp", scatter_dimension=0, tiled=True),
        lax.psum_scatter(summed[2], "dp", scatter_dimension=0, tiled=True),
        lax.psum_scatter(summed[3], "dp", scatter_dimension=0, tiled=True),
        lax.psum_scatter(summed[4], "dp", scatter_dimension=0, tiled=True),
        lax.psum_scatter(summed[5], "dp", scatter_dimension=0, tiled=True),
    )
    bias_sums = lax.psum((acc_attn_bias, acc_up_bias), "dp")
    block_out = jnp.concatenate(block_parts, axis=1)
    input_grad = jnp.concatenate(input_parts, axis=1)
    return (
        block_out,
        input_grad,
        owned[4],
        owned[5],
        owned[0],
        bias_sums[0],
        owned[1],
        owned[6],
        owned[7],
        owned[8],
        owned[2],
        bias_sums[1],
        owned[3],
        owned[9],
    )

MESH = pl.DeviceIdType.MESH
F32 = jnp.float32
BF16 = jnp.bfloat16
TILES = 12
T = 4
NP = 4
ROWS = D // (2 * NP)
COLS = D // T
VROWS = 32


def place():
    d = lax.axis_index("dp")
    t = lax.axis_index("tensor")
    c = lax.rem(d, 2)
    p = d // 2
    px = p + 1 - 2 * lax.rem(p, 2)
    py = p + 2 - 4 * (p // 2)
    return d, t, c, p, px, py, 3 - p


def greet(d, t, c, p, px, py):
    barrier = pltpu.get_barrier_semaphore()
    me = c * T + t
    for step in range(1, 2 * T):
        other = lax.rem(me + step, 2 * T)
        pl.semaphore_signal(
            barrier, inc=1, device_id=(2 * p + other // T, lax.rem(other, T)), device_id_type=MESH
        )
    for q in (px, py):
        pl.semaphore_signal(barrier, inc=1, device_id=(2 * q + c, t), device_id_type=MESH)
    pl.semaphore_wait(barrier, 2 * T + 1)


def remote(src, dst, send, recv, device):
    return pltpu.make_async_remote_copy(
        src_ref=src,
        dst_ref=dst,
        send_sem=send,
        recv_sem=recv,
        device_id=device,
        device_id_type=MESH,
    )


class Exchange:
    def __init__(self, src, dst, send, recv, spot, full):
        d, t, c, p, px, py, pd = spot
        self.c, self.t, self.p = c, t, p
        self.src, self.dst, self.send, self.recv = src, dst, send, recv
        self.full = full

    def slot_out(self):
        return self.t if self.full else lax.rem(self.t, 2)

    def slot_in(self, k):
        return 2 * self.c + k if self.full else k

    def mine(self, k):
        return jnp.logical_and(self.t // 2 == self.c, lax.rem(self.t, 2) == k)

    def copy(self, k):
        return remote(
            self.src.at[k],
            self.dst.at[self.slot_out()],
            self.send.at[k],
            self.recv.at[lax.rem(self.t, 2)],
            (2 * self.p + self.t // 2, 2 * self.c + k),
        )

    def local(self, k):
        return pltpu.make_async_copy(
            self.src.at[k], self.dst.at[self.slot_out()], self.send.at[k]
        )

    def start(self):
        for k in range(2):

            @pl.when(self.mine(k))
            def _():
                self.local(k).start()

            @pl.when(jnp.logical_not(self.mine(k)))
            def _():
                self.copy(k).start()

    def wait_in(self, k):
        @pl.when(self.mine(k))
        def _():
            self.local(k).wait()

        @pl.when(jnp.logical_not(self.mine(k)))
        def _():
            remote(
                self.src.at[k],
                self.dst.at[self.slot_in(k)],
                self.send.at[k],
                self.recv.at[k],
                (2 * self.p + self.t // 2, 2 * self.c + k),
            ).wait_recv()

    def wait_out(self, k):
        @pl.when(jnp.logical_not(self.mine(k)))
        def _():
            self.copy(k).wait_send()


class Gather:
    def __init__(self, src, dst, sems, j, spot):
        self.d, self.t, self.c, self.p, self.px, self.py, self.pd = spot
        self.src, self.dst, self.j = src, dst, j
        self.zin, self.zout, self.own_sem, self.rin, self.rout, self.cin, self.cout = sems
        self.half = src.shape[0] // 2
        self.width = src.shape[1]

    def row(self, q):
        return self.dst.at[q, self.c]

    def cell(self, tau):
        start = pl.multiple_of(tau * self.width, self.width)
        return self.dst.at[self.p, self.c, :, pl.ds(start, self.width)]

    def local(self):
        return pltpu.make_async_copy(self.src, self.cell(self.t), self.own_sem.at[self.j])

    def line(self, tau, way, k):
        src = self.src if k == 0 else self.cell(tau)
        return remote(
            src,
            self.cell(tau),
            self.zout.at[self.j, way, k],
            self.zin.at[self.j, tau],
            (self.d, self.t + (1 if way == 0 else -1)),
        )

    def own(self):
        self.local().start()

        @pl.when(self.t < T - 1)
        def _():
            self.line(self.t, 0, 0).start()

        @pl.when(self.t > 0)
        def _():
            self.line(self.t, 1, 0).start()

    def hop(self, k):
        t = self.t

        @pl.when(t >= k)
        def _():
            self.line(t - k, 0, k).wait_recv()

            @pl.when(t < T - 1)
            def _():
                self.line(t - k, 0, k).start()

        @pl.when(t + k < T)
        def _():
            self.line(t + k, 1, k).wait_recv()

            @pl.when(t > 0)
            def _():
                self.line(t + k, 1, k).start()

    def side(self, way):
        q = self.px if way == 0 else self.py
        return (2 * q + self.c, self.t)

    def near(self, way):
        return remote(
            self.row(self.p),
            self.row(self.p),
            self.rout.at[self.j, way],
            self.rin.at[self.j, way],
            self.side(way),
        )

    def near_in(self, way):
        q = self.px if way == 0 else self.py
        return remote(
            self.row(q), self.row(q), self.rout.at[self.j, way], self.rin.at[self.j, way], self.side(way)
        )

    def far(self, way):
        q = self.px if way == 0 else self.py
        part = self.row(q).at[pl.ds(way * self.half, self.half)]
        return remote(
            part, part, self.rout.at[self.j, 2 + way], self.rin.at[self.j, 2 + way], self.side(1 - way)
        )

    def far_in(self, way):
        part = self.row(self.pd).at[pl.ds(way * self.half, self.half)]
        return remote(
            part, part, self.rout.at[self.j, 2 + way], self.rin.at[self.j, 2 + way], self.side(1 - way)
        )

    def ring_one(self):
        self.local().wait()
        self.near(0).start()
        self.near(1).start()

    def ring_two(self):
        for way in range(2):
            self.near_in(way).wait_recv()
            self.far(way).start()

    def pair(self, c):
        return remote(
            self.dst.at[:, c],
            self.dst.at[:, c],
            self.cout.at[self.j],
            self.cin.at[self.j],
            (2 * self.p + 1 - self.c, self.t),
        )

    def ring_three(self):
        for way in range(2):
            self.far_in(way).wait_recv()
        self.pair(self.c).start()

    def ready(self):
        self.pair(1 - self.c).wait_recv()

    def finish(self):
        t = self.t
        for k in range(T):

            @pl.when(jnp.logical_and(t >= k, t < T - 1))
            def _():
                self.line(t - k, 0, k).wait_send()

            @pl.when(jnp.logical_and(t + k < T, t > 0))
            def _():
                self.line(t + k, 1, k).wait_send()

        for way in range(2):
            self.near(way).wait_send()
            self.far(way).wait_send()
        self.pair(self.c).wait_send()


LAGS = (1, 2, 3, 5, 7)
ORDER = (0, 1, 2, 3, 4, 8, 5, 9, 6, 10, 7, 11)
QUARTERS = 4
TILE = 256


def tiles(n, size, body):
    def run(i, carry):
        body(pl.ds(pl.multiple_of(i * size, size), size), i)
        return carry

    lax.fori_loop(0, n // size, run, 0)


def to_lanes(a):
    return a.astype(F32).T.astype(BF16)


def matrix(w, j, cols=None):
    a = w[j] if cols is None else w[j, :, :, :, cols]
    return a.reshape(D, a.shape[-1])


def matrix_rows(w, j, n):
    return w[j, n].reshape(2 * ROWS, D)


def forward_kernel(
    w, v, x, cot, valid,
    o_w, o_vec, o_x, o_cot, o_bias, o_q, o_k, o_v, o_att, o_nt, o_n2t, o_mgt, o_hid, o_pre,
    o_n2g, o_resid, o_blk, o_ups,
    gw, gv, xf, cf, mf, vec, bias, normed, q_s, k_s, v_s, att, resid, n2, nt, n2t, mgt, hid, pre,
    n2g, mlp, slope, blk, ups,
    ex_sem, mask_sem, pass_sem, out_sem, *chunk_sems,
):
    spot = place()
    d, t, c, p, px, py, pd = spot
    greet(d, t, c, p, px, py)
    partner = (2 * p + 1 - c, t)
    swap_x = Exchange(x, xf, ex_sem.at[0], ex_sem.at[1], spot, True)
    swap_c = Exchange(cot, cf, ex_sem.at[2], ex_sem.at[3], spot, False)
    mask_out = remote(valid, mf.at[c], mask_sem.at[0], mask_sem.at[1], partner)
    mask_in = remote(valid, mf.at[1 - c], mask_sem.at[0], mask_sem.at[1], partner)
    mask_own = pltpu.make_async_copy(valid, mf.at[c], mask_sem.at[2])

    def passed(core, k):
        view = xf.at[2 * core + k]
        return remote(view, view, pass_sem.at[0, k], pass_sem.at[1, k], partner)

    chunks = [Gather(v, gv, chunk_sems, 0, spot)]
    for i, j in enumerate(ORDER):
        chunks.append(Gather(w.at[j], gw.at[j], chunk_sems, i + 1, spot))
    count = len(chunks)

    def comm(s):
        for lag, stage in (
            (LAGS[4], lambda g: g.ring_three()),
            (LAGS[3], lambda g: g.ring_two()),
            (LAGS[2], lambda g: (g.hop(3), g.ring_one())),
            (LAGS[1], lambda g: g.hop(2)),
            (LAGS[0], lambda g: g.hop(1)),
            (0, lambda g: g.own()),
        ):
            if 0 <= s - lag < count:
                stage(chunks[s - lag])
        if s == 1:
            swap_x.start()
            mask_out.start()
            mask_own.start()
        if s == 4:
            for k in range(2):
                swap_x.wait_in(k)
                passed(c, k).start()
        if s == 8:
            swap_c.start()

    nq = q_s.shape[0]
    nk = k_s.shape[0]
    block = xf.shape[1]
    own_rows = pl.ds(pl.multiple_of(c * nq, nq), nq)
    copies = []

    def emit(src, dst):
        copy = pltpu.make_async_copy(src, dst, out_sem.at[len(copies)])
        copy.start()
        copies.append(copy)

    def vectors():
        for q in range(NP):
            for core in range(2):
                part = gv[q, core].astype(F32)
                first = (2 * q + core) * ROWS
                vec[0:6, first : first + ROWS] = part[0:6, 0:ROWS]
        part = gv[0, 0].astype(F32)
        per = COLS // 128
        for i in range(2 + QUARTERS):
            for tau in range(T):
                for r in range(per):
                    row = 6 + i * per + r
                    at = tau * COLS + r * 128
                    vec[6 + i : 7 + i, at : at + 128] = part[row : row + 1, tau * 128 : tau * 128 + 128]
        emit(vec, o_vec)
        mask_in.wait_recv()
        mask_own.wait()
        rows = mf[t // 2].T
        col = jnp.where(lax.rem(t, 2) == 0, rows[:, 0:1], rows[:, 1:2])
        bias[...] = jnp.where(col > 0, 0.0, NEG).astype(F32)
        emit(bias, o_bias)

    def norm_one():
        for k in range(2):
            passed(1 - c, k).wait_recv()
        emit(xf.at[pl.ds(2 * c, 2)], o_x)
        size = 32
        per = block // size

        def run(i, carry):
            at = pl.ds(pl.multiple_of(lax.rem(i, per) * size, size), size)
            unit, unused = norm_parts(xf[i // per, at].astype(F32))
            normed[pl.ds(pl.multiple_of(i * size, size), size)] = (
                unit * vec[0:1] + vec[1:2]
            ).astype(BF16)
            return carry

        lax.fori_loop(0, nk // size, run, 0)

        def flip(cols, i):
            nt[cols] = to_lanes(normed[own_rows, cols])

        tiles(D, TILE, flip)
        emit(nt, o_nt)

    def project(j, dst, rows, shift):
        a = normed[rows]

        def run(cols, i):
            out = jnp.dot(a, matrix(gw, j, cols), preferred_element_type=F32)
            if shift is not None:
                out = out + vec[shift : shift + 1, cols]
            dst[:, cols] = out.astype(BF16)

        tiles(D, TILE, run)

    def heads(first, last):
        def run(i, carry):
            cols = pl.ds(pl.multiple_of(i * 2 * HD, 2 * HD), 2 * HD)
            q_t = (q_s[:, cols].astype(F32).T * HD ** (-0.5)).astype(BF16)
            v_t = to_lanes(v_s[:, cols])
            k = k_s[:, cols]
            parts = []
            for h in range(2):
                probs = head_probs(k, head_rows(q_t, h), bias[...]).astype(BF16)
                parts.append(
                    jnp.dot(v_t[h * HD : (h + 1) * HD], probs, preferred_element_type=F32)
                )
            att[:, cols] = jnp.concatenate(parts, axis=0).T.astype(BF16)
            return carry

        lax.fori_loop(first, last, run, 0)

    def middle():
        emit(att, o_att)
        a = att[...]
        x_own = xf.at[pl.ds(2 * c, 2)]

        def run(cols, i):
            out = dot_nt(a, matrix_rows(gw, 3, i))
            resid[:, cols] = (
                x_own[:, :, cols].astype(F32).reshape(nq, TILE) + out + vec[2:3, cols]
            )

        tiles(D, TILE, run)
        emit(resid, o_resid)

        def norm(rows, i):
            unit, unused = norm_parts(resid[rows])
            n2[rows] = (unit * vec[3:4] + vec[4:5]).astype(BF16)

        tiles(nq, 64, norm)

        def flip(cols, i):
            n2t[cols] = to_lanes(n2[:, cols])

        tiles(D, TILE, flip)
        emit(n2t, o_n2t)

    def grads_in():
        for k in range(2):
            swap_c.wait_in(k)
        emit(cf, o_cot)

        def flip(cols, i):
            mgt[cols] = to_lanes(cf[:, :, cols].reshape(nq, TILE))

        tiles(D, TILE, flip)
        emit(mgt, o_mgt)

    def quarter_up(j):
        a = n2[...]

        def run(cols, i):
            z = jnp.dot(a, matrix(gw, 4 + j, cols), preferred_element_type=F32)
            z = z + vec[8 + j : 9 + j, cols]
            share = 0.5 + 0.5 * lax.erf(z * 0.5**0.5)
            hid[j, :, cols] = (z * share).astype(BF16)
            slope[:, cols] = share + z * (jnp.exp(-0.5 * z * z) * (0.5 / jnp.pi) ** 0.5)

        tiles(D, TILE, run)
        emit(hid.at[j], o_hid.at[j])

    def quarter_down(j):
        g = cf[...].reshape(nq, D)

        def back(cols, i):
            h = jnp.dot(g, matrix(gw, 8 + j, cols), preferred_element_type=F32)
            grad = (slope[:, cols] * h).astype(BF16)
            pre[j, :, cols] = grad
            ups[j : j + 1, cols] = jnp.sum(grad.astype(F32), axis=0, keepdims=True)

        tiles(D, TILE, back)
        emit(pre.at[j], o_pre.at[j])

        def outs(cols, i):
            m = dot_nt(hid[j], matrix_rows(gw, 8 + j, i))
            n = dot_nt(pre[j], matrix_rows(gw, 4 + j, i))
            if j == 0:
                mlp[:, cols] = m
                n2g[:, cols] = n
            elif j < QUARTERS - 1:
                mlp[:, cols] += m
                n2g[:, cols] += n
            else:
                n2g[:, cols] += n
                blk[:, cols] = (resid[:, cols] + mlp[:, cols] + m + vec[5:6, cols]).astype(BF16)

        tiles(D, TILE, outs)

    whole = pl.ds(0, nk)
    after = {
        8: (vectors, norm_one),
        9: (lambda: project(0, q_s, own_rows, 6), lambda: emit(q_s, o_q)),
        10: (lambda: project(1, k_s, whole, None), lambda: emit(k_s, o_k)),
        11: (lambda: project(2, v_s, whole, 7), lambda: emit(v_s, o_v), lambda: heads(0, 2)),
        12: (lambda: heads(2, 6),),
        13: (lambda: heads(6, 8), middle),
        14: (lambda: quarter_up(0), grads_in, lambda: quarter_down(0)),
        15: (lambda: quarter_up(1),),
        16: (lambda: quarter_down(1),),
        17: (lambda: quarter_up(2),),
        18: (lambda: quarter_down(2),),
        19: (lambda: quarter_up(3),),
        20: (lambda: quarter_down(3),),
    }
    for s in range(count + LAGS[4] + 1):
        comm(s)
        if 0 <= s - LAGS[4] - 1 < count:
            i = s - LAGS[4] - 1
            chunks[i].ready()
            if 1 <= i <= 4:
                emit(gw.at[ORDER[i - 1]], o_w.at[ORDER[i - 1]])
        for unit in after.get(s, ()):
            unit()
    emit(n2g, o_n2g)
    emit(blk, o_blk)
    emit(ups, o_ups)
    for chunk in chunks:
        chunk.finish()
    for k in range(2):
        passed(c, k).wait_send()
        swap_x.wait_out(k)
        swap_c.wait_out(k)
    mask_out.wait_send()
    for copy in copies:
        copy.wait()


def forward_all(w, v, x, cot, valid):
    any_space = pl.BlockSpec(memory_space=pl.ANY)
    dma = pltpu.SemaphoreType.DMA
    n = TILES + 1
    block = x.shape[1]
    nk = T * block
    nq = nk // 2
    gathered = (NP, 2, ROWS, D)

    def half(rows, cols=D):
        return (rows, cols), BF16

    outs = (
        ((4,) + gathered, BF16),
        ((16, D), F32),
        ((2, block, D), BF16),
        ((2, block, D), BF16),
        ((nk, 1), F32),
        half(nq),
        half(nk),
        half(nk),
        half(nq),
        half(D, nq),
        half(D, nq),
        half(D, nq),
        ((QUARTERS, nq, D), BF16),
        ((QUARTERS, nq, D), BF16),
        ((nq, D), F32),
        ((nq, D), F32),
        half(nq),
        ((8, D), F32),
    )
    scratch = (
        ((TILES,) + gathered, BF16),
        ((NP, 2, VROWS, 128 * T), BF16),
        ((T, block, D), BF16),
        ((2, block, D), BF16),
        ((2,) + valid.shape, F32),
        ((16, D), F32),
        ((nk, 1), F32),
        half(nk),
        half(nq),
        half(nk),
        half(nk),
        half(nq),
        ((nq, D), F32),
        half(nq),
        half(D, nq),
        half(D, nq),
        half(D, nq),
        ((QUARTERS, nq, D), BF16),
        ((QUARTERS, nq, D), BF16),
        ((nq, D), F32),
        ((nq, D), F32),
        ((nq, D), F32),
        half(nq),
        ((8, D), F32),
    )
    return pl.pallas_call(
        forward_kernel,
        out_shape=[jax.ShapeDtypeStruct(*o) for o in outs],
        in_specs=[any_space] * 5,
        out_specs=[any_space] * len(outs),
        scratch_shapes=[pltpu.VMEM(*o) for o in scratch]
        + [
            dma((4, 2)),
            dma((3,)),
            dma((2, 2)),
            dma((32,)),
            dma((n, T)),
            dma((n, 2, T)),
            dma((n,)),
            dma((n, 4)),
            dma((n, 4)),
            dma((n,)),
            dma((n,)),
        ],
        name="forward_all",
        compiler_params=pltpu.CompilerParams(
            collective_id=0, has_side_effects=True, vmem_limit_bytes=60 << 20
        ),
    )(w, v, x, cot, valid)


def scatter_kernel(
    at, b, vec, blk, ig, out, vec_out, own_blk, own_ig,
    stage, held, far_in, near_in, line_in, vec_held, vec_in,
    pair_out, pair_in, far_sem, near_sem, line_sem, vec_sem, ex_sem,
):
    spot = place()
    d, t, c, p, px, py, pd = spot
    greet(d, t, c, p, px, py)
    partner = (2 * p + 1 - c, t)
    side = ((2 * px + c, t), (2 * py + c, t))
    swap_b = Exchange(blk, own_blk, ex_sem.at[0], ex_sem.at[1], spot, False)
    swap_i = Exchange(ig, own_ig, ex_sem.at[2], ex_sem.at[3], spot, False)
    half = ROWS // 2

    def pair(j):
        return remote(
            stage.at[lax.rem(j, 2)], held.at[j], pair_out.at[lax.rem(j, 2)], pair_in.at[j], partner
        )

    def far(j, way):
        return remote(
            held.at[j, pd, pl.ds(way * half, half)],
            far_in.at[j, way],
            far_sem.at[0, j, way],
            far_sem.at[1, j, way],
            side[way],
        )

    def near(j, way):
        return remote(
            held.at[j, (px, py)[way]],
            near_in.at[j, way],
            near_sem.at[0, j, way],
            near_sem.at[1, j, way],
            side[way],
        )

    def line(j, tau, way):
        return remote(
            held.at[j, p, :, pl.ds(tau * COLS, COLS)],
            line_in.at[j, way, tau],
            line_sem.at[0, j, way, tau],
            line_sem.at[1, j, way, tau],
            (d, t + (1 if way == 0 else -1)),
        )

    vec_partners = (
        partner,
        side[0],
        side[1],
        (d, t + 1 - 2 * lax.rem(t, 2)),
        (d, t + 2 - 4 * (t // 2)),
    )

    def vec_copy(r):
        return remote(vec_held.at[r], vec_in.at[r], vec_sem.at[0, r], vec_sem.at[1, r], vec_partners[r])

    def product(j, q, core):
        kind = (j + 4) // 4 - (14 - j) // 12
        rows = pl.ds(pl.multiple_of((2 * q + core) * ROWS, ROWS), ROWS)
        return jnp.dot(at[kind, rows], b[j], preferred_element_type=F32)

    vec_held[0] = vec[...]
    vec_copy(0).start()
    swap_b.start()
    swap_i.start()

    def step(s, carry):
        for r in range(5):

            @pl.when(s == 2 * r + 1)
            def _():
                vec_copy(r).wait_recv()
                vec_held[r + 1] = vec_held[r] + vec_in[r]
                if r < 4:
                    vec_copy(r + 1).start()

        @pl.when(s < TILES)
        def _():
            @pl.when(s >= 2)
            def _():
                pair(s - 2).wait_send()

            slot = lax.rem(s, 2)
            for q in range(NP):
                stage[slot, q] = product(s, q, 1 - c).astype(BF16)
            pair(s).start()

        @pl.when(jnp.logical_and(s >= 1, s < TILES + 1))
        def _():
            j = s - 1
            pair(j).wait_recv()
            for q in range(NP):
                held[j, q] = (product(j, q, c) + held[j, q].astype(F32)).astype(BF16)
            for way in range(2):
                far(j, way).start()

        @pl.when(jnp.logical_and(s >= 2, s < TILES + 2))
        def _():
            j = s - 2
            for way in range(2):
                far(j, way).wait_recv()
                part = pl.ds(way * half, half)
                q = (py, px)[way]
                held[j, q, part] = (
                    held[j, q, part].astype(F32) + far_in[j, way].astype(F32)
                ).astype(BF16)
                near(j, 1 - way).start()

        @pl.when(jnp.logical_and(s >= 3, s < TILES + 3))
        def _():
            j = s - 3
            near(j, 0).wait_recv()
            near(j, 1).wait_recv()
            for tau in range(T):
                cols = pl.ds(tau * COLS, COLS)
                total = (
                    held[j, p, :, cols].astype(F32)
                    + near_in[j, 0, :, cols].astype(F32)
                    + near_in[j, 1, :, cols].astype(F32)
                )
                held[j, p, :, cols] = total.astype(BF16)

                @pl.when(t == tau)
                def _():
                    out[j] = total

        for way in range(2):
            hop = t if way == 0 else T - 1 - t
            j = s - 4 - hop

            @pl.when(jnp.logical_and(j >= 0, j < TILES))
            def _():
                for tau in range(T):

                    @pl.when((tau > t) if way == 0 else (tau < t))
                    def _():
                        cols = pl.ds(tau * COLS, COLS)

                        @pl.when(hop > 0)
                        def _():
                            line(j, tau, way).wait_recv()
                            held[j, p, :, cols] = (
                                held[j, p, :, cols].astype(F32) + line_in[j, way, tau].astype(F32)
                            ).astype(BF16)

                        line(j, tau, way).start()

        @pl.when(s >= 8)
        def _():
            j = s - 8
            for way in range(2):

                @pl.when((t > 0) if way == 0 else (t < T - 1))
                def _():
                    for tau in range(T):

                        @pl.when(t == tau)
                        def _():
                            line(j, tau, way).wait_recv()
                            out[j] += line_in[j, way, tau].astype(F32)

        return carry

    lax.fori_loop(0, TILES + 8, step, 0)

    def drain(j, carry):
        for way in range(2):
            far(j, way).wait_send()
            near(j, way).wait_send()
            for tau in range(T):

                @pl.when((tau > t) if way == 0 else (tau < t))
                def _():
                    line(j, tau, way).wait_send()

        return carry

    lax.fori_loop(0, TILES, drain, 0)
    pair(TILES - 2).wait_send()
    pair(TILES - 1).wait_send()
    vec_out[...] = vec_held[5]
    for r in range(5):
        vec_copy(r).wait_send()
    for swap in (swap_b, swap_i):
        for k in range(2):
            swap.wait_in(k)
            swap.wait_out(k)


def scatter_all(at, b, vec, blk, ig):
    any_space = pl.BlockSpec(memory_space=pl.ANY)
    vmem = pl.BlockSpec(memory_space=pltpu.VMEM)
    dma = pltpu.SemaphoreType.DMA
    n = TILES
    return pl.pallas_call(
        scatter_kernel,
        out_shape=(
            jax.ShapeDtypeStruct((n, ROWS, COLS), F32),
            jax.ShapeDtypeStruct(vec.shape, F32),
            jax.ShapeDtypeStruct(blk.shape, BF16),
            jax.ShapeDtypeStruct(ig.shape, BF16),
        ),
        in_specs=[vmem, vmem, vmem, any_space, any_space],
        out_specs=[vmem, vmem, any_space, any_space],
        scratch_shapes=[
            pltpu.VMEM((2, NP, ROWS, D), BF16),
            pltpu.VMEM((n, NP, ROWS, D), BF16),
            pltpu.VMEM((n, 2, ROWS // 2, D), BF16),
            pltpu.VMEM((n, 2, ROWS, D), BF16),
            pltpu.VMEM((n, 2, T, ROWS, COLS), BF16),
            pltpu.VMEM((6,) + vec.shape, F32),
            pltpu.VMEM((5,) + vec.shape, F32),
            dma((2,)),
            dma((n,)),
            dma((2, n, 2)),
            dma((2, n, 2)),
            dma((2, n, 2, T)),
            dma((2, 5)),
            dma((4, 2)),
        ],
        name="scatter_all",
        compiler_params=pltpu.CompilerParams(
            collective_id=1, has_side_effects=True, vmem_limit_bytes=58 << 20
        ),
    )(at, b, vec, blk, ig)


def head_probs(k, q_t, bias):
    s = jnp.dot(k, q_t, preferred_element_type=F32) + bias
    e = jnp.exp(s - jnp.max(s, axis=0, keepdims=True))
    return e / jnp.sum(e, axis=0, keepdims=True)


def head_rows(q_t, h):
    row = lax.broadcasted_iota(jnp.int32, q_t.shape, 0) // HD
    return jnp.where(row == h, q_t, jnp.zeros_like(q_t))


def head_lanes(q, h):
    lane = lax.broadcasted_iota(jnp.int32, q.shape, 1) // HD
    return jnp.where(lane == h, q, jnp.zeros_like(q))


def attend_back_kernel(q, k, v, g, bias, dq, dk, dv):
    q_s = (q[...].astype(F32) * HD ** (-0.5)).astype(BF16)
    q_t = q_s.astype(F32).T.astype(BF16)
    g_t = g[...].astype(F32).T.astype(BF16)
    k_t = k[...].astype(F32).T.astype(BF16)
    parts = []
    dk_sum = jnp.zeros(dk.shape, F32)
    dv_sum = jnp.zeros(dv.shape, F32)
    for h in range(2):
        probs = head_probs(k[...], head_rows(q_t, h), bias[...])
        dv_sum += jnp.dot(probs.astype(BF16), head_lanes(g[...], h), preferred_element_type=F32)
        dp = jnp.dot(v[...], head_rows(g_t, h), preferred_element_type=F32)
        ds = (probs * (dp - jnp.sum(dp * probs, axis=0, keepdims=True))).astype(BF16)
        parts.append(jnp.dot(k_t[h * HD : (h + 1) * HD], ds, preferred_element_type=F32))
        dk_sum += jnp.dot(ds, head_lanes(q_s, h), preferred_element_type=F32)
    dq[...] = (jnp.concatenate(parts, axis=0).T * HD ** (-0.5)).astype(BF16)
    dk[...] = dk_sum.astype(dk.dtype)
    dv[...] = dv_sum.astype(dv.dtype)


def columns(rows):
    return pl.BlockSpec((rows, 2 * HD), lambda i: (0, i))


def attend_back(q, k, v, g, bias):
    nq, nk = q.shape[0], k.shape[0]
    return pl.pallas_call(
        attend_back_kernel,
        grid=(H // 2,),
        out_shape=(
            jax.ShapeDtypeStruct((nq, D), BF16),
            jax.ShapeDtypeStruct((nk, D), BF16),
            jax.ShapeDtypeStruct((nk, D), BF16),
        ),
        in_specs=[
            columns(nq),
            columns(nk),
            columns(nk),
            columns(nq),
            pl.BlockSpec((nk, 1), lambda i: (0, 0)),
        ],
        out_specs=(columns(nq), columns(nk), columns(nk)),
        name="attend_back",
        compiler_params=pltpu.CompilerParams(vmem_limit_bytes=48 << 20),
    )(q, k, v, g, bias)


def norm_parts(values):
    center = values - jnp.mean(values, axis=-1, keepdims=True)
    spread = jnp.mean(center * center, axis=-1, keepdims=True)
    inverse = lax.rsqrt(spread + EPS)
    return center * inverse, inverse


def norm_back(grad, unit, inverse, gain):
    scaled = grad * gain
    return inverse * (
        scaled
        - jnp.mean(scaled, axis=-1, keepdims=True)
        - unit * jnp.mean(scaled * unit, axis=-1, keepdims=True)
    )


def dot_nn(a, b):
    return lax.dot_general(a, b, (((1,), (0,)), ((), ())), preferred_element_type=F32)


def dot_nt(a, b):
    return lax.dot_general(a, b, (((1,), (1,)), ((), ())), preferred_element_type=F32)


def per_device_chips(
    activations, cotangent, token_valid, image_counts, pre_gain, pre_shift, attn_weight,
    attn_bias, proj_weight, proj_bias, mid_gain, mid_shift, up_weight, up_bias, down_weight,
    down_bias,
):
    local_rows = activations.shape[0]
    slots = activations.shape[1]
    block = -(-local_rows // 16) * 16
    pad = block - local_rows
    d = lax.axis_index("dp")
    t = lax.axis_index("tensor")
    c = lax.rem(d, 2)
    first_row = t * local_rows
    my_valid = lax.dynamic_slice_in_dim(token_valid, first_row, local_rows, 1).astype(F32)
    slot_live = (jnp.arange(slots, dtype=jnp.int32) < image_counts[0]).astype(F32)
    out_mask = jnp.transpose(slot_live[:, None] * my_valid)[:, :, None]

    def to_blocks(a):
        return jnp.pad(jnp.transpose(a, (1, 0, 2)), ((0, 0), (0, pad), (0, 0)))

    x_blocks = to_blocks(activations)
    c_blocks = to_blocks((cotangent.astype(F32) * out_mask).astype(BF16))
    valid = jnp.pad(
        token_valid.astype(F32).reshape(slots, T, local_rows), ((0, 0), (0, 0), (0, pad))
    ).reshape(slots, T * block)
    valid = jnp.pad(valid, ((0, 8 - slots), (0, 0)))
    per_j = up_weight.shape[1] // COLS
    w = jnp.concatenate(
        [
            attn_weight,
            jnp.transpose(proj_weight)[None],
            jnp.transpose(up_weight.reshape(ROWS, per_j, COLS), (1, 0, 2)),
            jnp.transpose(down_weight.reshape(per_j, COLS, ROWS), (0, 2, 1)),
        ],
        axis=0,
    )
    v = jnp.concatenate(
        [
            jnp.stack([pre_gain, pre_shift, proj_bias, mid_gain, mid_shift, down_bias]),
            attn_bias.reshape(-1, 128),
            up_bias.reshape(-1, 128),
        ],
        axis=0,
    )
    v = jnp.pad(v, ((0, VROWS - v.shape[0]), (0, 0)))
    (
        full_w, vec, x_own, own_cot, bias, queries, keys, values, attended, normed_t, normed2_t,
        mlp_grad_t, hidden, pre_grad, normed2_grad, resid, block_own, up_sums,
    ) = forward_all(w, v, x_blocks, c_blocks, valid)
    g = full_w.reshape(4, D, D)
    nq = resid.shape[0]
    gain_one, gain_two = vec[0:1], vec[3:4]
    unit_one, inverse_one = norm_parts(x_own.reshape(nq, D).astype(F32))

    def mine(a):
        return lax.dynamic_slice_in_dim(a, c * nq, nq, 0)

    def other(a):
        return lax.dynamic_slice_in_dim(a, (1 - c) * nq, nq, 0)

    unit_two, inverse_two = norm_parts(resid)
    outer = own_cot.reshape(nq, D).astype(F32)
    resid_grad = outer + norm_back(normed2_grad, unit_two, inverse_two, gain_two)
    branch = resid_grad.astype(BF16)
    att_grad = dot_nn(branch, g[3]).astype(BF16)
    dq, dk, dv = attend_back(queries, keys, values, att_grad, bias)
    swap = [(i, i + 1 - 2 * (i % 2)) for i in range(2 * NP)]
    dkv = jnp.concatenate([dk, dv], axis=1)
    came = lax.ppermute(other(dkv), "dp", swap)
    dkv = (mine(dkv).astype(F32) + came.astype(F32)).astype(BF16)
    dk, dv = dkv[:, :D], dkv[:, D:]
    normed_grad = dot_nt(dq, g[0]) + dot_nt(dk, g[1]) + dot_nt(dv, g[2])
    input_own = resid_grad + norm_back(normed_grad, unit_one, inverse_one, gain_one)
    sums = jnp.stack(
        [
            jnp.sum(normed_grad * unit_one, axis=0),
            jnp.sum(normed_grad, axis=0),
            jnp.sum(branch.astype(F32), axis=0),
            jnp.sum(normed2_grad * unit_two, axis=0),
            jnp.sum(normed2_grad, axis=0),
            jnp.sum(outer, axis=0),
            jnp.sum(dq.astype(F32), axis=0),
            jnp.sum(dv.astype(F32), axis=0),
        ]
        + [up_sums[j] for j in range(QUARTERS)]
    )
    at = jnp.stack([normed_t, jnp.transpose(branch), normed2_t, mlp_grad_t])
    b = jnp.concatenate([jnp.stack([dq, dk, dv, attended]), pre_grad, hidden], axis=0)
    grads, totals, own_block, own_input = scatter_all(
        at,
        b,
        sums.reshape(-1, 128),
        block_own.reshape(2, block, D),
        input_own.astype(BF16).reshape(2, block, D),
    )
    totals = totals.reshape(-1, D)
    owned = lax.dynamic_slice(totals, (0, d * ROWS), (6, ROWS))
    parted = lax.dynamic_slice(totals, (0, t * COLS), (totals.shape[0], COLS))

    def from_blocks(a):
        return jnp.transpose(a[:, :local_rows], (1, 0, 2))

    block_out = (from_blocks(own_block).astype(F32) * out_mask).astype(BF16)
    input_grad = from_blocks(own_input).astype(F32)
    return (
        block_out,
        input_grad,
        owned[0],
        owned[1],
        grads[0:3],
        parted[6:8],
        jnp.transpose(grads[3]),
        owned[2],
        owned[3],
        owned[4],
        jnp.transpose(grads[4 : 4 + per_j], (1, 0, 2)).reshape(ROWS, per_j * COLS),
        parted[8 : 8 + per_j].reshape(-1),
        jnp.transpose(grads[4 + per_j :], (0, 2, 1)).reshape(per_j * COLS, ROWS),
        owned[5],
    )


def solution(mesh):
    sizes = (mesh.shape["dp"], mesh.shape["tensor"])
    per_device = per_device_chips if sizes == (2 * NP, T) else per_device_general
    return jax.shard_map(
        per_device,
        mesh=mesh,
        in_specs=(
            P("tensor", "dp", None),
            P("tensor", "dp", None),
            P("dp", None),
            P("dp"),
            P("dp"),
            P("dp"),
            P(None, "dp", "tensor"),
            P(None, "tensor"),
            P("tensor", "dp"),
            P("dp"),
            P("dp"),
            P("dp"),
            P("dp", "tensor"),
            P("tensor"),
            P("tensor", "dp"),
            P("dp"),
        ),
        out_specs=(
            P("tensor", "dp", None),
            P("tensor", "dp", None),
            P("dp"),
            P("dp"),
            P(None, "dp", "tensor"),
            P(None, "tensor"),
            P("tensor", "dp"),
            P("dp"),
            P("dp"),
            P("dp"),
            P("dp", "tensor"),
            P("tensor"),
            P("tensor", "dp"),
            P("dp"),
        ),
        check_vma=False,
    )
```

```python
import functools

import jax
import jax.numpy as jnp
from jax import lax
from jax.experimental import pallas as pl
from jax.experimental.pallas import tpu as pltpu
from jax.sharding import PartitionSpec as P

D = 1024
H = 16
HD = 64
MB = 2


EPS = 1e-06
NEG = -1000000000.0


def layer_norm(values, gain, shift):
    center = values - jnp.mean(values, axis=-1, keepdims=True)
    spread = jnp.mean(center * center, axis=-1, keepdims=True)
    return center * lax.rsqrt(spread + EPS) * gain + shift


def gelu_exact(values):
    return jax.nn.gelu(values, approximate=False)


def per_device_general(
    activations,
    cotangent,
    token_valid,
    image_counts,
    pre_gain,
    pre_shift,
    attn_weight,
    attn_bias,
    proj_weight,
    proj_bias,
    mid_gain,
    mid_shift,
    up_weight,
    up_bias,
    down_weight,
    down_bias,
):
    f32 = jnp.float32
    bf16 = jnp.bfloat16
    tensor_size = lax.axis_size("tensor")
    local_rows = activations.shape[0]
    slots = activations.shape[1]
    per_micro = slots // MB
    heads_here = H // tensor_size
    width_here = attn_weight.shape[2]
    hidden_here = up_weight.shape[1]
    scale = HD ** (-0.5)
    first_row = lax.axis_index("tensor") * local_rows
    my_valid = lax.dynamic_slice_in_dim(token_valid, first_row, local_rows, 1).astype(f32)
    slot_live = (jnp.arange(slots, dtype=jnp.int32) < image_counts[0]).astype(f32)
    attn_bias_f = attn_bias.astype(f32)
    up_bias_f = up_bias.astype(f32)
    acc_attn = jnp.zeros((3, D, width_here), f32)
    acc_proj = jnp.zeros((width_here, D), f32)
    acc_up = jnp.zeros((D, hidden_here), f32)
    acc_down = jnp.zeros((hidden_here, D), f32)
    acc_attn_bias = jnp.zeros((2, width_here), f32)
    acc_up_bias = jnp.zeros((hidden_here,), f32)
    acc_vectors = [jnp.zeros((D,), f32) for unused in range(6)]
    block_parts = []
    input_parts = []
    for micro_step in range(MB):
        gathered = (
            lax.all_gather(attn_weight, "dp", axis=1, tiled=True),
            lax.all_gather(proj_weight, "dp", axis=1, tiled=True),
            lax.all_gather(up_weight, "dp", axis=0, tiled=True),
            lax.all_gather(down_weight, "dp", axis=1, tiled=True),
            lax.all_gather(pre_gain, "dp", axis=0, tiled=True),
            lax.all_gather(pre_shift, "dp", axis=0, tiled=True),
            lax.all_gather(proj_bias, "dp", axis=0, tiled=True),
            lax.all_gather(mid_gain, "dp", axis=0, tiled=True),
            lax.all_gather(mid_shift, "dp", axis=0, tiled=True),
            lax.all_gather(down_bias, "dp", axis=0, tiled=True),
        )
        qkv_full, proj_full, upw_full, downw_full = (
            gathered[0],
            gathered[1],
            gathered[2],
            gathered[3],
        )
        gain_one, shift_one, proj_bias_f, gain_two, shift_two, down_bias_f = [
            item.astype(f32) for item in gathered[4:]
        ]
        offset = micro_step * per_micro
        inputs_f = activations[:, offset : offset + per_micro].astype(f32)
        key_valid = token_valid[offset : offset + per_micro]
        key_bias = jnp.where(key_valid > 0, 0.0, NEG).astype(f32)
        out_mask = jnp.transpose(
            slot_live[offset : offset + per_micro][:, None] * my_valid[offset : offset + per_micro]
        )[:, :, None]
        normed = layer_norm(inputs_f, gain_one, shift_one).astype(bf16)
        normed_all = lax.all_gather(normed, "tensor", axis=0, tiled=True)
        full_rows = normed_all.shape[0]
        projected = jnp.einsum("sid,cde->csie", normed_all, qkv_full, preferred_element_type=f32)
        queries = (
            (projected[0] + attn_bias_f[0])
            .astype(bf16)
            .reshape(full_rows, per_micro, heads_here, HD)
        )
        keys = projected[1].astype(bf16).reshape(full_rows, per_micro, heads_here, HD)
        values = (
            (projected[2] + attn_bias_f[1])
            .astype(bf16)
            .reshape(full_rows, per_micro, heads_here, HD)
        )

        def scores_of(query_part, key_part):
            raw = jnp.einsum("qihe,kihe->ihqk", query_part, key_part, preferred_element_type=f32)
            return raw * scale + key_bias[:, None, None, :]

        scores = scores_of(queries, keys)
        top = jnp.max(scores, axis=-1, keepdims=True)
        expo = jnp.exp(scores - top)
        total = jnp.sum(expo, axis=-1, keepdims=True)
        logsum = top + jnp.log(total)
        probs_low = (expo / total).astype(bf16)
        attended = (
            jnp.einsum("ihqk,kihe->qihe", probs_low, values, preferred_element_type=f32)
            .astype(bf16)
            .reshape(full_rows, per_micro, width_here)
        )
        resid = (
            inputs_f
            + lax.psum_scatter(
                jnp.einsum("sie,ed->sid", attended, proj_full, preferred_element_type=f32),
                "tensor",
                scatter_dimension=0,
                tiled=True,
            )
            + proj_bias_f
        )
        normed2 = layer_norm(resid, gain_two, shift_two).astype(bf16)
        normed2_all = lax.all_gather(normed2, "tensor", axis=0, tiled=True)
        hidden_pre = (
            jnp.einsum("sid,df->sif", normed2_all, upw_full, preferred_element_type=f32) + up_bias_f
        )
        hidden = gelu_exact(hidden_pre).astype(bf16)
        mlp_out = (
            lax.psum_scatter(
                jnp.einsum("sif,fd->sid", hidden, downw_full, preferred_element_type=f32).astype(
                    jnp.bfloat16
                ),
                "tensor",
                scatter_dimension=0,
                tiled=True,
            ).astype(jnp.float32)
            + down_bias_f
        )
        block_parts.append(((resid + mlp_out) * out_mask).astype(bf16))
        outer = cotangent[:, offset : offset + per_micro].astype(f32) * out_mask
        mlp_grad = outer.astype(bf16)
        acc_vectors[5] = acc_vectors[5] + jnp.sum(mlp_grad.astype(f32), axis=(0, 1))
        mlp_grad_all = lax.all_gather(mlp_grad, "tensor", axis=0, tiled=True)
        acc_down = acc_down + jnp.einsum(
            "sif,sid->fd", hidden, mlp_grad_all, preferred_element_type=f32
        )
        hidden_grad = jnp.einsum(
            "sid,fd->sif", mlp_grad_all, downw_full, preferred_element_type=f32
        )
        unused, gelu_back = jax.vjp(gelu_exact, hidden_pre)
        pre_grad = gelu_back(hidden_grad)[0].astype(bf16)
        acc_up_bias = acc_up_bias + jnp.sum(pre_grad.astype(f32), axis=(0, 1))
        acc_up = acc_up + jnp.einsum(
            "sid,sif->df", normed2_all, pre_grad, preferred_element_type=f32
        )
        normed2_grad = lax.psum_scatter(
            jnp.einsum("sif,df->sid", pre_grad, upw_full, preferred_element_type=f32),
            "tensor",
            scatter_dimension=0,
            tiled=True,
        )
        unused, second_back = jax.vjp(layer_norm, resid, gain_two, shift_two)
        resid_part, gain_two_grad, shift_two_grad = second_back(normed2_grad)
        acc_vectors[3] = acc_vectors[3] + gain_two_grad
        acc_vectors[4] = acc_vectors[4] + shift_two_grad
        resid_grad = outer + resid_part
        branch_grad = resid_grad.astype(bf16)
        acc_vectors[2] = acc_vectors[2] + jnp.sum(branch_grad.astype(f32), axis=(0, 1))
        branch_all = lax.all_gather(branch_grad, "tensor", axis=0, tiled=True)
        acc_proj = acc_proj + jnp.einsum(
            "sie,sid->ed", attended, branch_all, preferred_element_type=f32
        )
        att_grad = (
            jnp.einsum("sid,ed->sie", branch_all, proj_full, preferred_element_type=f32)
            .astype(bf16)
            .reshape(full_rows, per_micro, heads_here, HD)
        )
        probs = jnp.exp(scores_of(queries, keys) - logsum)
        probs_again = probs.astype(bf16)
        value_grad = jnp.einsum(
            "ihqk,qihe->kihe", probs_again, att_grad, preferred_element_type=f32
        ).astype(bf16)
        prob_grad = jnp.einsum("qihe,kihe->ihqk", att_grad, values, preferred_element_type=f32)
        score_grad = (
            probs * (prob_grad - jnp.sum(prob_grad * probs, axis=-1, keepdims=True))
        ).astype(bf16)
        query_grad = (
            jnp.einsum("ihqk,kihe->qihe", score_grad, keys, preferred_element_type=f32) * scale
        ).astype(bf16)
        key_grad = (
            jnp.einsum("ihqk,qihe->kihe", score_grad, queries, preferred_element_type=f32) * scale
        ).astype(bf16)
        qkv_grad = jnp.stack([query_grad, key_grad, value_grad]).reshape(
            3, full_rows, per_micro, width_here
        )
        acc_attn_bias = acc_attn_bias + jnp.stack(
            [
                jnp.sum(qkv_grad[0].astype(f32), axis=(0, 1)),
                jnp.sum(qkv_grad[2].astype(f32), axis=(0, 1)),
            ]
        )
        acc_attn = acc_attn + jnp.einsum(
            "sid,csie->cde", normed_all, qkv_grad, preferred_element_type=f32
        )
        normed_grad = lax.psum_scatter(
            jnp.einsum("csie,cde->sid", qkv_grad, qkv_full, preferred_element_type=f32),
            "tensor",
            scatter_dimension=0,
            tiled=True,
        )
        unused, first_back = jax.vjp(layer_norm, inputs_f, gain_one, shift_one)
        input_part, gain_one_grad, shift_one_grad = first_back(normed_grad)
        acc_vectors[0] = acc_vectors[0] + gain_one_grad
        acc_vectors[1] = acc_vectors[1] + shift_one_grad
        input_parts.append(resid_grad + input_part)
    summed = lax.psum(
        (
            acc_vectors[0],
            acc_vectors[1],
            acc_vectors[2],
            acc_vectors[3],
            acc_vectors[4],
            acc_vectors[5],
        ),
        "tensor",
    )
    owned = (
        lax.psum_scatter(acc_attn, "dp", scatter_dimension=1, tiled=True),
        lax.psum_scatter(acc_proj, "dp", scatter_dimension=1, tiled=True),
        lax.psum_scatter(acc_up, "dp", scatter_dimension=0, tiled=True),
        lax.psum_scatter(acc_down, "dp", scatter_dimension=1, tiled=True),
        lax.psum_scatter(summed[0], "dp", scatter_dimension=0, tiled=True),
        lax.psum_scatter(summed[1], "dp", scatter_dimension=0, tiled=True),
        lax.psum_scatter(summed[2], "dp", scatter_dimension=0, tiled=True),
        lax.psum_scatter(summed[3], "dp", scatter_dimension=0, tiled=True),
        lax.psum_scatter(summed[4], "dp", scatter_dimension=0, tiled=True),
        lax.psum_scatter(summed[5], "dp", scatter_dimension=0, tiled=True),
    )
    bias_sums = lax.psum((acc_attn_bias, acc_up_bias), "dp")
    block_out = jnp.concatenate(block_parts, axis=1)
    input_grad = jnp.concatenate(input_parts, axis=1)
    return (
        block_out,
        input_grad,
        owned[4],
        owned[5],
        owned[0],
        bias_sums[0],
        owned[1],
        owned[6],
        owned[7],
        owned[8],
        owned[2],
        bias_sums[1],
        owned[3],
        owned[9],
    )

MESH = pl.DeviceIdType.MESH
F32 = jnp.float32
BF16 = jnp.bfloat16
TILES = 12
T = 4
NP = 4
ROWS = D // (2 * NP)
COLS = D // T
VROWS = 32


def place():
    d = lax.axis_index("dp")
    t = lax.axis_index("tensor")
    c = lax.rem(d, 2)
    p = d // 2
    px = p + 1 - 2 * lax.rem(p, 2)
    py = p + 2 - 4 * (p // 2)
    return d, t, c, p, px, py, 3 - p


def greet(d, t, c, p, px, py):
    barrier = pltpu.get_barrier_semaphore()
    me = c * T + t
    for step in range(1, 2 * T):
        other = lax.rem(me + step, 2 * T)
        pl.semaphore_signal(
            barrier, inc=1, device_id=(2 * p + other // T, lax.rem(other, T)), device_id_type=MESH
        )
    for q in (px, py):
        pl.semaphore_signal(barrier, inc=1, device_id=(2 * q + c, t), device_id_type=MESH)
    pl.semaphore_wait(barrier, 2 * T + 1)


def remote(src, dst, send, recv, device):
    return pltpu.make_async_remote_copy(
        src_ref=src,
        dst_ref=dst,
        send_sem=send,
        recv_sem=recv,
        device_id=device,
        device_id_type=MESH,
    )


class Exchange:
    def __init__(self, src, dst, send, recv, spot, full):
        d, t, c, p, px, py, pd = spot
        self.c, self.t, self.p = c, t, p
        self.src, self.dst, self.send, self.recv = src, dst, send, recv
        self.full = full

    def slot_out(self):
        return self.t if self.full else lax.rem(self.t, 2)

    def slot_in(self, k):
        return 2 * self.c + k if self.full else k

    def mine(self, k):
        return jnp.logical_and(self.t // 2 == self.c, lax.rem(self.t, 2) == k)

    def copy(self, k):
        return remote(
            self.src.at[k],
            self.dst.at[self.slot_out()],
            self.send.at[k],
            self.recv.at[lax.rem(self.t, 2)],
            (2 * self.p + self.t // 2, 2 * self.c + k),
        )

    def local(self, k):
        return pltpu.make_async_copy(
            self.src.at[k], self.dst.at[self.slot_out()], self.send.at[k]
        )

    def start(self):
        for k in range(2):

            @pl.when(self.mine(k))
            def _():
                self.local(k).start()

            @pl.when(jnp.logical_not(self.mine(k)))
            def _():
                self.copy(k).start()

    def wait_in(self, k):
        @pl.when(self.mine(k))
        def _():
            self.local(k).wait()

        @pl.when(jnp.logical_not(self.mine(k)))
        def _():
            remote(
                self.src.at[k],
                self.dst.at[self.slot_in(k)],
                self.send.at[k],
                self.recv.at[k],
                (2 * self.p + self.t // 2, 2 * self.c + k),
            ).wait_recv()

    def wait_out(self, k):
        @pl.when(jnp.logical_not(self.mine(k)))
        def _():
            self.copy(k).wait_send()


class Gather:
    def __init__(self, src, dst, sems, j, spot):
        self.d, self.t, self.c, self.p, self.px, self.py, self.pd = spot
        self.src, self.dst, self.j = src, dst, j
        self.zin, self.zout, self.own_sem, self.rin, self.rout, self.cin, self.cout = sems
        self.half = src.shape[0] // 2
        self.width = src.shape[1]

    def row(self, q):
        return self.dst.at[q, self.c]

    def cell(self, tau):
        start = pl.multiple_of(tau * self.width, self.width)
        return self.dst.at[self.p, self.c, :, pl.ds(start, self.width)]

    def local(self):
        return pltpu.make_async_copy(self.src, self.cell(self.t), self.own_sem.at[self.j])

    def line(self, tau, way, k):
        src = self.src if k == 0 else self.cell(tau)
        return remote(
            src,
            self.cell(tau),
            self.zout.at[self.j, way, k],
            self.zin.at[self.j, tau],
            (self.d, self.t + (1 if way == 0 else -1)),
        )

    def own(self):
        self.local().start()

        @pl.when(self.t < T - 1)
        def _():
            self.line(self.t, 0, 0).start()

        @pl.when(self.t > 0)
        def _():
            self.line(self.t, 1, 0).start()

    def hop(self, k):
        t = self.t

        @pl.when(t >= k)
        def _():
            self.line(t - k, 0, k).wait_recv()

            @pl.when(t < T - 1)
            def _():
                self.line(t - k, 0, k).start()

        @pl.when(t + k < T)
        def _():
            self.line(t + k, 1, k).wait_recv()

            @pl.when(t > 0)
            def _():
                self.line(t + k, 1, k).start()

    def side(self, way):
        q = self.px if way == 0 else self.py
        return (2 * q + self.c, self.t)

    def near(self, way):
        return remote(
            self.row(self.p),
            self.row(self.p),
            self.rout.at[self.j, way],
            self.rin.at[self.j, way],
            self.side(way),
        )

    def near_in(self, way):
        q = self.px if way == 0 else self.py
        return remote(
            self.row(q), self.row(q), self.rout.at[self.j, way], self.rin.at[self.j, way], self.side(way)
        )

    def far(self, way):
        q = self.px if way == 0 else self.py
        part = self.row(q).at[pl.ds(way * self.half, self.half)]
        return remote(
            part, part, self.rout.at[self.j, 2 + way], self.rin.at[self.j, 2 + way], self.side(1 - way)
        )

    def far_in(self, way):
        part = self.row(self.pd).at[pl.ds(way * self.half, self.half)]
        return remote(
            part, part, self.rout.at[self.j, 2 + way], self.rin.at[self.j, 2 + way], self.side(1 - way)
        )

    def ring_one(self):
        self.local().wait()
        self.near(0).start()
        self.near(1).start()

    def ring_two(self):
        for way in range(2):
            self.near_in(way).wait_recv()
            self.far(way).start()

    def pair(self, c):
        return remote(
            self.dst.at[:, c],
            self.dst.at[:, c],
            self.cout.at[self.j],
            self.cin.at[self.j],
            (2 * self.p + 1 - self.c, self.t),
        )

    def ring_three(self):
        for way in range(2):
            self.far_in(way).wait_recv()
        self.pair(self.c).start()

    def ready(self):
        self.pair(1 - self.c).wait_recv()

    def finish(self):
        t = self.t
        for k in range(T):

            @pl.when(jnp.logical_and(t >= k, t < T - 1))
            def _():
                self.line(t - k, 0, k).wait_send()

            @pl.when(jnp.logical_and(t + k < T, t > 0))
            def _():
                self.line(t + k, 1, k).wait_send()

        for way in range(2):
            self.near(way).wait_send()
            self.far(way).wait_send()
        self.pair(self.c).wait_send()


LAGS = (1, 2, 3, 5, 7)
ORDER = (0, 1, 2, 3, 4, 8, 5, 9, 6, 10, 7, 11)
QUARTERS = 4
TILE = 256


def tiles(n, size, body):
    def run(i, carry):
        body(pl.ds(pl.multiple_of(i * size, size), size), i)
        return carry

    lax.fori_loop(0, n // size, run, 0)


def to_lanes(a):
    return a.astype(F32).T.astype(BF16)


def matrix(w, j, cols=None):
    a = w[j] if cols is None else w[j, :, :, :, cols]
    return a.reshape(D, a.shape[-1])


def matrix_rows(w, j, n):
    return w[j, n].reshape(2 * ROWS, D)


def forward_kernel(
    w, v, x, cot, valid,
    o_w, o_vec, o_x, o_cot, o_bias, o_q, o_k, o_v, o_att, o_nt, o_n2t, o_mgt, o_hid, o_pre,
    o_n2g, o_resid, o_blk, o_ups,
    gw, gv, xf, cf, mf, vec, bias, normed, q_s, k_s, v_s, att, resid, n2, nt, n2t, mgt, hid, pre,
    n2g, mlp, slope, blk, ups,
    ex_sem, mask_sem, pass_sem, out_sem, *chunk_sems,
):
    spot = place()
    d, t, c, p, px, py, pd = spot
    greet(d, t, c, p, px, py)
    partner = (2 * p + 1 - c, t)
    swap_x = Exchange(x, xf, ex_sem.at[0], ex_sem.at[1], spot, True)
    swap_c = Exchange(cot, cf, ex_sem.at[2], ex_sem.at[3], spot, False)
    mask_out = remote(valid, mf.at[c], mask_sem.at[0], mask_sem.at[1], partner)
    mask_in = remote(valid, mf.at[1 - c], mask_sem.at[0], mask_sem.at[1], partner)
    mask_own = pltpu.make_async_copy(valid, mf.at[c], mask_sem.at[2])

    def passed(core, k):
        view = xf.at[2 * core + k]
        return remote(view, view, pass_sem.at[0, k], pass_sem.at[1, k], partner)

    chunks = [Gather(v, gv, chunk_sems, 0, spot)]
    for i, j in enumerate(ORDER):
        chunks.append(Gather(w.at[j], gw.at[j], chunk_sems, i + 1, spot))
    count = len(chunks)

    def comm(s):
        for lag, stage in (
            (LAGS[4], lambda g: g.ring_three()),
            (LAGS[3], lambda g: g.ring_two()),
            (LAGS[2], lambda g: (g.hop(3), g.ring_one())),
            (LAGS[1], lambda g: g.hop(2)),
            (LAGS[0], lambda g: g.hop(1)),
            (0, lambda g: g.own()),
        ):
            if 0 <= s - lag < count:
                stage(chunks[s - lag])
        if s == 1:
            swap_x.start()
            mask_out.start()
            mask_own.start()
        if s == 4:
            for k in range(2):
                swap_x.wait_in(k)
                passed(c, k).start()
        if s == 8:
            swap_c.start()

    nq = q_s.shape[0]
    nk = k_s.shape[0]
    block = xf.shape[1]
    own_rows = pl.ds(pl.multiple_of(c * nq, nq), nq)
    copies = []

    def emit(src, dst):
        copy = pltpu.make_async_copy(src, dst, out_sem.at[len(copies)])
        copy.start()
        copies.append(copy)

    def vectors():
        for q in range(NP):
            for core in range(2):
                part = gv[q, core].astype(F32)
                first = (2 * q + core) * ROWS
                vec[0:6, first : first + ROWS] = part[0:6, 0:ROWS]
        part = gv[0, 0].astype(F32)
        per = COLS // 128
        for i in range(2 + QUARTERS):
            for tau in range(T):
                for r in range(per):
                    row = 6 + i * per + r
                    at = tau * COLS + r * 128
                    vec[6 + i : 7 + i, at : at + 128] = part[row : row + 1, tau * 128 : tau * 128 + 128]
        emit(vec, o_vec)
        mask_in.wait_recv()
        mask_own.wait()
        rows = mf[t // 2].T
        col = jnp.where(lax.rem(t, 2) == 0, rows[:, 0:1], rows[:, 1:2])
        bias[...] = jnp.where(col > 0, 0.0, NEG).astype(F32)
        emit(bias, o_bias)

    def norm_one():
        for k in range(2):
            passed(1 - c, k).wait_recv()
        emit(xf.at[pl.ds(2 * c, 2)], o_x)
        size = 32
        per = block // size

        def run(i, carry):
            at = pl.ds(pl.multiple_of(lax.rem(i, per) * size, size), size)
            unit, unused = norm_parts(xf[i // per, at].astype(F32))
            normed[pl.ds(pl.multiple_of(i * size, size), size)] = (
                unit * vec[0:1] + vec[1:2]
            ).astype(BF16)
            return carry

        lax.fori_loop(0, nk // size, run, 0)

        def flip(cols, i):
            nt[cols] = to_lanes(normed[own_rows, cols])

        tiles(D, TILE, flip)
        emit(nt, o_nt)

    def project(j, dst, rows, shift):
        a = normed[rows]

        def run(cols, i):
            out = jnp.dot(a, matrix(gw, j, cols), preferred_element_type=F32)
            if shift is not None:
                out = out + vec[shift : shift + 1, cols]
            dst[:, cols] = out.astype(BF16)

        tiles(D, TILE, run)

    def heads(first, last):
        def run(i, carry):
            cols = pl.ds(pl.multiple_of(i * 2 * HD, 2 * HD), 2 * HD)
            q_t = (q_s[:, cols].astype(F32).T * HD ** (-0.5)).astype(BF16)
            v_t = to_lanes(v_s[:, cols])
            k = k_s[:, cols]
            parts = []
            for h in range(2):
                probs = head_probs(k, head_rows(q_t, h), bias[...]).astype(BF16)
                parts.append(
                    jnp.dot(v_t[h * HD : (h + 1) * HD], probs, preferred_element_type=F32)
                )
            att[:, cols] = jnp.concatenate(parts, axis=0).T.astype(BF16)
            return carry

        lax.fori_loop(first, last, run, 0)

    def middle():
        emit(att, o_att)
        a = att[...]
        x_own = xf.at[pl.ds(2 * c, 2)]

        def run(cols, i):
            out = dot_nt(a, matrix_rows(gw, 3, i))
            resid[:, cols] = (
                x_own[:, :, cols].astype(F32).reshape(nq, TILE) + out + vec[2:3, cols]
            )

        tiles(D, TILE, run)
        emit(resid, o_resid)

        def norm(rows, i):
            unit, unused = norm_parts(resid[rows])
            n2[rows] = (unit * vec[3:4] + vec[4:5]).astype(BF16)

        tiles(nq, 64, norm)

        def flip(cols, i):
            n2t[cols] = to_lanes(n2[:, cols])

        tiles(D, TILE, flip)
        emit(n2t, o_n2t)

    def grads_in():
        for k in range(2):
            swap_c.wait_in(k)
        emit(cf, o_cot)

        def flip(cols, i):
            mgt[cols] = to_lanes(cf[:, :, cols].reshape(nq, TILE))

        tiles(D, TILE, flip)
        emit(mgt, o_mgt)

    def quarter_up(j):
        a = n2[...]

        def run(cols, i):
            z = jnp.dot(a, matrix(gw, 4 + j, cols), preferred_element_type=F32)
            z = z + vec[8 + j : 9 + j, cols]
            share = 0.5 + 0.5 * lax.erf(z * 0.5**0.5)
            hid[j, :, cols] = (z * share).astype(BF16)
            slope[:, cols] = share + z * (jnp.exp(-0.5 * z * z) * (0.5 / jnp.pi) ** 0.5)

        tiles(D, TILE, run)
        emit(hid.at[j], o_hid.at[j])

    def quarter_down(j):
        g = cf[...].reshape(nq, D)

        def back(cols, i):
            h = jnp.dot(g, matrix(gw, 8 + j, cols), preferred_element_type=F32)
            grad = (slope[:, cols] * h).astype(BF16)
            pre[j, :, cols] = grad
            ups[j : j + 1, cols] = jnp.sum(grad.astype(F32), axis=0, keepdims=True)

        tiles(D, TILE, back)
        emit(pre.at[j], o_pre.at[j])

        def outs(cols, i):
            m = dot_nt(hid[j], matrix_rows(gw, 8 + j, i))
            n = dot_nt(pre[j], matrix_rows(gw, 4 + j, i))
            if j == 0:
                mlp[:, cols] = m
                n2g[:, cols] = n
            elif j < QUARTERS - 1:
                mlp[:, cols] += m
                n2g[:, cols] += n
            else:
                n2g[:, cols] += n
                blk[:, cols] = (resid[:, cols] + mlp[:, cols] + m + vec[5:6, cols]).astype(BF16)

        tiles(D, TILE, outs)

    whole = pl.ds(0, nk)
    after = {
        8: (vectors, norm_one),
        9: (lambda: project(0, q_s, own_rows, 6), lambda: emit(q_s, o_q)),
        10: (lambda: project(1, k_s, whole, None), lambda: emit(k_s, o_k)),
        11: (lambda: project(2, v_s, whole, 7), lambda: emit(v_s, o_v), lambda: heads(0, 2)),
        12: (lambda: heads(2, 6),),
        13: (lambda: heads(6, 8), middle),
        14: (lambda: quarter_up(0), grads_in, lambda: quarter_down(0)),
        15: (lambda: quarter_up(1),),
        16: (lambda: quarter_down(1),),
        17: (lambda: quarter_up(2),),
        18: (lambda: quarter_down(2),),
        19: (lambda: quarter_up(3),),
        20: (lambda: quarter_down(3),),
    }
    for s in range(count + LAGS[4] + 1):
        comm(s)
        if 0 <= s - LAGS[4] - 1 < count:
            i = s - LAGS[4] - 1
            chunks[i].ready()
            if 1 <= i <= 4:
                emit(gw.at[ORDER[i - 1]], o_w.at[ORDER[i - 1]])
        for unit in after.get(s, ()):
            unit()
    emit(n2g, o_n2g)
    emit(blk, o_blk)
    emit(ups, o_ups)
    for chunk in chunks:
        chunk.finish()
    for k in range(2):
        passed(c, k).wait_send()
        swap_x.wait_out(k)
        swap_c.wait_out(k)
    mask_out.wait_send()
    for copy in copies:
        copy.wait()


def forward_all(w, v, x, cot, valid):
    any_space = pl.BlockSpec(memory_space=pl.ANY)
    dma = pltpu.SemaphoreType.DMA
    n = TILES + 1
    block = x.shape[1]
    nk = T * block
    nq = nk // 2
    gathered = (NP, 2, ROWS, D)

    def half(rows, cols=D):
        return (rows, cols), BF16

    outs = (
        ((4,) + gathered, BF16),
        ((16, D), F32),
        ((2, block, D), BF16),
        ((2, block, D), BF16),
        ((nk, 1), F32),
        half(nq),
        half(nk),
        half(nk),
        half(nq),
        half(D, nq),
        half(D, nq),
        half(D, nq),
        ((QUARTERS, nq, D), BF16),
        ((QUARTERS, nq, D), BF16),
        ((nq, D), F32),
        ((nq, D), F32),
        half(nq),
        ((8, D), F32),
    )
    scratch = (
        ((TILES,) + gathered, BF16),
        ((NP, 2, VROWS, 128 * T), BF16),
        ((T, block, D), BF16),
        ((2, block, D), BF16),
        ((2,) + valid.shape, F32),
        ((16, D), F32),
        ((nk, 1), F32),
        half(nk),
        half(nq),
        half(nk),
        half(nk),
        half(nq),
        ((nq, D), F32),
        half(nq),
        half(D, nq),
        half(D, nq),
        half(D, nq),
        ((QUARTERS, nq, D), BF16),
        ((QUARTERS, nq, D), BF16),
        ((nq, D), F32),
        ((nq, D), F32),
        ((nq, D), F32),
        half(nq),
        ((8, D), F32),
    )
    return pl.pallas_call(
        forward_kernel,
        out_shape=[jax.ShapeDtypeStruct(*o) for o in outs],
        in_specs=[any_space] * 5,
        out_specs=[any_space] * len(outs),
        scratch_shapes=[pltpu.VMEM(*o) for o in scratch]
        + [
            dma((4, 2)),
            dma((3,)),
            dma((2, 2)),
            dma((32,)),
            dma((n, T)),
            dma((n, 2, T)),
            dma((n,)),
            dma((n, 4)),
            dma((n, 4)),
            dma((n,)),
            dma((n,)),
        ],
        name="forward_all",
        compiler_params=pltpu.CompilerParams(
            collective_id=0, has_side_effects=True, vmem_limit_bytes=60 << 20
        ),
    )(w, v, x, cot, valid)


STAGES = (1, 3, 5, 6)
SEQUENCE = (8, 4, 9, 5, 10, 6, 11, 7, 3, 2, 1, 0)
SLOTS = 6


def backward_kernel(
    i_w, i_vec, i_x, i_cot, i_bias, i_q, i_k, i_v, i_att, i_nt, i_n2t, i_mgt, i_hid, i_pre,
    i_n2g, i_resid, blk, i_ups,
    out, vec_out, own_blk, own_ig,
    vec, x, cot, bias, q_s, k_s, v_s, att, at, hid, pre, grad, resid, wb, branch, att_g,
    dq, dk, dv, came, ig, sums,
    stage, held, far_in, near_in, line_in, vec_held, vec_in,
    load_sem, swap_sem, pair_out, pair_in, far_sem, near_sem, line_sem, vec_sem, ex_sem,
):
    spot = place()
    d, t, c, p, px, py, pd = spot
    loads = {}

    def load(name, src, dst):
        copy = pltpu.make_async_copy(src, dst, load_sem.at[len(loads)])
        copy.start()
        loads[name] = copy

    load("mgt", i_mgt, at.at[3])
    load("hid0", i_hid.at[0], hid.at[0])
    load("n2t", i_n2t, at.at[2])
    load("pre0", i_pre.at[0], pre.at[0])
    load("vec", i_vec, vec)
    load("resid", i_resid, resid)
    load("grad", i_n2g, grad)
    load("cot", i_cot, cot)
    load("wp", i_w.at[3], wb.at[0])
    load("hid1", i_hid.at[1], hid.at[1])
    load("pre1", i_pre.at[1], pre.at[1])
    load("q", i_q, q_s)
    load("k", i_k, k_s)
    load("v", i_v, v_s)
    load("bias", i_bias, bias)
    load("wk", i_w.at[1], wb.at[1])
    load("hid2", i_hid.at[2], hid.at[2])
    load("pre2", i_pre.at[2], pre.at[2])
    load("hid3", i_hid.at[3], hid.at[3])
    load("pre3", i_pre.at[3], pre.at[3])
    load("att", i_att, att)
    load("nt", i_nt, at.at[0])
    load("x", i_x, x)
    load("ups", i_ups, sums.at[pl.ds(8, 8)])

    greet(d, t, c, p, px, py)
    partner = (2 * p + 1 - c, t)
    side = ((2 * px + c, t), (2 * py + c, t))
    swap_b = Exchange(blk, own_blk, ex_sem.at[0], ex_sem.at[1], spot, False)
    swap_i = Exchange(ig, own_ig, ex_sem.at[2], ex_sem.at[3], spot, False)
    half = ROWS // 2
    nq = resid.shape[0]
    own_rows = pl.ds(pl.multiple_of(c * nq, nq), nq)
    other_rows = pl.ds(pl.multiple_of((1 - c) * nq, nq), nq)

    def slot(j):
        return j % SLOTS

    def pair(j):
        return remote(stage.at[j % 2], held.at[j], pair_out.at[j % 2], pair_in.at[j], partner)

    def far(j, way):
        return remote(
            held.at[j, pd, pl.ds(way * half, half)],
            far_in.at[slot(j), way],
            far_sem.at[0, j, way],
            far_sem.at[1, j, way],
            side[way],
        )

    def near(j, way):
        return remote(
            held.at[j, (px, py)[way]],
            near_in.at[slot(j), way],
            near_sem.at[0, j, way],
            near_sem.at[1, j, way],
            side[way],
        )

    def line(j, tau, way):
        return remote(
            held.at[j, p, :, pl.ds(tau * COLS, COLS)],
            line_in.at[j, tau + 1 - way],
            line_sem.at[0, j, tau + 1 - way],
            line_sem.at[1, j, tau + 1 - way],
            (d, t + (1 if way == 0 else -1)),
        )

    vec_partners = (
        partner,
        side[0],
        side[1],
        (d, t + 1 - 2 * lax.rem(t, 2)),
        (d, t + 2 - 4 * (t // 2)),
    )

    def vec_copy(r):
        return remote(vec_held.at[r], vec_in.at[r], vec_sem.at[0, r], vec_sem.at[1, r], vec_partners[r])

    def factors(j):
        m = SEQUENCE[j]
        if m >= 8:
            return at.at[3], hid.at[m - 8]
        if m >= 4:
            return at.at[2], pre.at[m - 4]
        if m == 3:
            return at.at[1], att
        return at.at[0], (dq, dk.at[own_rows], dv.at[own_rows])[m]

    waits = {
        0: ("mgt", "hid0"), 1: ("n2t", "pre0"), 2: ("hid1",), 3: ("pre1",), 4: ("hid2",),
        5: ("pre2",), 6: ("hid3",), 7: ("pre3",), 8: ("att",), 9: ("nt",),
    }

    def product(j, q, core):
        a, b = factors(j)
        rows = pl.ds(pl.multiple_of((2 * q + core) * ROWS, ROWS), ROWS)
        return jnp.dot(a[rows], b[...], preferred_element_type=F32)

    def each_chip(body):
        def run(q, carry):
            body(q)
            return carry

        lax.fori_loop(0, NP, run, 0)

    def first(j):
        for name in waits.get(j, ()):
            loads[name].wait()
        if j >= 2:
            pair(j - 2).wait_send()

        def make(q):
            stage[j % 2, q] = product(j, q, 1 - c).astype(BF16)

        each_chip(make)
        pair(j).start()

    def second(j):
        pair(j).wait_recv()

        def make(q):
            held[j, q] = (product(j, q, c) + held[j, q].astype(F32)).astype(BF16)

        each_chip(make)
        for way in range(2):
            far(j, way).start()

    def third(j):
        for way in range(2):
            far(j, way).wait_recv()
            part = pl.ds(way * half, half)
            q = (py, px)[way]
            held[j, q, part] = (
                held[j, q, part].astype(F32) + far_in[slot(j), way].astype(F32)
            ).astype(BF16)
            near(j, 1 - way).start()

    def fourth(j):
        near(j, 0).wait_recv()
        near(j, 1).wait_recv()
        for tau in range(T):
            cols = pl.ds(tau * COLS, COLS)
            total = (
                held[j, p, :, cols].astype(F32)
                + near_in[slot(j), 0, :, cols].astype(F32)
                + near_in[slot(j), 1, :, cols].astype(F32)
            )
            held[j, p, :, cols] = total.astype(BF16)

            @pl.when(t == tau)
            def _():
                out[j] = total

    def lines(s):
        for way in range(2):
            hop = t if way == 0 else T - 1 - t
            j = s - STAGES[3] - hop

            @pl.when(jnp.logical_and(j >= 0, j < TILES))
            def _():
                for tau in range(T):

                    @pl.when((tau > t) if way == 0 else (tau < t))
                    def _():
                        cols = pl.ds(tau * COLS, COLS)

                        @pl.when(hop > 0)
                        def _():
                            line(j, tau, way).wait_recv()
                            held[j, p, :, cols] = (
                                held[j, p, :, cols].astype(F32)
                                + line_in[j, tau + 1 - way].astype(F32)
                            ).astype(BF16)

                        line(j, tau, way).start()

    def last(j):
        for way in range(2):

            @pl.when((t > 0) if way == 0 else (t < T - 1))
            def _():
                for tau in range(T):

                    @pl.when(t == tau)
                    def _():
                        line(j, tau, way).wait_recv()
                        out[j] += line_in[j, tau + 1 - way].astype(F32)

    def comm(s):
        for lag, work in ((0, first), (STAGES[0], second), (STAGES[1], third), (STAGES[2], fourth)):
            if 0 <= s - lag < TILES:
                work(s - lag)
        if STAGES[3] <= s < TILES + STAGES[3] + T - 1:
            lines(s)
        if 0 <= s - STAGES[3] - T < TILES:
            last(s - STAGES[3] - T)

    def add(row, a):
        sums[row : row + 1] += jnp.sum(a, axis=0, keepdims=True)

    def mid_back():
        for name in ("vec", "resid", "grad", "cot", "ups"):
            loads[name].wait()
        sums[0:8] = jnp.zeros((8, D), F32)

        def run(rows, i):
            unit, inverse = norm_parts(resid[rows])
            g = grad[rows]
            outer = cot[rows].astype(F32)
            total = outer + norm_back(g, unit, inverse, vec[3:4])
            resid[rows] = total
            low = total.astype(BF16)
            branch[rows] = low
            add(2, low.astype(F32))
            add(3, g * unit)
            add(4, g)
            add(5, outer)

        tiles(nq, 64, run)

    def att_back():
        loads["wp"].wait()
        a = branch[...]

        def run(cols, i):
            at[1, cols] = to_lanes(branch[:, cols])
            att_g[:, cols] = jnp.dot(a, matrix(wb, 0, cols), preferred_element_type=F32).astype(BF16)

        tiles(D, TILE, run)
        load("wq", i_w.at[0], wb.at[0])

    def heads(first_pair, last_pair):
        if first_pair == 0:
            for name in ("q", "k", "v", "bias"):
                loads[name].wait()

        def run(i, carry):
            cols = pl.ds(pl.multiple_of(i * 2 * HD, 2 * HD), 2 * HD)
            k, v, g = k_s[:, cols], v_s[:, cols], att_g[:, cols]
            q_f = q_s[:, cols].astype(F32) * HD ** (-0.5)
            q_l = q_f.astype(BF16)
            q_t = q_f.T.astype(BF16)
            g_t = to_lanes(g)
            k_t = to_lanes(k)
            parts, dk_parts, dv_parts = [], [], []
            for h in range(2):
                probs = head_probs(k, head_rows(q_t, h), bias[...])
                dv_parts.append(
                    jnp.dot(probs.astype(BF16), head_lanes(g, h), preferred_element_type=F32)
                )
                dp = jnp.dot(v, head_rows(g_t, h), preferred_element_type=F32)
                ds = (probs * (dp - jnp.sum(dp * probs, axis=0, keepdims=True))).astype(BF16)
                parts.append(jnp.dot(k_t[h * HD : (h + 1) * HD], ds, preferred_element_type=F32))
                dk_parts.append(jnp.dot(ds, head_lanes(q_l, h), preferred_element_type=F32))
            dq[:, cols] = (jnp.concatenate(parts, axis=0).T * HD ** (-0.5)).astype(BF16)
            dk[:, cols] = (dk_parts[0] + dk_parts[1]).astype(BF16)
            dv[:, cols] = (dv_parts[0] + dv_parts[1]).astype(BF16)
            return carry

        lax.fori_loop(first_pair, last_pair, run, 0)

    def pass_on(i):
        src = (dk, dv)[i].at[other_rows]
        return remote(src, came.at[i], swap_sem.at[0, i], swap_sem.at[1, i], partner)

    def query_back():
        pass_on(0).start()
        pass_on(1).start()
        loads["wq"].wait()
        a = dq[...]

        def run(cols, i):
            grad[:, cols] = dot_nt(a, matrix_rows(wb, 0, i))
            sums[6:7, cols] = jnp.sum(dq[:, cols].astype(F32), axis=0, keepdims=True)

        tiles(D, TILE, run)
        load("wv", i_w.at[2], wb.at[0])

    def key_back():
        for i, ref in enumerate((dk, dv)):
            pass_on(i).wait_recv()

            def join(cols, n):
                total = (ref[own_rows, cols].astype(F32) + came[i, :, cols].astype(F32)).astype(BF16)
                ref[own_rows, cols] = total
                if i == 1:
                    sums[7:8, cols] = jnp.sum(total.astype(F32), axis=0, keepdims=True)

            tiles(D, TILE, join)
        loads["wk"].wait()
        loads["wv"].wait()
        a, b = dk[own_rows], dv[own_rows]

        def run(cols, i):
            grad[:, cols] += dot_nt(a, matrix_rows(wb, 1, i)) + dot_nt(b, matrix_rows(wb, 0, i))

        tiles(D, TILE, run)

    def front_back():
        loads["x"].wait()
        size = 32
        per = ig.shape[1] // size

        def run(rows, i):
            unit, inverse = norm_parts(x[rows].astype(F32))
            g = grad[rows]
            add(0, g * unit)
            add(1, g)
            total = resid[rows] + norm_back(g, unit, inverse, vec[0:1])
            ig[i // per, pl.ds(pl.multiple_of(lax.rem(i, per) * size, size), size)] = total.astype(BF16)

        tiles(nq, size, run)
        swap_i.start()
        vec_held[0] = sums[...]
        vec_copy(0).start()

    def vec_round(r):
        vec_copy(r).wait_recv()
        vec_held[r + 1] = vec_held[r] + vec_in[r]
        if r < 4:
            vec_copy(r + 1).start()
        else:
            vec_out[...] = vec_held[5]

    after = {
        0: (mid_back,),
        1: (att_back,),
        2: (lambda: heads(0, 2),),
        3: (lambda: heads(2, 3),),
        4: (lambda: heads(3, 5),),
        5: (lambda: heads(5, 6),),
        6: (lambda: heads(6, 8), query_back),
        7: (key_back,),
        8: (front_back,),
        10: (lambda: vec_round(0),),
        11: (lambda: vec_round(1),),
        12: (lambda: vec_round(2),),
        13: (lambda: vec_round(3),),
        14: (lambda: vec_round(4),),
    }
    swap_b.start()
    for s in range(TILES + STAGES[3] + T):
        comm(s)
        for unit in after.get(s, ()):
            unit()
    for j in range(TILES):
        for way in range(2):
            far(j, way).wait_send()
            near(j, way).wait_send()
            for tau in range(T):

                @pl.when((tau > t) if way == 0 else (tau < t))
                def _():
                    line(j, tau, way).wait_send()

    pair(TILES - 2).wait_send()
    pair(TILES - 1).wait_send()
    for i in range(2):
        pass_on(i).wait_send()
    for r in range(5):
        vec_copy(r).wait_send()
    for swap in (swap_b, swap_i):
        for k in range(2):
            swap.wait_in(k)
            swap.wait_out(k)


def backward_all(*args):
    any_space = pl.BlockSpec(memory_space=pl.ANY)
    vmem = pl.BlockSpec(memory_space=pltpu.VMEM)
    dma = pltpu.SemaphoreType.DMA
    n = TILES
    blk, resid, bias = args[16], args[15], args[4]
    nq, nk = resid.shape[0], bias.shape[0]
    own = (nq, D)
    scratch = (
        ((16, D), F32),
        (own, BF16),
        (own, BF16),
        ((nk, 1), F32),
        (own, BF16),
        ((nk, D), BF16),
        ((nk, D), BF16),
        (own, BF16),
        ((4, D, nq), BF16),
        ((QUARTERS,) + own, BF16),
        ((QUARTERS,) + own, BF16),
        (own, F32),
        (own, F32),
        ((2, NP, 2, ROWS, D), BF16),
        (own, BF16),
        (own, BF16),
        (own, BF16),
        ((nk, D), BF16),
        ((nk, D), BF16),
        ((2,) + own, BF16),
        (blk.shape, BF16),
        ((16, D), F32),
        ((2, NP, ROWS, D), BF16),
        ((n, NP, ROWS, D), BF16),
        ((SLOTS, 2, ROWS // 2, D), BF16),
        ((SLOTS, 2, ROWS, D), BF16),
        ((n, T + 1, ROWS, COLS), BF16),
        ((6, 16, D), F32),
        ((5, 16, D), F32),
    )
    return pl.pallas_call(
        backward_kernel,
        out_shape=(
            jax.ShapeDtypeStruct((n, ROWS, COLS), F32),
            jax.ShapeDtypeStruct((16, D), F32),
            jax.ShapeDtypeStruct(blk.shape, BF16),
            jax.ShapeDtypeStruct(blk.shape, BF16),
        ),
        in_specs=[any_space] * len(args),
        out_specs=[vmem, vmem, any_space, any_space],
        scratch_shapes=[pltpu.VMEM(*o) for o in scratch]
        + [
            dma((32,)),
            dma((2, 2)),
            dma((2,)),
            dma((n,)),
            dma((2, n, 2)),
            dma((2, n, 2)),
            dma((2, n, T + 1)),
            dma((2, 5)),
            dma((4, 2)),
        ],
        name="backward_all",
        compiler_params=pltpu.CompilerParams(
            collective_id=1, has_side_effects=True, vmem_limit_bytes=60 << 20
        ),
    )(*args)


def head_probs(k, q_t, bias):
    s = jnp.dot(k, q_t, preferred_element_type=F32) + bias
    e = jnp.exp(s - jnp.max(s, axis=0, keepdims=True))
    return e / jnp.sum(e, axis=0, keepdims=True)


def head_rows(q_t, h):
    row = lax.broadcasted_iota(jnp.int32, q_t.shape, 0) // HD
    return jnp.where(row == h, q_t, jnp.zeros_like(q_t))


def head_lanes(q, h):
    lane = lax.broadcasted_iota(jnp.int32, q.shape, 1) // HD
    return jnp.where(lane == h, q, jnp.zeros_like(q))


def norm_parts(values):
    center = values - jnp.mean(values, axis=-1, keepdims=True)
    spread = jnp.mean(center * center, axis=-1, keepdims=True)
    inverse = lax.rsqrt(spread + EPS)
    return center * inverse, inverse


def norm_back(grad, unit, inverse, gain):
    scaled = grad * gain
    return inverse * (
        scaled
        - jnp.mean(scaled, axis=-1, keepdims=True)
        - unit * jnp.mean(scaled * unit, axis=-1, keepdims=True)
    )


def dot_nn(a, b):
    return lax.dot_general(a, b, (((1,), (0,)), ((), ())), preferred_element_type=F32)


def dot_nt(a, b):
    return lax.dot_general(a, b, (((1,), (1,)), ((), ())), preferred_element_type=F32)


def per_device_chips(
    activations, cotangent, token_valid, image_counts, pre_gain, pre_shift, attn_weight,
    attn_bias, proj_weight, proj_bias, mid_gain, mid_shift, up_weight, up_bias, down_weight,
    down_bias,
):
    local_rows = activations.shape[0]
    slots = activations.shape[1]
    block = -(-local_rows // 16) * 16
    pad = block - local_rows
    d = lax.axis_index("dp")
    t = lax.axis_index("tensor")
    c = lax.rem(d, 2)
    first_row = t * local_rows
    my_valid = lax.dynamic_slice_in_dim(token_valid, first_row, local_rows, 1).astype(F32)
    slot_live = (jnp.arange(slots, dtype=jnp.int32) < image_counts[0]).astype(F32)
    out_mask = jnp.transpose(slot_live[:, None] * my_valid)[:, :, None]

    def to_blocks(a):
        return jnp.pad(jnp.transpose(a, (1, 0, 2)), ((0, 0), (0, pad), (0, 0)))

    x_blocks = to_blocks(activations)
    c_blocks = to_blocks((cotangent.astype(F32) * out_mask).astype(BF16))
    valid = jnp.pad(
        token_valid.astype(F32).reshape(slots, T, local_rows), ((0, 0), (0, 0), (0, pad))
    ).reshape(slots, T * block)
    valid = jnp.pad(valid, ((0, 8 - slots), (0, 0)))
    per_j = up_weight.shape[1] // COLS
    w = jnp.concatenate(
        [
            attn_weight,
            jnp.transpose(proj_weight)[None],
            jnp.transpose(up_weight.reshape(ROWS, per_j, COLS), (1, 0, 2)),
            jnp.transpose(down_weight.reshape(per_j, COLS, ROWS), (0, 2, 1)),
        ],
        axis=0,
    )
    v = jnp.concatenate(
        [
            jnp.stack([pre_gain, pre_shift, proj_bias, mid_gain, mid_shift, down_bias]),
            attn_bias.reshape(-1, 128),
            up_bias.reshape(-1, 128),
        ],
        axis=0,
    )
    v = jnp.pad(v, ((0, VROWS - v.shape[0]), (0, 0)))
    (
        full_w, vec, x_own, own_cot, bias, queries, keys, values, attended, normed_t, normed2_t,
        mlp_grad_t, hidden, pre_grad, normed2_grad, resid, block_own, up_sums,
    ) = forward_all(w, v, x_blocks, c_blocks, valid)
    own = resid.shape
    grads, totals, own_block, own_input = backward_all(
        full_w, vec, x_own.reshape(own), own_cot.reshape(own), bias, queries, keys, values,
        attended, normed_t, normed2_t, mlp_grad_t, hidden, pre_grad, normed2_grad, resid,
        block_own.reshape(own_cot.shape), up_sums,
    )
    owned = lax.dynamic_slice(totals, (0, d * ROWS), (6, ROWS))
    parted = lax.dynamic_slice(totals, (0, t * COLS), (totals.shape[0], COLS))

    def from_blocks(a):
        return jnp.transpose(a[:, :local_rows], (1, 0, 2))

    block_out = (from_blocks(own_block).astype(F32) * out_mask).astype(BF16)
    input_grad = from_blocks(own_input).astype(F32)
    at = {m: i for i, m in enumerate(SEQUENCE)}
    quarters = range(QUARTERS)
    return (
        block_out,
        input_grad,
        owned[0],
        owned[1],
        jnp.stack([grads[at[m]] for m in range(3)]),
        parted[6:8],
        jnp.transpose(grads[at[3]]),
        owned[2],
        owned[3],
        owned[4],
        jnp.concatenate([grads[at[4 + j]] for j in quarters], axis=1),
        parted[8 : 8 + QUARTERS].reshape(-1),
        jnp.concatenate([jnp.transpose(grads[at[8 + j]]) for j in quarters], axis=0),
        owned[5],
    )


def solution(mesh):
    sizes = (mesh.shape["dp"], mesh.shape["tensor"])
    per_device = per_device_chips if sizes == (2 * NP, T) else per_device_general
    return jax.shard_map(
        per_device,
        mesh=mesh,
        in_specs=(
            P("tensor", "dp", None),
            P("tensor", "dp", None),
            P("dp", None),
            P("dp"),
            P("dp"),
            P("dp"),
            P(None, "dp", "tensor"),
            P(None, "tensor"),
            P("tensor", "dp"),
            P("dp"),
            P("dp"),
            P("dp"),
            P("dp", "tensor"),
            P("tensor"),
            P("tensor", "dp"),
            P("dp"),
        ),
        out_specs=(
            P("tensor", "dp", None),
            P("tensor", "dp", None),
            P("dp"),
            P("dp"),
            P(None, "dp", "tensor"),
            P(None, "tensor"),
            P("tensor", "dp"),
            P("dp"),
            P("dp"),
            P("dp"),
            P("dp", "tensor"),
            P("tensor"),
            P("tensor", "dp"),
            P("dp"),
        ),
        check_vma=False,
    )
```

```python
import functools

import jax
import jax.numpy as jnp
from jax import lax
from jax.experimental import pallas as pl
from jax.experimental.pallas import tpu as pltpu
from jax.sharding import PartitionSpec as P

D = 1024
H = 16
HD = 64
MB = 2


EPS = 1e-06
NEG = -1000000000.0


def layer_norm(values, gain, shift):
    center = values - jnp.mean(values, axis=-1, keepdims=True)
    spread = jnp.mean(center * center, axis=-1, keepdims=True)
    return center * lax.rsqrt(spread + EPS) * gain + shift


def gelu_exact(values):
    return jax.nn.gelu(values, approximate=False)


def per_device_general(
    activations,
    cotangent,
    token_valid,
    image_counts,
    pre_gain,
    pre_shift,
    attn_weight,
    attn_bias,
    proj_weight,
    proj_bias,
    mid_gain,
    mid_shift,
    up_weight,
    up_bias,
    down_weight,
    down_bias,
):
    f32 = jnp.float32
    bf16 = jnp.bfloat16
    tensor_size = lax.axis_size("tensor")
    local_rows = activations.shape[0]
    slots = activations.shape[1]
    per_micro = slots // MB
    heads_here = H // tensor_size
    width_here = attn_weight.shape[2]
    hidden_here = up_weight.shape[1]
    scale = HD ** (-0.5)
    first_row = lax.axis_index("tensor") * local_rows
    my_valid = lax.dynamic_slice_in_dim(token_valid, first_row, local_rows, 1).astype(f32)
    slot_live = (jnp.arange(slots, dtype=jnp.int32) < image_counts[0]).astype(f32)
    attn_bias_f = attn_bias.astype(f32)
    up_bias_f = up_bias.astype(f32)
    acc_attn = jnp.zeros((3, D, width_here), f32)
    acc_proj = jnp.zeros((width_here, D), f32)
    acc_up = jnp.zeros((D, hidden_here), f32)
    acc_down = jnp.zeros((hidden_here, D), f32)
    acc_attn_bias = jnp.zeros((2, width_here), f32)
    acc_up_bias = jnp.zeros((hidden_here,), f32)
    acc_vectors = [jnp.zeros((D,), f32) for unused in range(6)]
    block_parts = []
    input_parts = []
    for micro_step in range(MB):
        gathered = (
            lax.all_gather(attn_weight, "dp", axis=1, tiled=True),
            lax.all_gather(proj_weight, "dp", axis=1, tiled=True),
            lax.all_gather(up_weight, "dp", axis=0, tiled=True),
            lax.all_gather(down_weight, "dp", axis=1, tiled=True),
            lax.all_gather(pre_gain, "dp", axis=0, tiled=True),
            lax.all_gather(pre_shift, "dp", axis=0, tiled=True),
            lax.all_gather(proj_bias, "dp", axis=0, tiled=True),
            lax.all_gather(mid_gain, "dp", axis=0, tiled=True),
            lax.all_gather(mid_shift, "dp", axis=0, tiled=True),
            lax.all_gather(down_bias, "dp", axis=0, tiled=True),
        )
        qkv_full, proj_full, upw_full, downw_full = (
            gathered[0],
            gathered[1],
            gathered[2],
            gathered[3],
        )
        gain_one, shift_one, proj_bias_f, gain_two, shift_two, down_bias_f = [
            item.astype(f32) for item in gathered[4:]
        ]
        offset = micro_step * per_micro
        inputs_f = activations[:, offset : offset + per_micro].astype(f32)
        key_valid = token_valid[offset : offset + per_micro]
        key_bias = jnp.where(key_valid > 0, 0.0, NEG).astype(f32)
        out_mask = jnp.transpose(
            slot_live[offset : offset + per_micro][:, None] * my_valid[offset : offset + per_micro]
        )[:, :, None]
        normed = layer_norm(inputs_f, gain_one, shift_one).astype(bf16)
        normed_all = lax.all_gather(normed, "tensor", axis=0, tiled=True)
        full_rows = normed_all.shape[0]
        projected = jnp.einsum("sid,cde->csie", normed_all, qkv_full, preferred_element_type=f32)
        queries = (
            (projected[0] + attn_bias_f[0])
            .astype(bf16)
            .reshape(full_rows, per_micro, heads_here, HD)
        )
        keys = projected[1].astype(bf16).reshape(full_rows, per_micro, heads_here, HD)
        values = (
            (projected[2] + attn_bias_f[1])
            .astype(bf16)
            .reshape(full_rows, per_micro, heads_here, HD)
        )

        def scores_of(query_part, key_part):
            raw = jnp.einsum("qihe,kihe->ihqk", query_part, key_part, preferred_element_type=f32)
            return raw * scale + key_bias[:, None, None, :]

        scores = scores_of(queries, keys)
        top = jnp.max(scores, axis=-1, keepdims=True)
        expo = jnp.exp(scores - top)
        total = jnp.sum(expo, axis=-1, keepdims=True)
        logsum = top + jnp.log(total)
        probs_low = (expo / total).astype(bf16)
        attended = (
            jnp.einsum("ihqk,kihe->qihe", probs_low, values, preferred_element_type=f32)
            .astype(bf16)
            .reshape(full_rows, per_micro, width_here)
        )
        resid = (
            inputs_f
            + lax.psum_scatter(
                jnp.einsum("sie,ed->sid", attended, proj_full, preferred_element_type=f32),
                "tensor",
                scatter_dimension=0,
                tiled=True,
            )
            + proj_bias_f
        )
        normed2 = layer_norm(resid, gain_two, shift_two).astype(bf16)
        normed2_all = lax.all_gather(normed2, "tensor", axis=0, tiled=True)
        hidden_pre = (
            jnp.einsum("sid,df->sif", normed2_all, upw_full, preferred_element_type=f32) + up_bias_f
        )
        hidden = gelu_exact(hidden_pre).astype(bf16)
        mlp_out = (
            lax.psum_scatter(
                jnp.einsum("sif,fd->sid", hidden, downw_full, preferred_element_type=f32).astype(
                    jnp.bfloat16
                ),
                "tensor",
                scatter_dimension=0,
                tiled=True,
            ).astype(jnp.float32)
            + down_bias_f
        )
        block_parts.append(((resid + mlp_out) * out_mask).astype(bf16))
        outer = cotangent[:, offset : offset + per_micro].astype(f32) * out_mask
        mlp_grad = outer.astype(bf16)
        acc_vectors[5] = acc_vectors[5] + jnp.sum(mlp_grad.astype(f32), axis=(0, 1))
        mlp_grad_all = lax.all_gather(mlp_grad, "tensor", axis=0, tiled=True)
        acc_down = acc_down + jnp.einsum(
            "sif,sid->fd", hidden, mlp_grad_all, preferred_element_type=f32
        )
        hidden_grad = jnp.einsum(
            "sid,fd->sif", mlp_grad_all, downw_full, preferred_element_type=f32
        )
        unused, gelu_back = jax.vjp(gelu_exact, hidden_pre)
        pre_grad = gelu_back(hidden_grad)[0].astype(bf16)
        acc_up_bias = acc_up_bias + jnp.sum(pre_grad.astype(f32), axis=(0, 1))
        acc_up = acc_up + jnp.einsum(
            "sid,sif->df", normed2_all, pre_grad, preferred_element_type=f32
        )
        normed2_grad = lax.psum_scatter(
            jnp.einsum("sif,df->sid", pre_grad, upw_full, preferred_element_type=f32),
            "tensor",
            scatter_dimension=0,
            tiled=True,
        )
        unused, second_back = jax.vjp(layer_norm, resid, gain_two, shift_two)
        resid_part, gain_two_grad, shift_two_grad = second_back(normed2_grad)
        acc_vectors[3] = acc_vectors[3] + gain_two_grad
        acc_vectors[4] = acc_vectors[4] + shift_two_grad
        resid_grad = outer + resid_part
        branch_grad = resid_grad.astype(bf16)
        acc_vectors[2] = acc_vectors[2] + jnp.sum(branch_grad.astype(f32), axis=(0, 1))
        branch_all = lax.all_gather(branch_grad, "tensor", axis=0, tiled=True)
        acc_proj = acc_proj + jnp.einsum(
            "sie,sid->ed", attended, branch_all, preferred_element_type=f32
        )
        att_grad = (
            jnp.einsum("sid,ed->sie", branch_all, proj_full, preferred_element_type=f32)
            .astype(bf16)
            .reshape(full_rows, per_micro, heads_here, HD)
        )
        probs = jnp.exp(scores_of(queries, keys) - logsum)
        probs_again = probs.astype(bf16)
        value_grad = jnp.einsum(
            "ihqk,qihe->kihe", probs_again, att_grad, preferred_element_type=f32
        ).astype(bf16)
        prob_grad = jnp.einsum("qihe,kihe->ihqk", att_grad, values, preferred_element_type=f32)
        score_grad = (
            probs * (prob_grad - jnp.sum(prob_grad * probs, axis=-1, keepdims=True))
        ).astype(bf16)
        query_grad = (
            jnp.einsum("ihqk,kihe->qihe", score_grad, keys, preferred_element_type=f32) * scale
        ).astype(bf16)
        key_grad = (
            jnp.einsum("ihqk,qihe->kihe", score_grad, queries, preferred_element_type=f32) * scale
        ).astype(bf16)
        qkv_grad = jnp.stack([query_grad, key_grad, value_grad]).reshape(
            3, full_rows, per_micro, width_here
        )
        acc_attn_bias = acc_attn_bias + jnp.stack(
            [
                jnp.sum(qkv_grad[0].astype(f32), axis=(0, 1)),
                jnp.sum(qkv_grad[2].astype(f32), axis=(0, 1)),
            ]
        )
        acc_attn = acc_attn + jnp.einsum(
            "sid,csie->cde", normed_all, qkv_grad, preferred_element_type=f32
        )
        normed_grad = lax.psum_scatter(
            jnp.einsum("csie,cde->sid", qkv_grad, qkv_full, preferred_element_type=f32),
            "tensor",
            scatter_dimension=0,
            tiled=True,
        )
        unused, first_back = jax.vjp(layer_norm, inputs_f, gain_one, shift_one)
        input_part, gain_one_grad, shift_one_grad = first_back(normed_grad)
        acc_vectors[0] = acc_vectors[0] + gain_one_grad
        acc_vectors[1] = acc_vectors[1] + shift_one_grad
        input_parts.append(resid_grad + input_part)
    summed = lax.psum(
        (
            acc_vectors[0],
            acc_vectors[1],
            acc_vectors[2],
            acc_vectors[3],
            acc_vectors[4],
            acc_vectors[5],
        ),
        "tensor",
    )
    owned = (
        lax.psum_scatter(acc_attn, "dp", scatter_dimension=1, tiled=True),
        lax.psum_scatter(acc_proj, "dp", scatter_dimension=1, tiled=True),
        lax.psum_scatter(acc_up, "dp", scatter_dimension=0, tiled=True),
        lax.psum_scatter(acc_down, "dp", scatter_dimension=1, tiled=True),
        lax.psum_scatter(summed[0], "dp", scatter_dimension=0, tiled=True),
        lax.psum_scatter(summed[1], "dp", scatter_dimension=0, tiled=True),
        lax.psum_scatter(summed[2], "dp", scatter_dimension=0, tiled=True),
        lax.psum_scatter(summed[3], "dp", scatter_dimension=0, tiled=True),
        lax.psum_scatter(summed[4], "dp", scatter_dimension=0, tiled=True),
        lax.psum_scatter(summed[5], "dp", scatter_dimension=0, tiled=True),
    )
    bias_sums = lax.psum((acc_attn_bias, acc_up_bias), "dp")
    block_out = jnp.concatenate(block_parts, axis=1)
    input_grad = jnp.concatenate(input_parts, axis=1)
    return (
        block_out,
        input_grad,
        owned[4],
        owned[5],
        owned[0],
        bias_sums[0],
        owned[1],
        owned[6],
        owned[7],
        owned[8],
        owned[2],
        bias_sums[1],
        owned[3],
        owned[9],
    )

MESH = pl.DeviceIdType.MESH
F32 = jnp.float32
BF16 = jnp.bfloat16
TILES = 12
T = 4
NP = 4
ROWS = D // (2 * NP)
COLS = D // T
VROWS = 32


def place():
    d = lax.axis_index("dp")
    t = lax.axis_index("tensor")
    c = lax.rem(d, 2)
    p = d // 2
    px = p + 1 - 2 * lax.rem(p, 2)
    py = p + 2 - 4 * (p // 2)
    return d, t, c, p, px, py, 3 - p


def greet(d, t, c, p, px, py):
    barrier = pltpu.get_barrier_semaphore()
    me = c * T + t
    for step in range(1, 2 * T):
        other = lax.rem(me + step, 2 * T)
        pl.semaphore_signal(
            barrier, inc=1, device_id=(2 * p + other // T, lax.rem(other, T)), device_id_type=MESH
        )
    for q in (px, py):
        pl.semaphore_signal(barrier, inc=1, device_id=(2 * q + c, t), device_id_type=MESH)
    pl.semaphore_wait(barrier, 2 * T + 1)


def remote(src, dst, send, recv, device):
    return pltpu.make_async_remote_copy(
        src_ref=src,
        dst_ref=dst,
        send_sem=send,
        recv_sem=recv,
        device_id=device,
        device_id_type=MESH,
    )


class Exchange:
    def __init__(self, src, dst, send, recv, spot, full):
        d, t, c, p, px, py, pd = spot
        self.c, self.t, self.p = c, t, p
        self.src, self.dst, self.send, self.recv = src, dst, send, recv
        self.full = full

    def slot_out(self):
        return self.t if self.full else lax.rem(self.t, 2)

    def slot_in(self, k):
        return 2 * self.c + k if self.full else k

    def mine(self, k):
        return jnp.logical_and(self.t // 2 == self.c, lax.rem(self.t, 2) == k)

    def copy(self, k):
        return remote(
            self.src.at[k],
            self.dst.at[self.slot_out()],
            self.send.at[k],
            self.recv.at[lax.rem(self.t, 2)],
            (2 * self.p + self.t // 2, 2 * self.c + k),
        )

    def local(self, k):
        return pltpu.make_async_copy(
            self.src.at[k], self.dst.at[self.slot_out()], self.send.at[k]
        )

    def start(self):
        for k in range(2):

            @pl.when(self.mine(k))
            def _():
                self.local(k).start()

            @pl.when(jnp.logical_not(self.mine(k)))
            def _():
                self.copy(k).start()

    def wait_in(self, k):
        @pl.when(self.mine(k))
        def _():
            self.local(k).wait()

        @pl.when(jnp.logical_not(self.mine(k)))
        def _():
            remote(
                self.src.at[k],
                self.dst.at[self.slot_in(k)],
                self.send.at[k],
                self.recv.at[k],
                (2 * self.p + self.t // 2, 2 * self.c + k),
            ).wait_recv()

    def wait_out(self, k):
        @pl.when(jnp.logical_not(self.mine(k)))
        def _():
            self.copy(k).wait_send()


OWN = (0,)
REST = (1, 2)


class Gather:
    kinds = OWN + REST

    def __init__(self, src, dst, sems, j, spot):
        self.d, self.t, self.c, self.p, self.px, self.py, self.pd = spot
        self.src, self.dst, self.j = src, dst, j
        self.zin, self.zout, self.own_sem, self.rin, self.rout, self.cin, self.cout = sems
        self.half = src.shape[0] // 2
        self.width = src.shape[1]

    def row(self, q):
        return self.dst.at[q, self.c]

    def cell(self, tau):
        start = pl.multiple_of(tau * self.width, self.width)
        return self.dst.at[self.p, self.c, :, pl.ds(start, self.width)]

    def local(self):
        return pltpu.make_async_copy(self.src, self.cell(self.t), self.own_sem.at[self.j])

    def line(self, tau, way, k):
        src = self.src if k == 0 else self.cell(tau)
        return remote(
            src,
            self.cell(tau),
            self.zout.at[self.j, way, k],
            self.zin.at[self.j, tau],
            (self.d, self.t + (1 if way == 0 else -1)),
        )

    def own(self):
        self.local().start()

        @pl.when(self.t < T - 1)
        def _():
            self.line(self.t, 0, 0).start()

        @pl.when(self.t > 0)
        def _():
            self.line(self.t, 1, 0).start()

    def near_own(self):
        self.spread(OWN, self.near)

    def hop(self, k):
        t = self.t

        @pl.when(t >= k)
        def _():
            self.line(t - k, 0, k).wait_recv()

            @pl.when(t < T - 1)
            def _():
                self.line(t - k, 0, k).start()

        @pl.when(t + k < T)
        def _():
            self.line(t + k, 1, k).wait_recv()

            @pl.when(t > 0)
            def _():
                self.line(t + k, 1, k).start()

    def side(self, way):
        q = self.px if way == 0 else self.py
        return (2 * q + self.c, self.t)

    def spread(self, kinds, make, act="start"):
        for place_z in range(T):

            @pl.when(self.t == place_z)
            def _():
                for kind in kinds:
                    first, last = ((place_z, place_z + 1), (0, place_z), (place_z + 1, T))[kind]
                    if first < last:
                        for way in range(2):
                            getattr(make(way, kind, first, last), act)()

    def piece(self, q, first, last):
        return self.dst.at[q, self.c, :, pl.ds(first * self.width, (last - first) * self.width)]

    def near(self, way, kind, first, last):
        part = self.piece(self.p, first, last)
        return remote(
            self.src if kind == 0 else part,
            part,
            self.rout.at[self.j, 2 * kind + way],
            self.rin.at[self.j, 2 * kind + way],
            self.side(way),
        )

    def near_in(self, way, kind, first, last):
        part = self.piece(self.px if way == 0 else self.py, first, last)
        sem = self.rin.at[self.j, 2 * kind + way]
        return remote(part, part, self.rout.at[self.j, 2 * kind + way], sem, self.side(way))

    def passed(self, q, way, kind, first, last):
        part = self.piece(q, first, last).at[pl.ds(way * self.half, self.half)]
        at = 6 + 2 * kind + way
        return remote(
            part, part, self.rout.at[self.j, at], self.rin.at[self.j, at], self.side(1 - way)
        )

    def far(self, way, kind, first, last):
        return self.passed(self.px if way == 0 else self.py, way, kind, first, last)

    def far_in(self, way, kind, first, last):
        return self.passed(self.pd, way, kind, first, last)

    def near_rest(self):
        self.spread(REST, self.near)

    def far_own(self):
        self.spread(OWN, self.near_in, "wait_recv")
        self.spread(OWN, self.far)

    def far_rest(self):
        self.spread(REST, self.near_in, "wait_recv")
        self.spread(REST, self.far)

    def pair(self, c):
        return remote(
            self.dst.at[:, c],
            self.dst.at[:, c],
            self.cout.at[self.j],
            self.cin.at[self.j],
            (2 * self.p + 1 - self.c, self.t),
        )

    def cross(self):
        self.local().wait()
        self.spread(OWN + REST, self.far_in, "wait_recv")
        self.pair(self.c).start()

    def ready(self):
        self.pair(1 - self.c).wait_recv()

    def finish(self):
        t = self.t
        for k in range(T):

            @pl.when(jnp.logical_and(t >= k, t < T - 1))
            def _():
                self.line(t - k, 0, k).wait_send()

            @pl.when(jnp.logical_and(t + k < T, t > 0))
            def _():
                self.line(t + k, 1, k).wait_send()

        self.spread(self.kinds, self.near, "wait_send")
        self.spread(self.kinds, self.far, "wait_send")
        self.pair(self.c).wait_send()


class GatherFlip(Gather):
    kinds = OWN

    def column(self, tau):
        start = pl.multiple_of(tau * self.width, self.width)
        return self.dst.at[:, self.c, :, pl.ds(start, self.width)]

    def line(self, tau, way, k):
        part = self.column(tau)
        return remote(
            part,
            part,
            self.zout.at[self.j, way, k],
            self.zin.at[self.j, tau],
            (self.d, self.t + (1 if way == 0 else -1)),
        )

    def own(self):
        self.local().start()
        self.spread(OWN, self.near)

    def line_own(self):
        self.local().wait()
        self.spread(OWN, self.far_in, "wait_recv")

        @pl.when(self.t < T - 1)
        def _():
            self.line(self.t, 0, 0).start()

        @pl.when(self.t > 0)
        def _():
            self.line(self.t, 1, 0).start()

    def cross(self):
        self.pair(self.c).start()


LAGS = (1, 2, 3, -3, 5, 7)
LEAD = 5
ORDER = (0, 1, 2, 3, 4, 8, 5, 9, 6, 10, 11)
FLIPPED = 7
FLIP_STEPS = (0, 1, 9, 11, 13, 15, 16)
SWAP_STEPS = (3, 8, 12)
QUARTERS = 4
TILE = 256


def tiles(n, size, body):
    def run(i, carry):
        body(pl.ds(pl.multiple_of(i * size, size), size), i)
        return carry

    lax.fori_loop(0, n // size, run, 0)


def to_lanes(a):
    return a.astype(F32).T.astype(BF16)


def matrix(w, j, cols=None):
    a = w[j] if cols is None else w[j, :, :, :, cols]
    return a.reshape(D, a.shape[-1])


def matrix_rows(w, j, n):
    return w[j, n].reshape(2 * ROWS, D)


def forward_kernel(
    w, v, x, cot, valid,
    o_w, o_vec, o_x, o_cot, o_bias, o_q, o_k, o_v, o_att, o_nt, o_n2t, o_mgt, o_hid, o_pre,
    o_n2g, o_resid, o_blk, o_ups,
    gw, gv, xf, cf, mf, vec, bias, normed, q_s, k_s, v_s, att, resid, n2, nt, n2t, mgt, hid, pre,
    n2g, mlp, slope, blk, ups,
    ex_sem, mask_sem, pass_sem, out_sem, *chunk_sems,
):
    spot = place()
    d, t, c, p, px, py, pd = spot
    greet(d, t, c, p, px, py)
    partner = (2 * p + 1 - c, t)
    swap_x = Exchange(x, xf, ex_sem.at[0], ex_sem.at[1], spot, True)
    swap_c = Exchange(cot, cf, ex_sem.at[2], ex_sem.at[3], spot, False)
    mask_out = remote(valid, mf.at[c], mask_sem.at[0], mask_sem.at[1], partner)
    mask_in = remote(valid, mf.at[1 - c], mask_sem.at[0], mask_sem.at[1], partner)
    mask_own = pltpu.make_async_copy(valid, mf.at[c], mask_sem.at[2])

    def passed(core, k):
        view = xf.at[2 * core + k]
        return remote(view, view, pass_sem.at[0, k], pass_sem.at[1, k], partner)

    chunks = [Gather(v, gv, chunk_sems, 0, spot)]
    for i, j in enumerate(ORDER):
        chunks.append(Gather(w.at[j], gw.at[j], chunk_sems, i + 1, spot))
    count = len(chunks)
    flipped = GatherFlip(w.at[FLIPPED], gw.at[FLIPPED], chunk_sems, count, spot)
    flip_work = (
        flipped.own,
        flipped.far_own,
        flipped.line_own,
        lambda: flipped.hop(1),
        lambda: flipped.hop(2),
        lambda: flipped.hop(3),
        flipped.cross,
    )

    def comm(s):
        for lag, stage in (
            (LAGS[5], lambda g: g.cross()),
            (LAGS[4], lambda g: g.far_rest()),
            (LAGS[2], lambda g: (g.hop(3), g.near_rest())),
            (LAGS[1], lambda g: g.hop(2)),
            (LAGS[0], lambda g: g.hop(1)),
            (0, lambda g: g.own()),
        ):
            if 0 <= s - lag < count:
                stage(chunks[s - lag])
        for i in range(count):
            if s == max(0, i - LEAD):
                chunks[i].near_own()
            if s == max(1, i + LAGS[3]):
                chunks[i].far_own()
        for at, work in zip(FLIP_STEPS, flip_work):
            if at == s:
                work()
        if s == SWAP_STEPS[0]:
            swap_x.start()
            mask_out.start()
            mask_own.start()
        if s == SWAP_STEPS[1]:
            for k in range(2):
                swap_x.wait_in(k)
                passed(c, k).start()
        if s == SWAP_STEPS[2]:
            swap_c.start()

    nq = q_s.shape[0]
    nk = k_s.shape[0]
    block = xf.shape[1]
    own_rows = pl.ds(pl.multiple_of(c * nq, nq), nq)
    copies = []

    def emit(src, dst):
        copy = pltpu.make_async_copy(src, dst, out_sem.at[len(copies)])
        copy.start()
        copies.append(copy)

    def vectors():
        for q in range(NP):
            for core in range(2):
                part = gv[q, core].astype(F32)
                first = (2 * q + core) * ROWS
                vec[0:6, first : first + ROWS] = part[0:6, 0:ROWS]
        part = gv[0, 0].astype(F32)
        per = COLS // 128
        for i in range(2 + QUARTERS):
            for tau in range(T):
                for r in range(per):
                    row = 6 + i * per + r
                    at = tau * COLS + r * 128
                    vec[6 + i : 7 + i, at : at + 128] = part[row : row + 1, tau * 128 : tau * 128 + 128]
        emit(vec, o_vec)
        mask_in.wait_recv()
        mask_own.wait()
        rows = mf[t // 2].T
        col = jnp.where(lax.rem(t, 2) == 0, rows[:, 0:1], rows[:, 1:2])
        bias[...] = jnp.where(col > 0, 0.0, NEG).astype(F32)
        emit(bias, o_bias)

    def norm_one():
        for k in range(2):
            passed(1 - c, k).wait_recv()
        emit(xf.at[pl.ds(2 * c, 2)], o_x)
        size = 32
        per = block // size

        def run(i, carry):
            at = pl.ds(pl.multiple_of(lax.rem(i, per) * size, size), size)
            unit, unused = norm_parts(xf[i // per, at].astype(F32))
            normed[pl.ds(pl.multiple_of(i * size, size), size)] = (
                unit * vec[0:1] + vec[1:2]
            ).astype(BF16)
            return carry

        lax.fori_loop(0, nk // size, run, 0)

        def flip(cols, i):
            nt[cols] = to_lanes(normed[own_rows, cols])

        tiles(D, TILE, flip)
        emit(nt, o_nt)

    def project(j, dst, rows, shift):
        a = normed[rows]

        def run(cols, i):
            out = jnp.dot(a, matrix(gw, j, cols), preferred_element_type=F32)
            if shift is not None:
                out = out + vec[shift : shift + 1, cols]
            dst[:, cols] = out.astype(BF16)

        tiles(D, TILE, run)

    def heads(first, last):
        def run(i, carry):
            cols = pl.ds(pl.multiple_of(i * 2 * HD, 2 * HD), 2 * HD)
            q_t = (q_s[:, cols].astype(F32).T * HD ** (-0.5)).astype(BF16)
            v_t = to_lanes(v_s[:, cols])
            k = k_s[:, cols]
            parts = []
            for h in range(2):
                probs = head_probs(k, head_rows(q_t, h), bias[...]).astype(BF16)
                parts.append(
                    jnp.dot(v_t[h * HD : (h + 1) * HD], probs, preferred_element_type=F32)
                )
            att[:, cols] = jnp.concatenate(parts, axis=0).T.astype(BF16)
            return carry

        lax.fori_loop(first, last, run, 0)

    def middle():
        emit(att, o_att)
        a = att[...]
        x_own = xf.at[pl.ds(2 * c, 2)]

        def run(cols, i):
            out = dot_nt(a, matrix_rows(gw, 3, i))
            resid[:, cols] = (
                x_own[:, :, cols].astype(F32).reshape(nq, TILE) + out + vec[2:3, cols]
            )

        tiles(D, TILE, run)
        emit(resid, o_resid)

        def norm(rows, i):
            unit, unused = norm_parts(resid[rows])
            n2[rows] = (unit * vec[3:4] + vec[4:5]).astype(BF16)

        tiles(nq, 64, norm)

        def flip(cols, i):
            n2t[cols] = to_lanes(n2[:, cols])

        tiles(D, TILE, flip)
        emit(n2t, o_n2t)

    def grads_in():
        for k in range(2):
            swap_c.wait_in(k)
        emit(cf, o_cot)

        def flip(cols, i):
            mgt[cols] = to_lanes(cf[:, :, cols].reshape(nq, TILE))

        tiles(D, TILE, flip)
        emit(mgt, o_mgt)

    def quarter_up(j):
        a = n2[...]

        def run(cols, i):
            z = jnp.dot(a, matrix(gw, 4 + j, cols), preferred_element_type=F32)
            z = z + vec[8 + j : 9 + j, cols]
            share = 0.5 + 0.5 * lax.erf(z * 0.5**0.5)
            hid[j, :, cols] = (z * share).astype(BF16)
            slope[:, cols] = share + z * (jnp.exp(-0.5 * z * z) * (0.5 / jnp.pi) ** 0.5)

        tiles(D, TILE, run)
        emit(hid.at[j], o_hid.at[j])

    def quarter_down(j):
        g = cf[...].reshape(nq, D)

        def back(cols, i):
            h = jnp.dot(g, matrix(gw, 8 + j, cols), preferred_element_type=F32)
            grad = (slope[:, cols] * h).astype(BF16)
            pre[j, :, cols] = grad
            ups[j : j + 1, cols] = jnp.sum(grad.astype(F32), axis=0, keepdims=True)

        tiles(D, TILE, back)
        emit(pre.at[j], o_pre.at[j])

        def outs(cols, i):
            m = dot_nt(hid[j], matrix_rows(gw, 8 + j, i))
            n = dot_nt(pre[j], matrix_rows(gw, 4 + j, i))
            if j == 0:
                mlp[:, cols] = m
                n2g[:, cols] = n
            elif j < QUARTERS - 1:
                mlp[:, cols] += m
                n2g[:, cols] += n
            else:
                n2g[:, cols] += n
                blk[:, cols] = (resid[:, cols] + mlp[:, cols] + m + vec[5:6, cols]).astype(BF16)

        tiles(D, TILE, outs)

    whole = pl.ds(0, nk)
    after = {
        8: (vectors, norm_one),
        9: (lambda: project(0, q_s, own_rows, 6), lambda: emit(q_s, o_q)),
        10: (lambda: project(1, k_s, whole, None), lambda: emit(k_s, o_k)),
        11: (lambda: project(2, v_s, whole, 7), lambda: emit(v_s, o_v), lambda: heads(0, 2)),
        12: (lambda: heads(2, 6),),
        13: (lambda: heads(6, 8), middle),
        14: (lambda: quarter_up(0), grads_in, lambda: quarter_down(0)),
        15: (lambda: quarter_up(1),),
        16: (lambda: quarter_down(1),),
        17: (lambda: quarter_up(2),),
        18: (lambda: quarter_down(2), flipped.ready, flipped.finish, lambda: quarter_up(3)),
        19: (lambda: quarter_down(3),),
    }
    lag = LAGS[5] + 1
    for s in range(count + lag):
        comm(s)
        if 0 <= s - lag < count:
            i = s - lag
            chunks[i].ready()
            if 1 <= i <= 4:
                emit(gw.at[ORDER[i - 1]], o_w.at[ORDER[i - 1]])
        for unit in after.get(s, ()):
            unit()
        if 0 <= s - lag - 1 < count:
            chunks[s - lag - 1].finish()
    emit(n2g, o_n2g)
    emit(blk, o_blk)
    emit(ups, o_ups)
    chunks[-1].finish()
    for k in range(2):
        passed(c, k).wait_send()
        swap_x.wait_out(k)
        swap_c.wait_out(k)
    mask_out.wait_send()
    for copy in copies:
        copy.wait()


def forward_all(w, v, x, cot, valid):
    any_space = pl.BlockSpec(memory_space=pl.ANY)
    dma = pltpu.SemaphoreType.DMA
    n = TILES + 1
    block = x.shape[1]
    nk = T * block
    nq = nk // 2
    gathered = (NP, 2, ROWS, D)

    def half(rows, cols=D):
        return (rows, cols), BF16

    outs = (
        ((4,) + gathered, BF16),
        ((16, D), F32),
        ((2, block, D), BF16),
        ((2, block, D), BF16),
        ((nk, 1), F32),
        half(nq),
        half(nk),
        half(nk),
        half(nq),
        half(D, nq),
        half(D, nq),
        half(D, nq),
        ((QUARTERS, nq, D), BF16),
        ((QUARTERS, nq, D), BF16),
        ((nq, D), F32),
        ((nq, D), F32),
        half(nq),
        ((8, D), F32),
    )
    scratch = (
        ((TILES,) + gathered, BF16),
        ((NP, 2, VROWS, 128 * T), BF16),
        ((T, block, D), BF16),
        ((2, block, D), BF16),
        ((2,) + valid.shape, F32),
        ((16, D), F32),
        ((nk, 1), F32),
        half(nk),
        half(nq),
        half(nk),
        half(nk),
        half(nq),
        ((nq, D), F32),
        half(nq),
        half(D, nq),
        half(D, nq),
        half(D, nq),
        ((QUARTERS, nq, D), BF16),
        ((QUARTERS, nq, D), BF16),
        ((nq, D), F32),
        ((nq, D), F32),
        ((nq, D), F32),
        half(nq),
        ((8, D), F32),
    )
    return pl.pallas_call(
        forward_kernel,
        out_shape=[jax.ShapeDtypeStruct(*o) for o in outs],
        in_specs=[any_space] * 5,
        out_specs=[any_space] * len(outs),
        scratch_shapes=[pltpu.VMEM(*o) for o in scratch]
        + [
            dma((4, 2)),
            dma((3,)),
            dma((2, 2)),
            dma((32,)),
            dma((n, T)),
            dma((n, 2, T)),
            dma((n,)),
            dma((n, 12)),
            dma((n, 12)),
            dma((n,)),
            dma((n,)),
        ],
        name="forward_all",
        compiler_params=pltpu.CompilerParams(
            collective_id=0, has_side_effects=True, vmem_limit_bytes=60 << 20
        ),
    )(w, v, x, cot, valid)


STAGES = (0, 1, 3, 4)
SEQUENCE = (8, 9, 5, 10, 6, 11, 7, 3, 0, 2, 1, 4)
CHAIN = TILES - 1
SLOTS = 5


def backward_kernel(
    i_w, i_vec, i_x, i_cot, i_bias, i_q, i_k, i_v, i_att, i_nt, i_n2t, i_mgt, i_hid, i_pre,
    i_n2g, i_resid, blk, i_ups,
    out, vec_out, own_blk, own_ig,
    vec, x, cot, bias, q_s, k_s, v_s, att, at, hid, pre, grad, resid, wb, branch, att_g,
    dq, dk, dv, came, ig, sums,
    stage, held, far_in, near_in, line_in, vec_held, vec_in, flip_line, flip_far, flip_near, flip_sum,
    load_sem, swap_sem, pair_out, pair_in, far_sem, near_sem, line_sem, vec_sem, ex_sem,
):
    spot = place()
    d, t, c, p, px, py, pd = spot
    loads = {}

    def load(name, src, dst):
        copy = pltpu.make_async_copy(src, dst, load_sem.at[len(loads)])
        copy.start()
        loads[name] = copy

    load("mgt", i_mgt, at.at[3])
    load("hid0", i_hid.at[0], hid.at[0])
    load("n2t", i_n2t, at.at[2])
    load("pre0", i_pre.at[0], pre.at[0])
    load("vec", i_vec, vec)
    load("resid", i_resid, resid)
    load("grad", i_n2g, grad)
    load("cot", i_cot, cot)
    load("wp", i_w.at[3], wb.at[0])
    load("hid1", i_hid.at[1], hid.at[1])
    load("pre1", i_pre.at[1], pre.at[1])
    load("q", i_q, q_s)
    load("k", i_k, k_s)
    load("v", i_v, v_s)
    load("bias", i_bias, bias)
    load("wk", i_w.at[1], wb.at[1])
    load("hid2", i_hid.at[2], hid.at[2])
    load("pre2", i_pre.at[2], pre.at[2])
    load("hid3", i_hid.at[3], hid.at[3])
    load("pre3", i_pre.at[3], pre.at[3])
    load("att", i_att, att)
    load("nt", i_nt, at.at[0])
    load("x", i_x, x)
    load("ups", i_ups, sums.at[pl.ds(8, 8)])

    greet(d, t, c, p, px, py)
    partner = (2 * p + 1 - c, t)
    side = ((2 * px + c, t), (2 * py + c, t))
    swap_b = Exchange(blk, own_blk, ex_sem.at[0], ex_sem.at[1], spot, False)
    swap_i = Exchange(ig, own_ig, ex_sem.at[2], ex_sem.at[3], spot, False)
    half = ROWS // 2
    nq = resid.shape[0]
    own_rows = pl.ds(pl.multiple_of(c * nq, nq), nq)
    other_rows = pl.ds(pl.multiple_of((1 - c) * nq, nq), nq)

    def slot(j):
        return j % SLOTS

    def outgoing(j):
        return stage.at[j % 2] if j < CHAIN else near_in.at[pl.ds(6, NP)]

    def pair(j):
        return remote(
            outgoing(j), held.at[j], pair_out.at[j % 2 if j < CHAIN else 2], pair_in.at[j], partner
        )

    def far(j, way):
        return remote(
            held.at[j, pd, pl.ds(way * half, half)],
            far_in.at[slot(j), way],
            far_sem.at[0, j, way],
            far_sem.at[1, j, way],
            side[way],
        )

    def near(j, way):
        return remote(
            held.at[j, (px, py)[way]],
            near_in.at[2 * slot(j) + way],
            near_sem.at[0, j, way],
            near_sem.at[1, j, way],
            side[way],
        )

    def line(j, tau, way):
        return remote(
            held.at[j, p, :, pl.ds(tau * COLS, COLS)],
            line_in.at[j, tau + 1 - way],
            line_sem.at[0, j, tau + 1 - way],
            line_sem.at[1, j, tau + 1 - way],
            (d, t + (1 if way == 0 else -1)),
        )

    vec_partners = (
        partner,
        side[0],
        side[1],
        (d, t + 1 - 2 * lax.rem(t, 2)),
        (d, t + 2 - 4 * (t // 2)),
    )

    def vec_copy(r):
        return remote(vec_held.at[r], vec_in.at[r], vec_sem.at[0, r], vec_sem.at[1, r], vec_partners[r])

    def factors(j):
        m = SEQUENCE[j]
        if m >= 8:
            return at.at[3], hid.at[m - 8]
        if m >= 4:
            return at.at[2], pre.at[m - 4]
        if m == 3:
            return at.at[1], att
        return at.at[0], (dq, dk.at[own_rows], dv.at[own_rows])[m]

    waits = {
        0: ("mgt", "hid0"), 1: ("hid1",), 2: ("pre1",), 3: ("hid2",), 4: ("pre2",), 5: ("hid3",),
        6: ("pre3",), 7: ("att",), 8: ("nt",), CHAIN: ("n2t", "pre0"),
    }

    def product(j, q, core):
        a, b = factors(j)
        rows = pl.ds(pl.multiple_of((2 * q + core) * ROWS, ROWS), ROWS)
        return jnp.dot(a[rows], b[...], preferred_element_type=F32)

    def each_chip(body):
        def run(q, carry):
            body(q)
            return carry

        lax.fori_loop(0, NP, run, 0)

    def first(j):
        for name in waits.get(j, ()):
            loads[name].wait()
        if 2 <= j < CHAIN:
            pair(j - 2).wait_send()

        def make(q):
            outgoing(j)[q] = product(j, q, 1 - c).astype(BF16)

        each_chip(make)
        pair(j).start()

    def second(j):
        pair(j).wait_recv()

        def make(q):
            held[j, q] = (product(j, q, c) + held[j, q].astype(F32)).astype(BF16)

        each_chip(make)
        if j < CHAIN:
            for way in range(2):
                far(j, way).start()

    def third(j):
        for way in range(2):
            far(j, way).wait_recv()
            part = pl.ds(way * half, half)
            q = (py, px)[way]
            held[j, q, part] = (
                held[j, q, part].astype(F32) + far_in[slot(j), way].astype(F32)
            ).astype(BF16)
            near(j, 1 - way).start()

    def fourth(j):
        near(j, 0).wait_recv()
        near(j, 1).wait_recv()
        for tau in range(T):
            cols = pl.ds(tau * COLS, COLS)
            total = (
                held[j, p, :, cols].astype(F32)
                + near_in[2 * slot(j), :, cols].astype(F32)
                + near_in[2 * slot(j) + 1, :, cols].astype(F32)
            )
            held[j, p, :, cols] = total.astype(BF16)

            @pl.when(t == tau)
            def _():
                out[j] = total

    def lines(s):
        for way in range(2):
            hop = t if way == 0 else T - 1 - t
            j = s - STAGES[3] - hop

            @pl.when(jnp.logical_and(j >= 0, j < CHAIN))
            def _():
                for tau in range(T) if way else reversed(range(T)):

                    @pl.when((tau > t) if way == 0 else (tau < t))
                    def _():
                        cols = pl.ds(tau * COLS, COLS)

                        @pl.when(hop > 0)
                        def _():
                            line(j, tau, way).wait_recv()
                            held[j, p, :, cols] = (
                                held[j, p, :, cols].astype(F32)
                                + line_in[j, tau + 1 - way].astype(F32)
                            ).astype(BF16)

                        line(j, tau, way).start()

    def last(j):
        for way in range(2):

            @pl.when((t > 0) if way == 0 else (t < T - 1))
            def _():
                for tau in range(T):

                    @pl.when(t == tau)
                    def _():
                        line(j, tau, way).wait_recv()
                        out[j] += line_in[j, tau + 1 - way].astype(F32)

    def drain(j):
        for way in range(2):
            far(j, way).wait_send()
            near(j, way).wait_send()
            for tau in range(T):

                @pl.when((tau > t) if way == 0 else (tau < t))
                def _():
                    line(j, tau, way).wait_send()

    def flip_copy(tau, way):
        part = held.at[CHAIN, :, :, pl.ds(tau * COLS, COLS)]
        at = tau + 1 - way
        return remote(
            part,
            flip_line.at[at],
            line_sem.at[0, CHAIN, at],
            line_sem.at[1, CHAIN, at],
            (d, t + (1 if way == 0 else -1)),
        )

    def flip_hop(hop):
        for way in range(2):
            for place_z in range(T):

                @pl.when(jnp.logical_and(t == place_z, hop == (t if way == 0 else T - 1 - t)))
                def _():
                    for tau in range(T) if way else reversed(range(T)):
                        if (tau < place_z) if way else (tau > place_z):
                            if hop > 0:
                                cols = pl.ds(tau * COLS, COLS)
                                flip_copy(tau, way).wait_recv()
                                held[CHAIN, :, :, cols] = (
                                    held[CHAIN, :, :, cols].astype(F32)
                                    + flip_line[tau + 1 - way].astype(F32)
                                ).astype(BF16)
                            flip_copy(tau, way).start()

    def flip_send(kind, way):
        if kind == 0:
            src = flip_sum.at[pd, pl.ds(way * half, half)]
            return remote(
                src, flip_far.at[way], far_sem.at[0, CHAIN, way], far_sem.at[1, CHAIN, way], side[way]
            )
        return remote(
            flip_sum.at[(px, py)[way]],
            flip_near.at[way],
            near_sem.at[0, CHAIN, way],
            near_sem.at[1, CHAIN, way],
            side[way],
        )

    def flip_join():
        for place_z in range(T):

            @pl.when(t == place_z)
            def _():
                total = held[CHAIN, :, :, pl.ds(place_z * COLS, COLS)].astype(F32)
                for way in range(2):
                    if place_z != (0, T - 1)[way]:
                        flip_copy(place_z, way).wait_recv()
                        total = total + flip_line[place_z + 1 - way].astype(F32)
                flip_sum[...] = total.astype(BF16)

        for way in range(2):
            flip_send(0, way).start()

    def flip_ring():
        for way in range(2):
            flip_send(0, way).wait_recv()
            part = pl.ds(way * half, half)
            q = (py, px)[way]
            flip_sum[q, part] = (
                flip_sum[q, part].astype(F32) + flip_far[way].astype(F32)
            ).astype(BF16)
            flip_send(1, 1 - way).start()

    def flip_last():
        for way in range(2):
            flip_send(1, way).wait_recv()
        out[CHAIN] = (
            flip_sum[p].astype(F32) + flip_near[0].astype(F32) + flip_near[1].astype(F32)
        )
        for way in range(2):
            flip_send(0, way).wait_send()
            flip_send(1, way).wait_send()
            for tau in range(T):

                @pl.when((tau > t) if way == 0 else (tau < t))
                def _():
                    flip_copy(tau, way).wait_send()

    def comm(s):
        for lag, work in ((STAGES[0], second), (STAGES[1], third), (STAGES[2], fourth)):
            if 0 <= s - lag < CHAIN:
                work(s - lag)
        if STAGES[3] <= s < CHAIN + STAGES[3] + T - 1:
            lines(s)
        if 0 <= s - STAGES[3] - T < CHAIN:
            last(s - STAGES[3] - T)
            drain(s - STAGES[3] - T)

    def add(row, a):
        sums[row : row + 1] += jnp.sum(a, axis=0, keepdims=True)

    def mid_back():
        for name in ("vec", "resid", "grad", "cot", "ups"):
            loads[name].wait()
        sums[0:8] = jnp.zeros((8, D), F32)

        def run(rows, i):
            unit, inverse = norm_parts(resid[rows])
            g = grad[rows]
            outer = cot[rows].astype(F32)
            total = outer + norm_back(g, unit, inverse, vec[3:4])
            resid[rows] = total
            low = total.astype(BF16)
            branch[rows] = low
            add(2, low.astype(F32))
            add(3, g * unit)
            add(4, g)
            add(5, outer)

        tiles(nq, 64, run)

    def att_back():
        loads["wp"].wait()
        a = branch[...]

        def run(cols, i):
            at[1, cols] = to_lanes(branch[:, cols])
            att_g[:, cols] = jnp.dot(a, matrix(wb, 0, cols), preferred_element_type=F32).astype(BF16)

        tiles(D, TILE, run)
        load("wq", i_w.at[0], wb.at[0])

    def heads(first_pair, last_pair):
        if first_pair == 0:
            for name in ("q", "k", "v", "bias"):
                loads[name].wait()

        def run(i, carry):
            cols = pl.ds(pl.multiple_of(i * 2 * HD, 2 * HD), 2 * HD)
            k, v, g = k_s[:, cols], v_s[:, cols], att_g[:, cols]
            q_f = q_s[:, cols].astype(F32) * HD ** (-0.5)
            q_l = q_f.astype(BF16)
            q_t = q_f.T.astype(BF16)
            g_t = to_lanes(g)
            k_t = to_lanes(k)
            parts, dk_parts, dv_parts = [], [], []
            for h in range(2):
                probs = head_probs(k, head_rows(q_t, h), bias[...])
                dv_parts.append(
                    jnp.dot(probs.astype(BF16), head_lanes(g, h), preferred_element_type=F32)
                )
                dp = jnp.dot(v, head_rows(g_t, h), preferred_element_type=F32)
                ds = (probs * (dp - jnp.sum(dp * probs, axis=0, keepdims=True))).astype(BF16)
                parts.append(jnp.dot(k_t[h * HD : (h + 1) * HD], ds, preferred_element_type=F32))
                dk_parts.append(jnp.dot(ds, head_lanes(q_l, h), preferred_element_type=F32))
            dq[:, cols] = (jnp.concatenate(parts, axis=0).T * HD ** (-0.5)).astype(BF16)
            dk[:, cols] = (dk_parts[0] + dk_parts[1]).astype(BF16)
            dv[:, cols] = (dv_parts[0] + dv_parts[1]).astype(BF16)
            return carry

        lax.fori_loop(first_pair, last_pair, run, 0)

    def pass_on(i):
        src = (dk, dv)[i].at[other_rows]
        return remote(src, came.at[i], swap_sem.at[0, i], swap_sem.at[1, i], partner)

    def query_back():
        pass_on(0).start()
        pass_on(1).start()
        loads["wq"].wait()
        a = dq[...]

        def run(cols, i):
            grad[:, cols] = dot_nt(a, matrix_rows(wb, 0, i))
            sums[6:7, cols] = jnp.sum(dq[:, cols].astype(F32), axis=0, keepdims=True)

        tiles(D, TILE, run)
        load("wv", i_w.at[2], wb.at[0])

    def key_back():
        for i, ref in enumerate((dk, dv)):
            pass_on(i).wait_recv()

            def join(cols, n):
                total = (ref[own_rows, cols].astype(F32) + came[i, :, cols].astype(F32)).astype(BF16)
                ref[own_rows, cols] = total
                if i == 1:
                    sums[7:8, cols] = jnp.sum(total.astype(F32), axis=0, keepdims=True)

            tiles(D, TILE, join)
        loads["wk"].wait()
        loads["wv"].wait()
        a, b = dk[own_rows], dv[own_rows]

        def run(cols, i):
            grad[:, cols] += dot_nt(a, matrix_rows(wb, 1, i)) + dot_nt(b, matrix_rows(wb, 0, i))

        tiles(D, TILE, run)

    def front_back():
        loads["x"].wait()
        size = 32
        per = ig.shape[1] // size

        def run(rows, i):
            unit, inverse = norm_parts(x[rows].astype(F32))
            g = grad[rows]
            add(0, g * unit)
            add(1, g)
            total = resid[rows] + norm_back(g, unit, inverse, vec[0:1])
            ig[i // per, pl.ds(pl.multiple_of(lax.rem(i, per) * size, size), size)] = total.astype(BF16)

        tiles(nq, size, run)
        swap_i.start()
        vec_held[0] = sums[...]
        vec_copy(0).start()

    def vec_round(r):
        vec_copy(r).wait_recv()
        vec_held[r + 1] = vec_held[r] + vec_in[r]
        if r < 4:
            vec_copy(r + 1).start()
        else:
            vec_out[...] = vec_held[5]

    def flip_start():
        pair(CHAIN).wait_send()
        second(CHAIN)
        flip_hop(0)

    between = {
        0: (lambda: first(CHAIN),),
        1: (flip_start,),
        2: (att_back, lambda: heads(0, 1)),
        3: (lambda: heads(1, 2),),
        4: (lambda: heads(2, 3),),
        5: (lambda: heads(3, 4),),
        6: (lambda: heads(4, 6),),
        7: (lambda: heads(6, 8), query_back),
        8: (key_back,),
        9: (front_back,),
    }
    after = {
        1: (mid_back,),
        3: (lambda: flip_hop(1), swap_b.start),
        5: (lambda: flip_hop(2),),
        7: (lambda: flip_hop(3),),
        9: (flip_join,),
        10: (flip_ring,),
        11: (lambda: vec_round(0),),
        12: (flip_last, lambda: vec_round(1)),
        13: (lambda: vec_round(2),),
        14: (lambda: vec_round(3),),
        15: (lambda: vec_round(4),),
    }
    for s in range(CHAIN + STAGES[3] + T):
        if s < CHAIN:
            first(s)
        for unit in between.get(s, ()):
            unit()
        comm(s)
        for unit in after.get(s, ()):
            unit()
    for j in (CHAIN - 2, CHAIN - 1):
        pair(j).wait_send()
    for i in range(2):
        pass_on(i).wait_send()
    for r in range(5):
        vec_copy(r).wait_send()
    for swap in (swap_b, swap_i):
        for k in range(2):
            swap.wait_in(k)
            swap.wait_out(k)


def backward_all(*args):
    any_space = pl.BlockSpec(memory_space=pl.ANY)
    vmem = pl.BlockSpec(memory_space=pltpu.VMEM)
    dma = pltpu.SemaphoreType.DMA
    n = TILES
    blk, resid, bias = args[16], args[15], args[4]
    nq, nk = resid.shape[0], bias.shape[0]
    own = (nq, D)
    scratch = (
        ((16, D), F32),
        (own, BF16),
        (own, BF16),
        ((nk, 1), F32),
        (own, BF16),
        ((nk, D), BF16),
        ((nk, D), BF16),
        (own, BF16),
        ((4, D, nq), BF16),
        ((QUARTERS,) + own, BF16),
        ((QUARTERS,) + own, BF16),
        (own, F32),
        (own, F32),
        ((2, NP, 2, ROWS, D), BF16),
        (own, BF16),
        (own, BF16),
        (own, BF16),
        ((nk, D), BF16),
        ((nk, D), BF16),
        ((2,) + own, BF16),
        (blk.shape, BF16),
        ((16, D), F32),
        ((2, NP, ROWS, D), BF16),
        ((n, NP, ROWS, D), BF16),
        ((SLOTS, 2, ROWS // 2, D), BF16),
        ((2 * SLOTS, ROWS, D), BF16),
        ((CHAIN, T + 1, ROWS, COLS), BF16),
        ((6, 16, D), F32),
        ((5, 16, D), F32),
        ((T + 1, NP, ROWS, COLS), BF16),
        ((2, ROWS // 2, COLS), BF16),
        ((2, ROWS, COLS), BF16),
        ((NP, ROWS, COLS), BF16),
    )
    return pl.pallas_call(
        backward_kernel,
        out_shape=(
            jax.ShapeDtypeStruct((n, ROWS, COLS), F32),
            jax.ShapeDtypeStruct((16, D), F32),
            jax.ShapeDtypeStruct(blk.shape, BF16),
            jax.ShapeDtypeStruct(blk.shape, BF16),
        ),
        in_specs=[any_space] * len(args),
        out_specs=[vmem, vmem, any_space, any_space],
        scratch_shapes=[pltpu.VMEM(*o) for o in scratch]
        + [
            dma((32,)),
            dma((2, 2)),
            dma((3,)),
            dma((n,)),
            dma((2, n, 2)),
            dma((2, n, 2)),
            dma((2, n, T + 1)),
            dma((2, 5)),
            dma((4, 2)),
        ],
        name="backward_all",
        compiler_params=pltpu.CompilerParams(
            collective_id=1, has_side_effects=True, vmem_limit_bytes=60 << 20
        ),
    )(*args)


def head_probs(k, q_t, bias):
    s = jnp.dot(k, q_t, preferred_element_type=F32) + bias
    e = jnp.exp(s - jnp.max(s, axis=0, keepdims=True))
    return e / jnp.sum(e, axis=0, keepdims=True)


def head_rows(q_t, h):
    row = lax.broadcasted_iota(jnp.int32, q_t.shape, 0) // HD
    return jnp.where(row == h, q_t, jnp.zeros_like(q_t))


def head_lanes(q, h):
    lane = lax.broadcasted_iota(jnp.int32, q.shape, 1) // HD
    return jnp.where(lane == h, q, jnp.zeros_like(q))


def norm_parts(values):
    center = values - jnp.mean(values, axis=-1, keepdims=True)
    spread = jnp.mean(center * center, axis=-1, keepdims=True)
    inverse = lax.rsqrt(spread + EPS)
    return center * inverse, inverse


def norm_back(grad, unit, inverse, gain):
    scaled = grad * gain
    return inverse * (
        scaled
        - jnp.mean(scaled, axis=-1, keepdims=True)
        - unit * jnp.mean(scaled * unit, axis=-1, keepdims=True)
    )


def dot_nn(a, b):
    return lax.dot_general(a, b, (((1,), (0,)), ((), ())), preferred_element_type=F32)


def dot_nt(a, b):
    return lax.dot_general(a, b, (((1,), (1,)), ((), ())), preferred_element_type=F32)


def per_device_chips(
    activations, cotangent, token_valid, image_counts, pre_gain, pre_shift, attn_weight,
    attn_bias, proj_weight, proj_bias, mid_gain, mid_shift, up_weight, up_bias, down_weight,
    down_bias,
):
    local_rows = activations.shape[0]
    slots = activations.shape[1]
    block = -(-local_rows // 16) * 16
    pad = block - local_rows
    d = lax.axis_index("dp")
    t = lax.axis_index("tensor")
    c = lax.rem(d, 2)
    first_row = t * local_rows
    my_valid = lax.dynamic_slice_in_dim(token_valid, first_row, local_rows, 1).astype(F32)
    slot_live = (jnp.arange(slots, dtype=jnp.int32) < image_counts[0]).astype(F32)
    out_mask = jnp.transpose(slot_live[:, None] * my_valid)[:, :, None]

    def to_blocks(a):
        return jnp.pad(jnp.transpose(a, (1, 0, 2)), ((0, 0), (0, pad), (0, 0)))

    x_blocks = to_blocks(activations)
    c_blocks = to_blocks((cotangent.astype(F32) * out_mask).astype(BF16))
    valid = jnp.pad(
        token_valid.astype(F32).reshape(slots, T, local_rows), ((0, 0), (0, 0), (0, pad))
    ).reshape(slots, T * block)
    valid = jnp.pad(valid, ((0, 8 - slots), (0, 0)))
    per_j = up_weight.shape[1] // COLS
    w = jnp.concatenate(
        [
            attn_weight,
            jnp.transpose(proj_weight)[None],
            jnp.transpose(up_weight.reshape(ROWS, per_j, COLS), (1, 0, 2)),
            jnp.transpose(down_weight.reshape(per_j, COLS, ROWS), (0, 2, 1)),
        ],
        axis=0,
    )
    v = jnp.concatenate(
        [
            jnp.stack([pre_gain, pre_shift, proj_bias, mid_gain, mid_shift, down_bias]),
            attn_bias.reshape(-1, 128),
            up_bias.reshape(-1, 128),
        ],
        axis=0,
    )
    v = jnp.pad(v, ((0, VROWS - v.shape[0]), (0, 0)))
    (
        full_w, vec, x_own, own_cot, bias, queries, keys, values, attended, normed_t, normed2_t,
        mlp_grad_t, hidden, pre_grad, normed2_grad, resid, block_own, up_sums,
    ) = forward_all(w, v, x_blocks, c_blocks, valid)
    own = resid.shape
    grads, totals, own_block, own_input = backward_all(
        full_w, vec, x_own.reshape(own), own_cot.reshape(own), bias, queries, keys,
        values, attended, normed_t, normed2_t, mlp_grad_t, hidden, pre_grad, normed2_grad, resid,
        block_own.reshape(own_cot.shape), up_sums,
    )
    owned = lax.dynamic_slice(totals, (0, d * ROWS), (6, ROWS))
    parted = lax.dynamic_slice(totals, (0, t * COLS), (totals.shape[0], COLS))

    def from_blocks(a):
        return jnp.transpose(a[:, :local_rows], (1, 0, 2))

    block_out = (from_blocks(own_block).astype(F32) * out_mask).astype(BF16)
    input_grad = from_blocks(own_input).astype(F32)
    at = {m: i for i, m in enumerate(SEQUENCE)}
    quarters = range(QUARTERS)
    return (
        block_out,
        input_grad,
        owned[0],
        owned[1],
        jnp.stack([grads[at[m]] for m in range(3)]),
        parted[6:8],
        jnp.transpose(grads[at[3]]),
        owned[2],
        owned[3],
        owned[4],
        jnp.concatenate([grads[at[4 + j]] for j in quarters], axis=1),
        parted[8 : 8 + QUARTERS].reshape(-1),
        jnp.concatenate([jnp.transpose(grads[at[8 + j]]) for j in quarters], axis=0),
        owned[5],
    )


def solution(mesh):
    sizes = (mesh.shape["dp"], mesh.shape["tensor"])
    per_device = per_device_chips if sizes == (2 * NP, T) else per_device_general
    return jax.shard_map(
        per_device,
        mesh=mesh,
        in_specs=(
            P("tensor", "dp", None),
            P("tensor", "dp", None),
            P("dp", None),
            P("dp"),
            P("dp"),
            P("dp"),
            P(None, "dp", "tensor"),
            P(None, "tensor"),
            P("tensor", "dp"),
            P("dp"),
            P("dp"),
            P("dp"),
            P("dp", "tensor"),
            P("tensor"),
            P("tensor", "dp"),
            P("dp"),
        ),
        out_specs=(
            P("tensor", "dp", None),
            P("tensor", "dp", None),
            P("dp"),
            P("dp"),
            P(None, "dp", "tensor"),
            P(None, "tensor"),
            P("tensor", "dp"),
            P("dp"),
            P("dp"),
            P("dp"),
            P("dp", "tensor"),
            P("tensor"),
            P("tensor", "dp"),
            P("dp"),
        ),
        check_vma=False,
    )
```

```python
import functools

import jax
import jax.numpy as jnp
from jax import lax
from jax.experimental import pallas as pl
from jax.experimental.pallas import tpu as pltpu
from jax.sharding import PartitionSpec as P

D = 1024
H = 16
HD = 64
MB = 2


EPS = 1e-06
NEG = -1000000000.0


def layer_norm(values, gain, shift):
    center = values - jnp.mean(values, axis=-1, keepdims=True)
    spread = jnp.mean(center * center, axis=-1, keepdims=True)
    return center * lax.rsqrt(spread + EPS) * gain + shift


def gelu_exact(values):
    return jax.nn.gelu(values, approximate=False)


def per_device_general(
    activations,
    cotangent,
    token_valid,
    image_counts,
    pre_gain,
    pre_shift,
    attn_weight,
    attn_bias,
    proj_weight,
    proj_bias,
    mid_gain,
    mid_shift,
    up_weight,
    up_bias,
    down_weight,
    down_bias,
):
    f32 = jnp.float32
    bf16 = jnp.bfloat16
    tensor_size = lax.axis_size("tensor")
    local_rows = activations.shape[0]
    slots = activations.shape[1]
    per_micro = slots // MB
    heads_here = H // tensor_size
    width_here = attn_weight.shape[2]
    hidden_here = up_weight.shape[1]
    scale = HD ** (-0.5)
    first_row = lax.axis_index("tensor") * local_rows
    my_valid = lax.dynamic_slice_in_dim(token_valid, first_row, local_rows, 1).astype(f32)
    slot_live = (jnp.arange(slots, dtype=jnp.int32) < image_counts[0]).astype(f32)
    attn_bias_f = attn_bias.astype(f32)
    up_bias_f = up_bias.astype(f32)
    acc_attn = jnp.zeros((3, D, width_here), f32)
    acc_proj = jnp.zeros((width_here, D), f32)
    acc_up = jnp.zeros((D, hidden_here), f32)
    acc_down = jnp.zeros((hidden_here, D), f32)
    acc_attn_bias = jnp.zeros((2, width_here), f32)
    acc_up_bias = jnp.zeros((hidden_here,), f32)
    acc_vectors = [jnp.zeros((D,), f32) for unused in range(6)]
    block_parts = []
    input_parts = []
    for micro_step in range(MB):
        gathered = (
            lax.all_gather(attn_weight, "dp", axis=1, tiled=True),
            lax.all_gather(proj_weight, "dp", axis=1, tiled=True),
            lax.all_gather(up_weight, "dp", axis=0, tiled=True),
            lax.all_gather(down_weight, "dp", axis=1, tiled=True),
            lax.all_gather(pre_gain, "dp", axis=0, tiled=True),
            lax.all_gather(pre_shift, "dp", axis=0, tiled=True),
            lax.all_gather(proj_bias, "dp", axis=0, tiled=True),
            lax.all_gather(mid_gain, "dp", axis=0, tiled=True),
            lax.all_gather(mid_shift, "dp", axis=0, tiled=True),
            lax.all_gather(down_bias, "dp", axis=0, tiled=True),
        )
        qkv_full, proj_full, upw_full, downw_full = (
            gathered[0],
            gathered[1],
            gathered[2],
            gathered[3],
        )
        gain_one, shift_one, proj_bias_f, gain_two, shift_two, down_bias_f = [
            item.astype(f32) for item in gathered[4:]
        ]
        offset = micro_step * per_micro
        inputs_f = activations[:, offset : offset + per_micro].astype(f32)
        key_valid = token_valid[offset : offset + per_micro]
        key_bias = jnp.where(key_valid > 0, 0.0, NEG).astype(f32)
        out_mask = jnp.transpose(
            slot_live[offset : offset + per_micro][:, None] * my_valid[offset : offset + per_micro]
        )[:, :, None]
        normed = layer_norm(inputs_f, gain_one, shift_one).astype(bf16)
        normed_all = lax.all_gather(normed, "tensor", axis=0, tiled=True)
        full_rows = normed_all.shape[0]
        projected = jnp.einsum("sid,cde->csie", normed_all, qkv_full, preferred_element_type=f32)
        queries = (
            (projected[0] + attn_bias_f[0])
            .astype(bf16)
            .reshape(full_rows, per_micro, heads_here, HD)
        )
        keys = projected[1].astype(bf16).reshape(full_rows, per_micro, heads_here, HD)
        values = (
            (projected[2] + attn_bias_f[1])
            .astype(bf16)
            .reshape(full_rows, per_micro, heads_here, HD)
        )

        def scores_of(query_part, key_part):
            raw = jnp.einsum("qihe,kihe->ihqk", query_part, key_part, preferred_element_type=f32)
            return raw * scale + key_bias[:, None, None, :]

        scores = scores_of(queries, keys)
        top = jnp.max(scores, axis=-1, keepdims=True)
        expo = jnp.exp(scores - top)
        total = jnp.sum(expo, axis=-1, keepdims=True)
        logsum = top + jnp.log(total)
        probs_low = (expo / total).astype(bf16)
        attended = (
            jnp.einsum("ihqk,kihe->qihe", probs_low, values, preferred_element_type=f32)
            .astype(bf16)
            .reshape(full_rows, per_micro, width_here)
        )
        resid = (
            inputs_f
            + lax.psum_scatter(
                jnp.einsum("sie,ed->sid", attended, proj_full, preferred_element_type=f32),
                "tensor",
                scatter_dimension=0,
                tiled=True,
            )
            + proj_bias_f
        )
        normed2 = layer_norm(resid, gain_two, shift_two).astype(bf16)
        normed2_all = lax.all_gather(normed2, "tensor", axis=0, tiled=True)
        hidden_pre = (
            jnp.einsum("sid,df->sif", normed2_all, upw_full, preferred_element_type=f32) + up_bias_f
        )
        hidden = gelu_exact(hidden_pre).astype(bf16)
        mlp_out = (
            lax.psum_scatter(
                jnp.einsum("sif,fd->sid", hidden, downw_full, preferred_element_type=f32).astype(
                    jnp.bfloat16
                ),
                "tensor",
                scatter_dimension=0,
                tiled=True,
            ).astype(jnp.float32)
            + down_bias_f
        )
        block_parts.append(((resid + mlp_out) * out_mask).astype(bf16))
        outer = cotangent[:, offset : offset + per_micro].astype(f32) * out_mask
        mlp_grad = outer.astype(bf16)
        acc_vectors[5] = acc_vectors[5] + jnp.sum(mlp_grad.astype(f32), axis=(0, 1))
        mlp_grad_all = lax.all_gather(mlp_grad, "tensor", axis=0, tiled=True)
        acc_down = acc_down + jnp.einsum(
            "sif,sid->fd", hidden, mlp_grad_all, preferred_element_type=f32
        )
        hidden_grad = jnp.einsum(
            "sid,fd->sif", mlp_grad_all, downw_full, preferred_element_type=f32
        )
        unused, gelu_back = jax.vjp(gelu_exact, hidden_pre)
        pre_grad = gelu_back(hidden_grad)[0].astype(bf16)
        acc_up_bias = acc_up_bias + jnp.sum(pre_grad.astype(f32), axis=(0, 1))
        acc_up = acc_up + jnp.einsum(
            "sid,sif->df", normed2_all, pre_grad, preferred_element_type=f32
        )
        normed2_grad = lax.psum_scatter(
            jnp.einsum("sif,df->sid", pre_grad, upw_full, preferred_element_type=f32),
            "tensor",
            scatter_dimension=0,
            tiled=True,
        )
        unused, second_back = jax.vjp(layer_norm, resid, gain_two, shift_two)
        resid_part, gain_two_grad, shift_two_grad = second_back(normed2_grad)
        acc_vectors[3] = acc_vectors[3] + gain_two_grad
        acc_vectors[4] = acc_vectors[4] + shift_two_grad
        resid_grad = outer + resid_part
        branch_grad = resid_grad.astype(bf16)
        acc_vectors[2] = acc_vectors[2] + jnp.sum(branch_grad.astype(f32), axis=(0, 1))
        branch_all = lax.all_gather(branch_grad, "tensor", axis=0, tiled=True)
        acc_proj = acc_proj + jnp.einsum(
            "sie,sid->ed", attended, branch_all, preferred_element_type=f32
        )
        att_grad = (
            jnp.einsum("sid,ed->sie", branch_all, proj_full, preferred_element_type=f32)
            .astype(bf16)
            .reshape(full_rows, per_micro, heads_here, HD)
        )
        probs = jnp.exp(scores_of(queries, keys) - logsum)
        probs_again = probs.astype(bf16)
        value_grad = jnp.einsum(
            "ihqk,qihe->kihe", probs_again, att_grad, preferred_element_type=f32
        ).astype(bf16)
        prob_grad = jnp.einsum("qihe,kihe->ihqk", att_grad, values, preferred_element_type=f32)
        score_grad = (
            probs * (prob_grad - jnp.sum(prob_grad * probs, axis=-1, keepdims=True))
        ).astype(bf16)
        query_grad = (
            jnp.einsum("ihqk,kihe->qihe", score_grad, keys, preferred_element_type=f32) * scale
        ).astype(bf16)
        key_grad = (
            jnp.einsum("ihqk,qihe->kihe", score_grad, queries, preferred_element_type=f32) * scale
        ).astype(bf16)
        qkv_grad = jnp.stack([query_grad, key_grad, value_grad]).reshape(
            3, full_rows, per_micro, width_here
        )
        acc_attn_bias = acc_attn_bias + jnp.stack(
            [
                jnp.sum(qkv_grad[0].astype(f32), axis=(0, 1)),
                jnp.sum(qkv_grad[2].astype(f32), axis=(0, 1)),
            ]
        )
        acc_attn = acc_attn + jnp.einsum(
            "sid,csie->cde", normed_all, qkv_grad, preferred_element_type=f32
        )
        normed_grad = lax.psum_scatter(
            jnp.einsum("csie,cde->sid", qkv_grad, qkv_full, preferred_element_type=f32),
            "tensor",
            scatter_dimension=0,
            tiled=True,
        )
        unused, first_back = jax.vjp(layer_norm, inputs_f, gain_one, shift_one)
        input_part, gain_one_grad, shift_one_grad = first_back(normed_grad)
        acc_vectors[0] = acc_vectors[0] + gain_one_grad
        acc_vectors[1] = acc_vectors[1] + shift_one_grad
        input_parts.append(resid_grad + input_part)
    summed = lax.psum(
        (
            acc_vectors[0],
            acc_vectors[1],
            acc_vectors[2],
            acc_vectors[3],
            acc_vectors[4],
            acc_vectors[5],
        ),
        "tensor",
    )
    owned = (
        lax.psum_scatter(acc_attn, "dp", scatter_dimension=1, tiled=True),
        lax.psum_scatter(acc_proj, "dp", scatter_dimension=1, tiled=True),
        lax.psum_scatter(acc_up, "dp", scatter_dimension=0, tiled=True),
        lax.psum_scatter(acc_down, "dp", scatter_dimension=1, tiled=True),
        lax.psum_scatter(summed[0], "dp", scatter_dimension=0, tiled=True),
        lax.psum_scatter(summed[1], "dp", scatter_dimension=0, tiled=True),
        lax.psum_scatter(summed[2], "dp", scatter_dimension=0, tiled=True),
        lax.psum_scatter(summed[3], "dp", scatter_dimension=0, tiled=True),
        lax.psum_scatter(summed[4], "dp", scatter_dimension=0, tiled=True),
        lax.psum_scatter(summed[5], "dp", scatter_dimension=0, tiled=True),
    )
    bias_sums = lax.psum((acc_attn_bias, acc_up_bias), "dp")
    block_out = jnp.concatenate(block_parts, axis=1)
    input_grad = jnp.concatenate(input_parts, axis=1)
    return (
        block_out,
        input_grad,
        owned[4],
        owned[5],
        owned[0],
        bias_sums[0],
        owned[1],
        owned[6],
        owned[7],
        owned[8],
        owned[2],
        bias_sums[1],
        owned[3],
        owned[9],
    )

MESH = pl.DeviceIdType.MESH
F32 = jnp.float32
BF16 = jnp.bfloat16
TILES = 12
T = 4
NP = 4
ROWS = D // (2 * NP)
COLS = D // T
VROWS = 32


def place():
    d = lax.axis_index("dp")
    t = lax.axis_index("tensor")
    c = lax.rem(d, 2)
    p = d // 2
    px = p + 1 - 2 * lax.rem(p, 2)
    py = p + 2 - 4 * (p // 2)
    return d, t, c, p, px, py, 3 - p


def greet(d, t, c, p, px, py):
    barrier = pltpu.get_barrier_semaphore()
    me = c * T + t
    for step in range(1, 2 * T):
        other = lax.rem(me + step, 2 * T)
        pl.semaphore_signal(
            barrier, inc=1, device_id=(2 * p + other // T, lax.rem(other, T)), device_id_type=MESH
        )
    for q in (px, py):
        pl.semaphore_signal(barrier, inc=1, device_id=(2 * q + c, t), device_id_type=MESH)
    pl.semaphore_wait(barrier, 2 * T + 1)


def remote(src, dst, send, recv, device):
    return pltpu.make_async_remote_copy(
        src_ref=src,
        dst_ref=dst,
        send_sem=send,
        recv_sem=recv,
        device_id=device,
        device_id_type=MESH,
    )


class Exchange:
    def __init__(self, src, dst, send, recv, spot, full):
        d, t, c, p, px, py, pd = spot
        self.c, self.t, self.p = c, t, p
        self.src, self.dst, self.send, self.recv = src, dst, send, recv
        self.full = full

    def slot_out(self):
        return self.t if self.full else lax.rem(self.t, 2)

    def slot_in(self, k):
        return 2 * self.c + k if self.full else k

    def mine(self, k):
        return jnp.logical_and(self.t // 2 == self.c, lax.rem(self.t, 2) == k)

    def copy(self, k):
        return remote(
            self.src.at[k],
            self.dst.at[self.slot_out()],
            self.send.at[k],
            self.recv.at[lax.rem(self.t, 2)],
            (2 * self.p + self.t // 2, 2 * self.c + k),
        )

    def local(self, k):
        return pltpu.make_async_copy(
            self.src.at[k], self.dst.at[self.slot_out()], self.send.at[k]
        )

    def start(self):
        for k in range(2):

            @pl.when(self.mine(k))
            def _():
                self.local(k).start()

            @pl.when(jnp.logical_not(self.mine(k)))
            def _():
                self.copy(k).start()

    def wait_in(self, k):
        @pl.when(self.mine(k))
        def _():
            self.local(k).wait()

        @pl.when(jnp.logical_not(self.mine(k)))
        def _():
            remote(
                self.src.at[k],
                self.dst.at[self.slot_in(k)],
                self.send.at[k],
                self.recv.at[k],
                (2 * self.p + self.t // 2, 2 * self.c + k),
            ).wait_recv()

    def wait_out(self, k):
        @pl.when(jnp.logical_not(self.mine(k)))
        def _():
            self.copy(k).wait_send()


OWN = (0,)
REST = (1, 2)


class Gather:
    kinds = OWN + REST

    def __init__(self, src, dst, sems, j, spot):
        self.d, self.t, self.c, self.p, self.px, self.py, self.pd = spot
        self.src, self.dst, self.j = src, dst, j
        self.zin, self.zout, self.own_sem, self.rin, self.rout, self.cin, self.cout = sems
        self.half = src.shape[0] // 2
        self.width = src.shape[1]

    def row(self, q):
        return self.dst.at[q, self.c]

    def cell(self, tau):
        start = pl.multiple_of(tau * self.width, self.width)
        return self.dst.at[self.p, self.c, :, pl.ds(start, self.width)]

    def local(self):
        return pltpu.make_async_copy(self.src, self.cell(self.t), self.own_sem.at[self.j])

    def line(self, tau, way, k):
        src = self.src if k == 0 else self.cell(tau)
        return remote(
            src,
            self.cell(tau),
            self.zout.at[self.j, way, k],
            self.zin.at[self.j, tau],
            (self.d, self.t + (1 if way == 0 else -1)),
        )

    def own(self):
        self.local().start()

        @pl.when(self.t < T - 1)
        def _():
            self.line(self.t, 0, 0).start()

        @pl.when(self.t > 0)
        def _():
            self.line(self.t, 1, 0).start()

    def near_own(self):
        self.spread(OWN, self.near)

    def hop(self, k):
        t = self.t

        @pl.when(t >= k)
        def _():
            self.line(t - k, 0, k).wait_recv()

            @pl.when(t < T - 1)
            def _():
                self.line(t - k, 0, k).start()

        @pl.when(t + k < T)
        def _():
            self.line(t + k, 1, k).wait_recv()

            @pl.when(t > 0)
            def _():
                self.line(t + k, 1, k).start()

    def side(self, way):
        q = self.px if way == 0 else self.py
        return (2 * q + self.c, self.t)

    def spread(self, kinds, make, act="start"):
        for place_z in range(T):

            @pl.when(self.t == place_z)
            def _():
                for kind in kinds:
                    first, last = ((place_z, place_z + 1), (0, place_z), (place_z + 1, T))[kind]
                    if first < last:
                        for way in range(2):
                            getattr(make(way, kind, first, last), act)()

    def piece(self, q, first, last):
        return self.dst.at[q, self.c, :, pl.ds(first * self.width, (last - first) * self.width)]

    def near(self, way, kind, first, last):
        part = self.piece(self.p, first, last)
        return remote(
            self.src if kind == 0 else part,
            part,
            self.rout.at[self.j, 2 * kind + way],
            self.rin.at[self.j, 2 * kind + way],
            self.side(way),
        )

    def near_in(self, way, kind, first, last):
        part = self.piece(self.px if way == 0 else self.py, first, last)
        sem = self.rin.at[self.j, 2 * kind + way]
        return remote(part, part, self.rout.at[self.j, 2 * kind + way], sem, self.side(way))

    def passed(self, q, way, kind, first, last):
        part = self.piece(q, first, last).at[pl.ds(way * self.half, self.half)]
        at = 6 + 2 * kind + way
        return remote(
            part, part, self.rout.at[self.j, at], self.rin.at[self.j, at], self.side(1 - way)
        )

    def far(self, way, kind, first, last):
        return self.passed(self.px if way == 0 else self.py, way, kind, first, last)

    def far_in(self, way, kind, first, last):
        return self.passed(self.pd, way, kind, first, last)

    def near_rest(self):
        self.spread(REST, self.near)

    def far_own(self):
        self.spread(OWN, self.near_in, "wait_recv")
        self.spread(OWN, self.far)

    def far_rest(self):
        self.spread(REST, self.near_in, "wait_recv")
        self.spread(REST, self.far)

    def pair(self, c):
        return remote(
            self.dst.at[:, c],
            self.dst.at[:, c],
            self.cout.at[self.j],
            self.cin.at[self.j],
            (2 * self.p + 1 - self.c, self.t),
        )

    def cross(self):
        self.local().wait()
        self.spread(OWN + REST, self.far_in, "wait_recv")
        self.pair(self.c).start()

    def ready(self):
        self.pair(1 - self.c).wait_recv()

    def finish(self):
        t = self.t
        for k in range(T):

            @pl.when(jnp.logical_and(t >= k, t < T - 1))
            def _():
                self.line(t - k, 0, k).wait_send()

            @pl.when(jnp.logical_and(t + k < T, t > 0))
            def _():
                self.line(t + k, 1, k).wait_send()

        self.spread(self.kinds, self.near, "wait_send")
        self.spread(self.kinds, self.far, "wait_send")
        self.pair(self.c).wait_send()


class GatherFlip(Gather):
    kinds = OWN

    def column(self, tau):
        start = pl.multiple_of(tau * self.width, self.width)
        return self.dst.at[:, self.c, :, pl.ds(start, self.width)]

    def line(self, tau, way, k):
        part = self.column(tau)
        return remote(
            part,
            part,
            self.zout.at[self.j, way, k],
            self.zin.at[self.j, tau],
            (self.d, self.t + (1 if way == 0 else -1)),
        )

    def own(self):
        self.local().start()
        self.spread(OWN, self.near)

    def line_own(self):
        self.local().wait()
        self.spread(OWN, self.far_in, "wait_recv")

        @pl.when(self.t < T - 1)
        def _():
            self.line(self.t, 0, 0).start()

        @pl.when(self.t > 0)
        def _():
            self.line(self.t, 1, 0).start()

    def cross(self):
        self.pair(self.c).start()


LAGS = (1, 2, 3, -3, 5, 7)
LEAD = 5
ORDER = (0, 1, 2, 3, 4, 8, 5, 9, 6, 10, 11)
FLIPPED = 7
FLIP_STEPS = (0, 1, 8, 10, 12, 14, 15)
SWAP_STEPS = (4, 8, 13)
QUARTERS = 4
TILE = 256


def tiles(n, size, body):
    def run(i, carry):
        body(pl.ds(pl.multiple_of(i * size, size), size), i)
        return carry

    lax.fori_loop(0, n // size, run, 0)


def to_lanes(a):
    return a.astype(F32).T.astype(BF16)


def matrix(w, j, cols=None):
    a = w[j] if cols is None else w[j, :, :, :, cols]
    return a.reshape(D, a.shape[-1])


def matrix_rows(w, j, n):
    return w[j, n].reshape(2 * ROWS, D)


def forward_kernel(
    w, v, x, cot, valid,
    o_w, o_vec, o_x, o_cot, o_bias, o_q, o_k, o_v, o_att, o_nt, o_n2t, o_mgt, o_hid, o_pre,
    o_n2g, o_resid, o_blk, o_ups,
    gw, gv, xf, cf, mf, vec, bias, normed, q_s, k_s, v_s, att, resid, n2, nt, n2t, mgt, hid, pre,
    n2g, mlp, slope, blk, ups,
    ex_sem, mask_sem, pass_sem, out_sem, *chunk_sems,
):
    spot = place()
    d, t, c, p, px, py, pd = spot
    greet(d, t, c, p, px, py)
    partner = (2 * p + 1 - c, t)
    swap_x = Exchange(x, xf, ex_sem.at[0], ex_sem.at[1], spot, True)
    swap_c = Exchange(cot, cf, ex_sem.at[2], ex_sem.at[3], spot, False)
    mask_out = remote(valid, mf.at[c], mask_sem.at[0], mask_sem.at[1], partner)
    mask_in = remote(valid, mf.at[1 - c], mask_sem.at[0], mask_sem.at[1], partner)
    mask_own = pltpu.make_async_copy(valid, mf.at[c], mask_sem.at[2])

    def passed(core, k):
        view = xf.at[2 * core + k]
        return remote(view, view, pass_sem.at[0, k], pass_sem.at[1, k], partner)

    chunks = [Gather(v, gv, chunk_sems, 0, spot)]
    for i, j in enumerate(ORDER):
        chunks.append(Gather(w.at[j], gw.at[j], chunk_sems, i + 1, spot))
    count = len(chunks)
    flipped = GatherFlip(w.at[FLIPPED], gw.at[FLIPPED], chunk_sems, count, spot)
    flip_work = (
        flipped.own,
        flipped.far_own,
        flipped.line_own,
        lambda: flipped.hop(1),
        lambda: flipped.hop(2),
        lambda: flipped.hop(3),
        flipped.cross,
    )

    def comm(s):
        for lag, stage in (
            (LAGS[5], lambda g: g.cross()),
            (LAGS[4], lambda g: g.far_rest()),
            (LAGS[2], lambda g: (g.hop(3), g.near_rest())),
            (LAGS[1], lambda g: g.hop(2)),
            (LAGS[0], lambda g: g.hop(1)),
            (0, lambda g: g.own()),
        ):
            if 0 <= s - lag < count:
                stage(chunks[s - lag])
        for i in range(count):
            if s == max(0, i - LEAD):
                chunks[i].near_own()
            if s == max(1, i + LAGS[3]):
                chunks[i].far_own()
        for at, work in zip(FLIP_STEPS, flip_work):
            if at == s:
                work()
        if s == SWAP_STEPS[0]:
            swap_x.start()
            mask_out.start()
            mask_own.start()
        if s == SWAP_STEPS[1]:
            for k in range(2):
                swap_x.wait_in(k)
                passed(c, k).start()
        if s == SWAP_STEPS[2]:
            swap_c.start()

    nq = q_s.shape[0]
    nk = k_s.shape[0]
    block = xf.shape[1]
    own_rows = pl.ds(pl.multiple_of(c * nq, nq), nq)
    copies = []

    def emit(src, dst):
        copy = pltpu.make_async_copy(src, dst, out_sem.at[len(copies)])
        copy.start()
        copies.append(copy)

    def vectors():
        for q in range(NP):
            for core in range(2):
                part = gv[q, core].astype(F32)
                first = (2 * q + core) * ROWS
                vec[0:6, first : first + ROWS] = part[0:6, 0:ROWS]
        part = gv[0, 0].astype(F32)
        per = COLS // 128
        for i in range(2 + QUARTERS):
            for tau in range(T):
                for r in range(per):
                    row = 6 + i * per + r
                    at = tau * COLS + r * 128
                    vec[6 + i : 7 + i, at : at + 128] = part[row : row + 1, tau * 128 : tau * 128 + 128]
        emit(vec, o_vec)
        mask_in.wait_recv()
        mask_own.wait()
        rows = mf[t // 2].T
        col = jnp.where(lax.rem(t, 2) == 0, rows[:, 0:1], rows[:, 1:2])
        bias[...] = jnp.where(col > 0, 0.0, NEG).astype(F32)
        emit(bias, o_bias)

    def norm_one():
        for k in range(2):
            passed(1 - c, k).wait_recv()
        emit(xf.at[pl.ds(2 * c, 2)], o_x)
        size = 32
        per = block // size

        def run(i, carry):
            at = pl.ds(pl.multiple_of(lax.rem(i, per) * size, size), size)
            unit, unused = norm_parts(xf[i // per, at].astype(F32))
            normed[pl.ds(pl.multiple_of(i * size, size), size)] = (
                unit * vec[0:1] + vec[1:2]
            ).astype(BF16)
            return carry

        lax.fori_loop(0, nk // size, run, 0)

        def flip(cols, i):
            nt[cols] = to_lanes(normed[own_rows, cols])

        tiles(D, TILE, flip)
        emit(nt, o_nt)

    def project(j, dst, rows, shift):
        a = normed[rows]

        def run(cols, i):
            out = jnp.dot(a, matrix(gw, j, cols), preferred_element_type=F32)
            if shift is not None:
                out = out + vec[shift : shift + 1, cols]
            dst[:, cols] = out.astype(BF16)

        tiles(D, TILE, run)

    def heads(first, last):
        def run(i, carry):
            cols = pl.ds(pl.multiple_of(i * 2 * HD, 2 * HD), 2 * HD)
            q_t = (q_s[:, cols].astype(F32).T * HD ** (-0.5)).astype(BF16)
            v_t = to_lanes(v_s[:, cols])
            k = k_s[:, cols]
            parts = []
            for h in range(2):
                probs = head_probs(k, head_rows(q_t, h), bias[...]).astype(BF16)
                parts.append(
                    jnp.dot(v_t[h * HD : (h + 1) * HD], probs, preferred_element_type=F32)
                )
            att[:, cols] = jnp.concatenate(parts, axis=0).T.astype(BF16)
            return carry

        lax.fori_loop(first, last, run, 0)

    def middle():
        emit(att, o_att)
        a = att[...]
        x_own = xf.at[pl.ds(2 * c, 2)]

        def run(cols, i):
            out = dot_nt(a, matrix_rows(gw, 3, i))
            resid[:, cols] = (
                x_own[:, :, cols].astype(F32).reshape(nq, TILE) + out + vec[2:3, cols]
            )

        tiles(D, TILE, run)
        emit(resid, o_resid)

        def norm(rows, i):
            unit, unused = norm_parts(resid[rows])
            n2[rows] = (unit * vec[3:4] + vec[4:5]).astype(BF16)

        tiles(nq, 64, norm)

        def flip(cols, i):
            n2t[cols] = to_lanes(n2[:, cols])

        tiles(D, TILE, flip)
        emit(n2t, o_n2t)

    def grads_in():
        for k in range(2):
            swap_c.wait_in(k)
        emit(cf, o_cot)

        def flip(cols, i):
            mgt[cols] = to_lanes(cf[:, :, cols].reshape(nq, TILE))

        tiles(D, TILE, flip)
        emit(mgt, o_mgt)

    def quarter_up(j):
        a = n2[...]

        def run(cols, i):
            z = jnp.dot(a, matrix(gw, 4 + j, cols), preferred_element_type=F32)
            z = z + vec[8 + j : 9 + j, cols]
            share = 0.5 + 0.5 * lax.erf(z * 0.5**0.5)
            hid[j, :, cols] = (z * share).astype(BF16)
            slope[:, cols] = share + z * (jnp.exp(-0.5 * z * z) * (0.5 / jnp.pi) ** 0.5)

        tiles(D, TILE, run)
        emit(hid.at[j], o_hid.at[j])

    def quarter_down(j):
        g = cf[...].reshape(nq, D)

        def back(cols, i):
            h = jnp.dot(g, matrix(gw, 8 + j, cols), preferred_element_type=F32)
            grad = (slope[:, cols] * h).astype(BF16)
            pre[j, :, cols] = grad
            ups[j : j + 1, cols] = jnp.sum(grad.astype(F32), axis=0, keepdims=True)

        tiles(D, TILE, back)
        emit(pre.at[j], o_pre.at[j])

        def outs(cols, i):
            m = dot_nt(hid[j], matrix_rows(gw, 8 + j, i))
            n = dot_nt(pre[j], matrix_rows(gw, 4 + j, i))
            if j == 0:
                mlp[:, cols] = m
                n2g[:, cols] = n
            elif j < QUARTERS - 1:
                mlp[:, cols] += m
                n2g[:, cols] += n
            else:
                n2g[:, cols] += n
                blk[:, cols] = (resid[:, cols] + mlp[:, cols] + m + vec[5:6, cols]).astype(BF16)

        tiles(D, TILE, outs)

    whole = pl.ds(0, nk)
    after = {
        8: (vectors, norm_one),
        9: (lambda: project(0, q_s, own_rows, 6), lambda: emit(q_s, o_q)),
        10: (lambda: project(1, k_s, whole, None), lambda: emit(k_s, o_k)),
        11: (lambda: project(2, v_s, whole, 7), lambda: emit(v_s, o_v), lambda: heads(0, 2)),
        12: (lambda: heads(2, 6),),
        13: (lambda: heads(6, 8), middle),
        14: (lambda: quarter_up(0), grads_in, lambda: quarter_down(0)),
        15: (lambda: quarter_up(1),),
        16: (lambda: quarter_down(1),),
        17: (lambda: quarter_up(2),),
        18: (lambda: quarter_down(2), flipped.ready, flipped.finish, lambda: quarter_up(3)),
        19: (lambda: quarter_down(3),),
    }
    lag = LAGS[5] + 1
    for s in range(count + lag):
        comm(s)
        if 0 <= s - lag < count:
            i = s - lag
            chunks[i].ready()
            if 1 <= i <= 4:
                emit(gw.at[ORDER[i - 1]], o_w.at[ORDER[i - 1]])
        for unit in after.get(s, ()):
            unit()
        if 0 <= s - lag - 1 < count:
            chunks[s - lag - 1].finish()
    emit(n2g, o_n2g)
    emit(blk, o_blk)
    emit(ups, o_ups)
    chunks[-1].finish()
    for k in range(2):
        passed(c, k).wait_send()
        swap_x.wait_out(k)
        swap_c.wait_out(k)
    mask_out.wait_send()
    for copy in copies:
        copy.wait()


def forward_all(w, v, x, cot, valid):
    any_space = pl.BlockSpec(memory_space=pl.ANY)
    dma = pltpu.SemaphoreType.DMA
    n = TILES + 1
    block = x.shape[1]
    nk = T * block
    nq = nk // 2
    gathered = (NP, 2, ROWS, D)

    def half(rows, cols=D):
        return (rows, cols), BF16

    outs = (
        ((4,) + gathered, BF16),
        ((16, D), F32),
        ((2, block, D), BF16),
        ((2, block, D), BF16),
        ((nk, 1), F32),
        half(nq),
        half(nk),
        half(nk),
        half(nq),
        half(D, nq),
        half(D, nq),
        half(D, nq),
        ((QUARTERS, nq, D), BF16),
        ((QUARTERS, nq, D), BF16),
        ((nq, D), F32),
        ((nq, D), F32),
        half(nq),
        ((8, D), F32),
    )
    scratch = (
        ((TILES,) + gathered, BF16),
        ((NP, 2, VROWS, 128 * T), BF16),
        ((T, block, D), BF16),
        ((2, block, D), BF16),
        ((2,) + valid.shape, F32),
        ((16, D), F32),
        ((nk, 1), F32),
        half(nk),
        half(nq),
        half(nk),
        half(nk),
        half(nq),
        ((nq, D), F32),
        half(nq),
        half(D, nq),
        half(D, nq),
        half(D, nq),
        ((QUARTERS, nq, D), BF16),
        ((QUARTERS, nq, D), BF16),
        ((nq, D), F32),
        ((nq, D), F32),
        ((nq, D), F32),
        half(nq),
        ((8, D), F32),
    )
    return pl.pallas_call(
        forward_kernel,
        out_shape=[jax.ShapeDtypeStruct(*o) for o in outs],
        in_specs=[any_space] * 5,
        out_specs=[any_space] * len(outs),
        scratch_shapes=[pltpu.VMEM(*o) for o in scratch]
        + [
            dma((4, 2)),
            dma((3,)),
            dma((2, 2)),
            dma((32,)),
            dma((n, T)),
            dma((n, 2, T)),
            dma((n,)),
            dma((n, 12)),
            dma((n, 12)),
            dma((n,)),
            dma((n,)),
        ],
        name="forward_all",
        compiler_params=pltpu.CompilerParams(
            collective_id=0, has_side_effects=True, vmem_limit_bytes=60 << 20
        ),
    )(w, v, x, cot, valid)


STAGES = (0, 1, 3, 4)
SEQUENCE = (8, 9, 5, 10, 6, 11, 7, 3, 0, 2, 1, 4)
CHAIN = TILES - 1
SLOTS = 5


def backward_kernel(
    i_w, i_vec, i_x, i_cot, i_bias, i_q, i_k, i_v, i_att, i_nt, i_n2t, i_mgt, i_hid, i_pre,
    i_n2g, i_resid, blk, i_ups,
    out, vec_out, own_blk, own_ig,
    vec, x, cot, bias, q_s, k_s, v_s, att, at, hid, pre, grad, resid, wb, branch, att_g,
    dq, dk, dv, came, ig, sums,
    stage, held, far_in, near_in, line_in, vec_held, vec_in, flip_line, flip_far, flip_near, flip_sum,
    load_sem, swap_sem, pair_out, pair_in, far_sem, near_sem, line_sem, vec_sem, ex_sem,
):
    spot = place()
    d, t, c, p, px, py, pd = spot
    loads = {}

    def load(name, src, dst):
        copy = pltpu.make_async_copy(src, dst, load_sem.at[len(loads)])
        copy.start()
        loads[name] = copy

    load("mgt", i_mgt, at.at[3])
    load("hid0", i_hid.at[0], hid.at[0])
    load("n2t", i_n2t, at.at[2])
    load("pre0", i_pre.at[0], pre.at[0])
    load("vec", i_vec, vec)
    load("resid", i_resid, resid)
    load("grad", i_n2g, grad)
    load("cot", i_cot, cot)
    load("wp", i_w.at[3], wb.at[0])
    load("hid1", i_hid.at[1], hid.at[1])
    load("pre1", i_pre.at[1], pre.at[1])
    load("q", i_q, q_s)
    load("k", i_k, k_s)
    load("v", i_v, v_s)
    load("bias", i_bias, bias)
    load("wk", i_w.at[1], wb.at[1])
    load("hid2", i_hid.at[2], hid.at[2])
    load("pre2", i_pre.at[2], pre.at[2])
    load("hid3", i_hid.at[3], hid.at[3])
    load("pre3", i_pre.at[3], pre.at[3])
    load("att", i_att, att)
    load("nt", i_nt, at.at[0])
    load("x", i_x, x)
    load("ups", i_ups, sums.at[pl.ds(8, 8)])

    greet(d, t, c, p, px, py)
    partner = (2 * p + 1 - c, t)
    side = ((2 * px + c, t), (2 * py + c, t))
    swap_b = Exchange(blk, own_blk, ex_sem.at[0], ex_sem.at[1], spot, False)
    swap_i = Exchange(ig, own_ig, ex_sem.at[2], ex_sem.at[3], spot, False)
    half = ROWS // 2
    nq = resid.shape[0]
    own_rows = pl.ds(pl.multiple_of(c * nq, nq), nq)
    other_rows = pl.ds(pl.multiple_of((1 - c) * nq, nq), nq)

    def slot(j):
        return j % SLOTS

    def outgoing(j):
        return stage.at[j % 2] if j < CHAIN else near_in.at[pl.ds(6, NP)]

    def pair(j):
        return remote(
            outgoing(j), held.at[j], pair_out.at[j % 2 if j < CHAIN else 2], pair_in.at[j], partner
        )

    def far(j, way):
        return remote(
            held.at[j, pd, pl.ds(way * half, half)],
            far_in.at[slot(j), way],
            far_sem.at[0, j, way],
            far_sem.at[1, j, way],
            side[way],
        )

    def near(j, way):
        return remote(
            held.at[j, (px, py)[way]],
            near_in.at[2 * slot(j) + way],
            near_sem.at[0, j, way],
            near_sem.at[1, j, way],
            side[way],
        )

    def line(j, tau, way):
        return remote(
            held.at[j, p, :, pl.ds(tau * COLS, COLS)],
            line_in.at[j, tau + 1 - way],
            line_sem.at[0, j, tau + 1 - way],
            line_sem.at[1, j, tau + 1 - way],
            (d, t + (1 if way == 0 else -1)),
        )

    vec_partners = (
        partner,
        side[0],
        side[1],
        (d, t + 1 - 2 * lax.rem(t, 2)),
        (d, t + 2 - 4 * (t // 2)),
    )

    def vec_copy(r):
        return remote(vec_held.at[r], vec_in.at[r], vec_sem.at[0, r], vec_sem.at[1, r], vec_partners[r])

    def factors(j):
        m = SEQUENCE[j]
        if m >= 8:
            return at.at[3], hid.at[m - 8]
        if m >= 4:
            return at.at[2], pre.at[m - 4]
        if m == 3:
            return at.at[1], att
        return at.at[0], (dq, dk.at[own_rows], dv.at[own_rows])[m]

    waits = {
        0: ("mgt", "hid0"), 1: ("hid1",), 2: ("pre1",), 3: ("hid2",), 4: ("pre2",), 5: ("hid3",),
        6: ("pre3",), 7: ("att",), 8: ("nt",), CHAIN: ("n2t", "pre0"),
    }

    def product(j, q, core):
        a, b = factors(j)
        rows = pl.ds(pl.multiple_of((2 * q + core) * ROWS, ROWS), ROWS)
        return jnp.dot(a[rows], b[...], preferred_element_type=F32)

    def each_chip(body):
        def run(q, carry):
            body(q)
            return carry

        lax.fori_loop(0, NP, run, 0)

    def first(j):
        for name in waits.get(j, ()):
            loads[name].wait()
        if 2 <= j < CHAIN:
            pair(j - 2).wait_send()

        def make(q):
            outgoing(j)[q] = product(j, q, 1 - c).astype(BF16)

        each_chip(make)
        pair(j).start()

    def second(j):
        pair(j).wait_recv()

        def make(q):
            held[j, q] = (product(j, q, c) + held[j, q].astype(F32)).astype(BF16)

        each_chip(make)
        if j < CHAIN:
            for way in range(2):
                far(j, way).start()

    def third(j):
        for way in range(2):
            far(j, way).wait_recv()
            part = pl.ds(way * half, half)
            q = (py, px)[way]
            held[j, q, part] = (
                held[j, q, part].astype(F32) + far_in[slot(j), way].astype(F32)
            ).astype(BF16)
            near(j, 1 - way).start()

    def fourth(j):
        near(j, 0).wait_recv()
        near(j, 1).wait_recv()
        for tau in range(T):
            cols = pl.ds(tau * COLS, COLS)
            total = (
                held[j, p, :, cols].astype(F32)
                + near_in[2 * slot(j), :, cols].astype(F32)
                + near_in[2 * slot(j) + 1, :, cols].astype(F32)
            )
            held[j, p, :, cols] = total.astype(BF16)

            @pl.when(t == tau)
            def _():
                out[j] = total

    def lines(s):
        for way in range(2):
            hop = t if way == 0 else T - 1 - t
            j = s - STAGES[3] - hop

            @pl.when(jnp.logical_and(j >= 0, j < CHAIN))
            def _():
                for tau in range(T) if way else reversed(range(T)):

                    @pl.when((tau > t) if way == 0 else (tau < t))
                    def _():
                        cols = pl.ds(tau * COLS, COLS)

                        @pl.when(hop > 0)
                        def _():
                            line(j, tau, way).wait_recv()
                            held[j, p, :, cols] = (
                                held[j, p, :, cols].astype(F32)
                                + line_in[j, tau + 1 - way].astype(F32)
                            ).astype(BF16)

                        line(j, tau, way).start()

    def last(j):
        for way in range(2):

            @pl.when((t > 0) if way == 0 else (t < T - 1))
            def _():
                for tau in range(T):

                    @pl.when(t == tau)
                    def _():
                        line(j, tau, way).wait_recv()
                        out[j] += line_in[j, tau + 1 - way].astype(F32)

    def drain(j):
        for way in range(2):
            far(j, way).wait_send()
            near(j, way).wait_send()
            for tau in range(T):

                @pl.when((tau > t) if way == 0 else (tau < t))
                def _():
                    line(j, tau, way).wait_send()

    def flip_copy(tau, way):
        part = held.at[CHAIN, :, :, pl.ds(tau * COLS, COLS)]
        at = tau + 1 - way
        return remote(
            part,
            flip_line.at[at],
            line_sem.at[0, CHAIN, at],
            line_sem.at[1, CHAIN, at],
            (d, t + (1 if way == 0 else -1)),
        )

    def flip_hop(hop):
        for way in range(2):
            for place_z in range(T):

                @pl.when(jnp.logical_and(t == place_z, hop == (t if way == 0 else T - 1 - t)))
                def _():
                    for tau in range(T) if way else reversed(range(T)):
                        if (tau < place_z) if way else (tau > place_z):
                            if hop > 0:
                                cols = pl.ds(tau * COLS, COLS)
                                flip_copy(tau, way).wait_recv()
                                held[CHAIN, :, :, cols] = (
                                    held[CHAIN, :, :, cols].astype(F32)
                                    + flip_line[tau + 1 - way].astype(F32)
                                ).astype(BF16)
                            flip_copy(tau, way).start()

    def flip_send(kind, way):
        if kind == 0:
            src = flip_sum.at[pd, pl.ds(way * half, half)]
            return remote(
                src, flip_far.at[way], far_sem.at[0, CHAIN, way], far_sem.at[1, CHAIN, way], side[way]
            )
        return remote(
            flip_sum.at[(px, py)[way]],
            flip_near.at[way],
            near_sem.at[0, CHAIN, way],
            near_sem.at[1, CHAIN, way],
            side[way],
        )

    def flip_join():
        for place_z in range(T):

            @pl.when(t == place_z)
            def _():
                total = held[CHAIN, :, :, pl.ds(place_z * COLS, COLS)].astype(F32)
                for way in range(2):
                    if place_z != (0, T - 1)[way]:
                        flip_copy(place_z, way).wait_recv()
                        total = total + flip_line[place_z + 1 - way].astype(F32)
                flip_sum[...] = total.astype(BF16)

        for way in range(2):
            flip_send(0, way).start()

    def flip_ring():
        for way in range(2):
            flip_send(0, way).wait_recv()
            part = pl.ds(way * half, half)
            q = (py, px)[way]
            flip_sum[q, part] = (
                flip_sum[q, part].astype(F32) + flip_far[way].astype(F32)
            ).astype(BF16)
            flip_send(1, 1 - way).start()

    def flip_last():
        for way in range(2):
            flip_send(1, way).wait_recv()
        out[CHAIN] = (
            flip_sum[p].astype(F32) + flip_near[0].astype(F32) + flip_near[1].astype(F32)
        )
        for way in range(2):
            flip_send(0, way).wait_send()
            flip_send(1, way).wait_send()
            for tau in range(T):

                @pl.when((tau > t) if way == 0 else (tau < t))
                def _():
                    flip_copy(tau, way).wait_send()

    def comm(s):
        for lag, work in ((STAGES[0], second), (STAGES[1], third), (STAGES[2], fourth)):
            if 0 <= s - lag < CHAIN:
                work(s - lag)
        if STAGES[3] <= s < CHAIN + STAGES[3] + T - 1:
            lines(s)
        if 0 <= s - STAGES[3] - T < CHAIN:
            last(s - STAGES[3] - T)
            drain(s - STAGES[3] - T)

    def add(row, a):
        sums[row : row + 1] += jnp.sum(a, axis=0, keepdims=True)

    def mid_back():
        for name in ("vec", "resid", "grad", "cot", "ups"):
            loads[name].wait()
        sums[0:8] = jnp.zeros((8, D), F32)

        def run(rows, i):
            unit, inverse = norm_parts(resid[rows])
            g = grad[rows]
            outer = cot[rows].astype(F32)
            total = outer + norm_back(g, unit, inverse, vec[3:4])
            resid[rows] = total
            low = total.astype(BF16)
            branch[rows] = low
            add(2, low.astype(F32))
            add(3, g * unit)
            add(4, g)
            add(5, outer)

        tiles(nq, 64, run)

    def att_back():
        loads["wp"].wait()
        a = branch[...]

        def run(cols, i):
            at[1, cols] = to_lanes(branch[:, cols])
            att_g[:, cols] = jnp.dot(a, matrix(wb, 0, cols), preferred_element_type=F32).astype(BF16)

        tiles(D, TILE, run)
        load("wq", i_w.at[0], wb.at[0])

    def heads(first_pair, last_pair):
        if first_pair == 0:
            for name in ("q", "k", "v", "bias"):
                loads[name].wait()

        def run(i, carry):
            cols = pl.ds(pl.multiple_of(i * 2 * HD, 2 * HD), 2 * HD)
            k, v, g = k_s[:, cols], v_s[:, cols], att_g[:, cols]
            q_f = q_s[:, cols].astype(F32) * HD ** (-0.5)
            q_l = q_f.astype(BF16)
            q_t = q_f.T.astype(BF16)
            g_t = to_lanes(g)
            k_t = to_lanes(k)
            parts, dk_parts, dv_parts = [], [], []
            for h in range(2):
                probs = head_probs(k, head_rows(q_t, h), bias[...])
                dv_parts.append(
                    jnp.dot(probs.astype(BF16), head_lanes(g, h), preferred_element_type=F32)
                )
                dp = jnp.dot(v, head_rows(g_t, h), preferred_element_type=F32)
                ds = (probs * (dp - jnp.sum(dp * probs, axis=0, keepdims=True))).astype(BF16)
                parts.append(jnp.dot(k_t[h * HD : (h + 1) * HD], ds, preferred_element_type=F32))
                dk_parts.append(jnp.dot(ds, head_lanes(q_l, h), preferred_element_type=F32))
            dq[:, cols] = (jnp.concatenate(parts, axis=0).T * HD ** (-0.5)).astype(BF16)
            dk[:, cols] = (dk_parts[0] + dk_parts[1]).astype(BF16)
            dv[:, cols] = (dv_parts[0] + dv_parts[1]).astype(BF16)
            return carry

        lax.fori_loop(first_pair, last_pair, run, 0)

    def pass_on(i):
        src = (dk, dv)[i].at[other_rows]
        return remote(src, came.at[i], swap_sem.at[0, i], swap_sem.at[1, i], partner)

    def query_back():
        pass_on(0).start()
        pass_on(1).start()
        loads["wq"].wait()
        a = dq[...]

        def run(cols, i):
            grad[:, cols] = dot_nt(a, matrix_rows(wb, 0, i))
            sums[6:7, cols] = jnp.sum(dq[:, cols].astype(F32), axis=0, keepdims=True)

        tiles(D, TILE, run)
        load("wv", i_w.at[2], wb.at[0])

    def key_back():
        for i, ref in enumerate((dk, dv)):
            pass_on(i).wait_recv()

            def join(cols, n):
                total = (ref[own_rows, cols].astype(F32) + came[i, :, cols].astype(F32)).astype(BF16)
                ref[own_rows, cols] = total
                if i == 1:
                    sums[7:8, cols] = jnp.sum(total.astype(F32), axis=0, keepdims=True)

            tiles(D, TILE, join)
        loads["wk"].wait()
        loads["wv"].wait()
        a, b = dk[own_rows], dv[own_rows]

        def run(cols, i):
            grad[:, cols] += dot_nt(a, matrix_rows(wb, 1, i)) + dot_nt(b, matrix_rows(wb, 0, i))

        tiles(D, TILE, run)

    def front_back():
        loads["x"].wait()
        size = 32
        per = ig.shape[1] // size

        def run(rows, i):
            unit, inverse = norm_parts(x[rows].astype(F32))
            g = grad[rows]
            add(0, g * unit)
            add(1, g)
            total = resid[rows] + norm_back(g, unit, inverse, vec[0:1])
            ig[i // per, pl.ds(pl.multiple_of(lax.rem(i, per) * size, size), size)] = total.astype(BF16)

        tiles(nq, size, run)
        swap_i.start()
        vec_held[0] = sums[...]
        vec_copy(0).start()

    def vec_round(r):
        vec_copy(r).wait_recv()
        vec_held[r + 1] = vec_held[r] + vec_in[r]
        if r < 4:
            vec_copy(r + 1).start()
        else:
            vec_out[...] = vec_held[5]

    def flip_start():
        pair(CHAIN).wait_send()
        second(CHAIN)
        flip_hop(0)

    between = {
        0: (lambda: first(CHAIN),),
        1: (flip_start,),
        2: (att_back, lambda: heads(0, 1)),
        3: (lambda: heads(1, 2),),
        4: (lambda: heads(2, 3),),
        5: (lambda: heads(3, 4),),
        6: (lambda: heads(4, 6),),
        7: (lambda: heads(6, 8), query_back),
        8: (key_back,),
        9: (front_back,),
    }
    after = {
        1: (mid_back,),
        3: (lambda: flip_hop(1), swap_b.start),
        5: (lambda: flip_hop(2),),
        7: (lambda: flip_hop(3),),
        9: (flip_join,),
        10: (flip_ring,),
        11: (lambda: vec_round(0),),
        12: (flip_last, lambda: vec_round(1)),
        13: (lambda: vec_round(2),),
        14: (lambda: vec_round(3),),
        15: (lambda: vec_round(4),),
    }
    for s in range(CHAIN + STAGES[3] + T):
        if s < CHAIN:
            first(s)
        for unit in between.get(s, ()):
            unit()
        comm(s)
        for unit in after.get(s, ()):
            unit()
    for j in (CHAIN - 2, CHAIN - 1):
        pair(j).wait_send()
    for i in range(2):
        pass_on(i).wait_send()
    for r in range(5):
        vec_copy(r).wait_send()
    for swap in (swap_b, swap_i):
        for k in range(2):
            swap.wait_in(k)
            swap.wait_out(k)


def backward_all(*args):
    any_space = pl.BlockSpec(memory_space=pl.ANY)
    vmem = pl.BlockSpec(memory_space=pltpu.VMEM)
    dma = pltpu.SemaphoreType.DMA
    n = TILES
    blk, resid, bias = args[16], args[15], args[4]
    nq, nk = resid.shape[0], bias.shape[0]
    own = (nq, D)
    scratch = (
        ((16, D), F32),
        (own, BF16),
        (own, BF16),
        ((nk, 1), F32),
        (own, BF16),
        ((nk, D), BF16),
        ((nk, D), BF16),
        (own, BF16),
        ((4, D, nq), BF16),
        ((QUARTERS,) + own, BF16),
        ((QUARTERS,) + own, BF16),
        (own, F32),
        (own, F32),
        ((2, NP, 2, ROWS, D), BF16),
        (own, BF16),
        (own, BF16),
        (own, BF16),
        ((nk, D), BF16),
        ((nk, D), BF16),
        ((2,) + own, BF16),
        (blk.shape, BF16),
        ((16, D), F32),
        ((2, NP, ROWS, D), BF16),
        ((n, NP, ROWS, D), BF16),
        ((SLOTS, 2, ROWS // 2, D), BF16),
        ((2 * SLOTS, ROWS, D), BF16),
        ((CHAIN, T + 1, ROWS, COLS), BF16),
        ((6, 16, D), F32),
        ((5, 16, D), F32),
        ((T + 1, NP, ROWS, COLS), BF16),
        ((2, ROWS // 2, COLS), BF16),
        ((2, ROWS, COLS), BF16),
        ((NP, ROWS, COLS), BF16),
    )
    return pl.pallas_call(
        backward_kernel,
        out_shape=(
            jax.ShapeDtypeStruct((n, ROWS, COLS), F32),
            jax.ShapeDtypeStruct((16, D), F32),
            jax.ShapeDtypeStruct(blk.shape, BF16),
            jax.ShapeDtypeStruct(blk.shape, BF16),
        ),
        in_specs=[any_space] * len(args),
        out_specs=[vmem, vmem, any_space, any_space],
        scratch_shapes=[pltpu.VMEM(*o) for o in scratch]
        + [
            dma((32,)),
            dma((2, 2)),
            dma((3,)),
            dma((n,)),
            dma((2, n, 2)),
            dma((2, n, 2)),
            dma((2, n, T + 1)),
            dma((2, 5)),
            dma((4, 2)),
        ],
        name="backward_all",
        compiler_params=pltpu.CompilerParams(
            collective_id=1, has_side_effects=True, vmem_limit_bytes=60 << 20
        ),
    )(*args)


def head_probs(k, q_t, bias):
    s = jnp.dot(k, q_t, preferred_element_type=F32) + bias
    e = jnp.exp(s - jnp.max(s, axis=0, keepdims=True))
    return e / jnp.sum(e, axis=0, keepdims=True)


def head_rows(q_t, h):
    row = lax.broadcasted_iota(jnp.int32, q_t.shape, 0) // HD
    return jnp.where(row == h, q_t, jnp.zeros_like(q_t))


def head_lanes(q, h):
    lane = lax.broadcasted_iota(jnp.int32, q.shape, 1) // HD
    return jnp.where(lane == h, q, jnp.zeros_like(q))


def norm_parts(values):
    center = values - jnp.mean(values, axis=-1, keepdims=True)
    spread = jnp.mean(center * center, axis=-1, keepdims=True)
    inverse = lax.rsqrt(spread + EPS)
    return center * inverse, inverse


def norm_back(grad, unit, inverse, gain):
    scaled = grad * gain
    return inverse * (
        scaled
        - jnp.mean(scaled, axis=-1, keepdims=True)
        - unit * jnp.mean(scaled * unit, axis=-1, keepdims=True)
    )


def dot_nn(a, b):
    return lax.dot_general(a, b, (((1,), (0,)), ((), ())), preferred_element_type=F32)


def dot_nt(a, b):
    return lax.dot_general(a, b, (((1,), (1,)), ((), ())), preferred_element_type=F32)


def per_device_chips(
    activations, cotangent, token_valid, image_counts, pre_gain, pre_shift, attn_weight,
    attn_bias, proj_weight, proj_bias, mid_gain, mid_shift, up_weight, up_bias, down_weight,
    down_bias,
):
    local_rows = activations.shape[0]
    slots = activations.shape[1]
    block = -(-local_rows // 16) * 16
    pad = block - local_rows
    d = lax.axis_index("dp")
    t = lax.axis_index("tensor")
    c = lax.rem(d, 2)
    first_row = t * local_rows
    my_valid = lax.dynamic_slice_in_dim(token_valid, first_row, local_rows, 1).astype(F32)
    slot_live = (jnp.arange(slots, dtype=jnp.int32) < image_counts[0]).astype(F32)
    out_mask = jnp.transpose(slot_live[:, None] * my_valid)[:, :, None]

    def to_blocks(a):
        return jnp.pad(jnp.transpose(a, (1, 0, 2)), ((0, 0), (0, pad), (0, 0)))

    x_blocks = to_blocks(activations)
    c_blocks = to_blocks((cotangent.astype(F32) * out_mask).astype(BF16))
    valid = jnp.pad(
        token_valid.astype(F32).reshape(slots, T, local_rows), ((0, 0), (0, 0), (0, pad))
    ).reshape(slots, T * block)
    valid = jnp.pad(valid, ((0, 8 - slots), (0, 0)))
    per_j = up_weight.shape[1] // COLS
    w = jnp.concatenate(
        [
            attn_weight,
            jnp.transpose(proj_weight)[None],
            jnp.transpose(up_weight.reshape(ROWS, per_j, COLS), (1, 0, 2)),
            jnp.transpose(down_weight.reshape(per_j, COLS, ROWS), (0, 2, 1)),
        ],
        axis=0,
    )
    v = jnp.concatenate(
        [
            jnp.stack([pre_gain, pre_shift, proj_bias, mid_gain, mid_shift, down_bias]),
            attn_bias.reshape(-1, 128),
            up_bias.reshape(-1, 128),
        ],
        axis=0,
    )
    v = jnp.pad(v, ((0, VROWS - v.shape[0]), (0, 0)))
    (
        full_w, vec, x_own, own_cot, bias, queries, keys, values, attended, normed_t, normed2_t,
        mlp_grad_t, hidden, pre_grad, normed2_grad, resid, block_own, up_sums,
    ) = forward_all(w, v, x_blocks, c_blocks, valid)
    own = resid.shape
    grads, totals, own_block, own_input = backward_all(
        full_w, vec, x_own.reshape(own), own_cot.reshape(own), bias, queries, keys,
        values, attended, normed_t, normed2_t, mlp_grad_t, hidden, pre_grad, normed2_grad, resid,
        block_own.reshape(own_cot.shape), up_sums,
    )
    owned = lax.dynamic_slice(totals, (0, d * ROWS), (6, ROWS))
    parted = lax.dynamic_slice(totals, (0, t * COLS), (totals.shape[0], COLS))

    def from_blocks(a):
        return jnp.transpose(a[:, :local_rows], (1, 0, 2))

    block_out = (from_blocks(own_block).astype(F32) * out_mask).astype(BF16)
    input_grad = from_blocks(own_input).astype(F32)
    at = {m: i for i, m in enumerate(SEQUENCE)}
    quarters = range(QUARTERS)
    return (
        block_out,
        input_grad,
        owned[0],
        owned[1],
        jnp.stack([grads[at[m]] for m in range(3)]),
        parted[6:8],
        jnp.transpose(grads[at[3]]),
        owned[2],
        owned[3],
        owned[4],
        jnp.concatenate([grads[at[4 + j]] for j in quarters], axis=1),
        parted[8 : 8 + QUARTERS].reshape(-1),
        jnp.concatenate([jnp.transpose(grads[at[8 + j]]) for j in quarters], axis=0),
        owned[5],
    )


def solution(mesh):
    sizes = (mesh.shape["dp"], mesh.shape["tensor"])
    per_device = per_device_chips if sizes == (2 * NP, T) else per_device_general
    return jax.shard_map(
        per_device,
        mesh=mesh,
        in_specs=(
            P("tensor", "dp", None),
            P("tensor", "dp", None),
            P("dp", None),
            P("dp"),
            P("dp"),
            P("dp"),
            P(None, "dp", "tensor"),
            P(None, "tensor"),
            P("tensor", "dp"),
            P("dp"),
            P("dp"),
            P("dp"),
            P("dp", "tensor"),
            P("tensor"),
            P("tensor", "dp"),
            P("dp"),
        ),
        out_specs=(
            P("tensor", "dp", None),
            P("tensor", "dp", None),
            P("dp"),
            P("dp"),
            P(None, "dp", "tensor"),
            P(None, "tensor"),
            P("tensor", "dp"),
            P("dp"),
            P("dp"),
            P("dp"),
            P("dp", "tensor"),
            P("tensor"),
            P("tensor", "dp"),
            P("dp"),
        ),
        check_vma=False,
    )
```
